32 devices in a mesh: dp: 8 (over y, x, core), tensor: 4 (over z).
Axes of the slice: x: 2, y: 2, z: 4, core: 2. Of those that a mesh axis runs over, the one named last changes fastest.
Arguments:
- tokens: bfloat16 [2, 8192, 2048], P(None, 'dp', 'tensor'), may hold values from -6 to 6
- cotangent: bfloat16 [2, 8192, 2048], P(None, 'dp', 'tensor'), may hold values from -6 to 6
- lengths: int32 [2, 8, 3], replicated, may hold values from 1 to 819, 1024 in all within a row
- dealing: int32 [2, 24], replicated, may hold values from 0 to 23, each once within a row
- query_weight: bfloat16 [2048, 2048], P(None, 'tensor'), may hold values from -0.125 to 0.125
- key_weight: bfloat16 [2048, 2048], P(None, 'tensor'), may hold values from -0.125 to 0.125
- value_weight: bfloat16 [2048, 2048], P(None, 'tensor'), may hold values from -0.125 to 0.125
- out_weight: bfloat16 [2048, 2048], P('tensor'), may hold values from -0.5 to 0.5
- query_bias: bfloat16 [2048], P('tensor'), may hold values from -4 to 4
- value_bias: bfloat16 [2048], P('tensor'), may hold values from -1.5 to 1.5
- out_bias: bfloat16 [2048], replicated, may hold values from -4 to 4
- up_weight: bfloat16 [2048, 8192], P(None, 'tensor'), may hold values from -0.125 to 0.125
- up_bias: bfloat16 [8192], P('tensor'), may hold values from -4 to 4
- down_weight: bfloat16 [8192, 2048], P('tensor'), may hold values from -0.0625 to 0.0625
- down_bias: bfloat16 [2048], replicated, may hold values from -4 to 4
- attn_gain: bfloat16 [2048], replicated, may hold values from 0.5 to 1.5
- attn_shift: bfloat16 [2048], replicated, may hold values from -3 to 3
- mlp_gain: bfloat16 [2048], replicated, may hold values from 0.5 to 1.5
- mlp_shift: bfloat16 [2048], replicated, may hold values from -3 to 3
Outputs:
- layer_out: bfloat16 [2, 8192, 2048], P(None, 'dp', 'tensor')
- input_grad: bfloat16 [2, 8192, 2048], P(None, 'dp', 'tensor')
- query_weight_grad: float32 [2048, 2048], P(None, 'tensor')
- key_weight_grad: float32 [2048, 2048], P(None, 'tensor')
- value_weight_grad: float32 [2048, 2048], P(None, 'tensor')
- out_weight_grad: float32 [2048, 2048], P('tensor')
- query_bias_grad: float32 [2048], P('tensor')
- value_bias_grad: float32 [2048], P('tensor')
- out_bias_grad: float32 [2048], replicated
- up_weight_grad: float32 [2048, 8192], P(None, 'tensor')
- up_bias_grad: float32 [8192], P('tensor')
- down_weight_grad: float32 [8192, 2048], P('tensor')
- down_bias_grad: float32 [2048], replicated
- attn_gain_grad: float32 [2048], replicated
- attn_shift_grad: float32 [2048], replicated
- mlp_gain_grad: float32 [2048], replicated
- mlp_shift_grad: float32 [2048], replicated
The draws below stay inside these ranges and needn't reach their ends.
Inputs may be any that keep to these rules, and one draw needn't show every extreme that they name: The 3 lengths of one data index in a micro-batch add up to 1024, and the longest of them is exactly 819. Each row of dealing names every sequence number once.
All inputs are finite; a program needn't handle non-finite values.
Results may differ from the reference program's by a relative error of at most 0.014.
Values may be sent and summed in bfloat16 or wider, within the bound.
A program may use at most 448 MiB of HBM per device.

```python
import math
import jax
import jax.numpy as jnp
import numpy as np
from jax import lax

D = 2048
HEADS = 32
HEAD_DIM = 64
FF = 8192
SEG = 512
SUMM = 50
SEQ_DEV = 3
MB = 2
TOK_DEV = 1024
LMAX = 819
NSEQ = 24
TOKENS = 8192
N_DP = 8


def block_levels(own_key, shape, cuts, least, largest):
    loudness, own = 1.0, jax.random.fold_in(own_key, 6)
    for axis_at, blocks in cuts:
        steps = jnp.exp(jax.random.uniform(jax.random.fold_in(own, axis_at), (blocks,), jnp.float32, least / len(cuts), largest / len(cuts)))
        loudness = loudness * jnp.repeat(steps, shape[axis_at] // blocks).reshape([-1 if axis == axis_at else 1 for axis in range(len(shape))])
    return loudness


def split_up(amount, total, most, lean):
    loads = [(1 << 20) // math.isqrt(standing ** lean) + 1 for standing in range(2, amount + 1)]
    spare, holding = total - most - (amount - 1), [1] * (amount - 1)
    while spare > 0:
        movable = [i for i in range(amount - 1) if holding[i] < most]
        whole, budget = sum([loads[i] for i in movable]), spare
        for i in movable:
            addition = min(most - holding[i], max(1, budget * loads[i] // whole), spare)
            holding[i] = holding[i] + addition
            spare = spare - addition
    return np.array([most] + holding)


def uneven(own_key, count, total, bound, lean):
    if count == 2:
        one = jax.random.randint(own_key, (), max(1, total - bound), min(bound, total - 1) + 1)
        return jnp.stack([one, total - one])
    tallies = jnp.asarray(split_up(count, total, bound, lean), jnp.int32)
    couples = (count - 1) // 2
    source_of, receiver = tallies[1:1 + 2 * couples:2], tallies[2:2 + 2 * couples:2]
    slack = jnp.minimum(source_of - 1, bound - receiver)
    moved = jax.random.randint(jax.random.fold_in(own_key, 1), (couples,), 0, 1 << 20) % (slack + 1)
    tallies = tallies.at[1:1 + 2 * couples:2].set(source_of - moved).at[2:2 + 2 * couples:2].set(receiver + moved)
    return tallies[jax.random.permutation(jax.random.fold_in(own_key, 2), count)]


def bell_draw(own_key, dims, deviation, most, shards=(), kind=jnp.bfloat16):
    level = block_levels(own_key, dims, shards, -0.22, 0.18) if shards else 1.0
    values = jax.random.normal(own_key, dims, jnp.float32) * deviation * level
    return jnp.minimum(jnp.maximum(values, -most), most).astype(kind)


def setup_inputs(seed: int = 0) -> dict:
    streams_of = jax.random.split(jax.random.key(seed), 20)
    tokens = bell_draw(streams_of[0], (MB, TOKENS, D), 1.0, 6.0, ((1, 8), (2, 4)))
    cotangent = bell_draw(streams_of[1], (MB, TOKENS, D), 1.0, 6.0, ((1, 8), (2, 4)))
    lengths = jax.vmap(lambda own: uneven(own, SEQ_DEV, TOK_DEV, LMAX, 2))(jax.random.split(streams_of[2], MB * N_DP)).reshape((MB, N_DP, SEQ_DEV)).astype(jnp.int32)
    dealing = jax.vmap(lambda own: jax.random.permutation(own, NSEQ))(jax.random.split(streams_of[3], MB)).reshape((MB, NSEQ)).astype(jnp.int32)
    query_weight = bell_draw(streams_of[4], (D, D), D ** -0.5, 0.125, ((1, 4),))
    key_weight = bell_draw(streams_of[5], (D, D), D ** -0.5, 0.125, ((1, 4),))
    value_weight = bell_draw(streams_of[6], (D, D), D ** -0.5, 0.125, ((1, 4),))
    out_weight = bell_draw(streams_of[7], (D, D), (D // 16) ** -0.5, 0.5, ((0, 4),))
    query_bias = bell_draw(streams_of[8], (D,), 0.3, 4.0, ((0, 4),))
    value_bias = bell_draw(streams_of[9], (D,), 0.1, 1.5, ((0, 4),))
    out_bias = bell_draw(streams_of[10], (D,), 0.3, 4.0)
    up_weight = bell_draw(streams_of[11], (D, FF), D ** -0.5, 0.125, ((1, 4),))
    up_bias = bell_draw(streams_of[12], (FF,), 0.3, 4.0, ((0, 4),))
    down_weight = bell_draw(streams_of[13], (FF, D), FF ** -0.5, 0.0625, ((0, 4),))
    down_bias = bell_draw(streams_of[14], (D,), 0.3, 4.0)
    attn_gain = jnp.clip(1.0 + 0.1 * jax.random.normal(streams_of[15], (D,), jnp.float32), 0.5, 1.5).astype(jnp.bfloat16)
    attn_shift = bell_draw(streams_of[16], (D,), 0.2, 3.0)
    mlp_gain = jnp.clip(1.0 + 0.1 * jax.random.normal(streams_of[17], (D,), jnp.float32), 0.5, 1.5).astype(jnp.bfloat16)
    mlp_shift = bell_draw(streams_of[18], (D,), 0.2, 3.0)
    return dict(tokens=tokens, cotangent=cotangent, lengths=lengths, dealing=dealing, query_weight=query_weight, key_weight=key_weight, value_weight=value_weight, out_weight=out_weight, query_bias=query_bias, value_bias=value_bias, out_bias=out_bias, up_weight=up_weight, up_bias=up_bias, down_weight=down_weight, down_bias=down_bias, attn_gain=attn_gain, attn_shift=attn_shift, mlp_gain=mlp_gain, mlp_shift=mlp_shift)


NORM_EPS = 1e-05
MASKED = -1e+30

@jax.custom_vjp
def low(v):
    return lax.optimization_barrier(v.astype(jnp.bfloat16)).astype(jnp.float32)

@jax.custom_vjp
def low_back(v):
    return v

def low_keep(v):
    return (low(v), None)

def low_pass(kept, grad):
    return (grad,)

def back_keep(v):
    return (v, None)

def back_low(kept, grad):
    return (low(grad),)
low.defvjp(low_keep, low_pass)
low_back.defvjp(back_keep, back_low)

def gelu_tanh(values):
    return jax.nn.gelu(values, approximate=True)

def exact_dot(left_array, right_array):
    return jnp.dot(left_array, right_array, precision=lax.Precision.HIGHEST, preferred_element_type=jnp.float32)

def norm_rows(values, gain_row, shift_row):
    center = lax.optimization_barrier(jnp.mean(values, axis=-1, keepdims=True))
    shifted = values - center
    spread = lax.optimization_barrier(jnp.mean(shifted * shifted, axis=-1, keepdims=True))
    return shifted * lax.rsqrt(spread + NORM_EPS) * gain_row + shift_row

def given_layout(lengths_mb, dealing_mb):
    seq_count = dealing_mb.shape[0]
    labels = jnp.arange(seq_count, dtype=jnp.int32)
    flat_lengths = lengths_mb.reshape(seq_count).astype(jnp.int32)
    one_hot = (dealing_mb.astype(jnp.int32)[:, None] == labels[None, :]).astype(jnp.int32)
    given_len = lax.optimization_barrier(jnp.sum(one_hot * flat_lengths[None, :], axis=1, dtype=jnp.int32))
    given_off = (jnp.cumsum(given_len, dtype=jnp.int32) - given_len).astype(jnp.int32)
    start_by_seq = lax.optimization_barrier(jnp.sum(one_hot * given_off[:, None], axis=0, dtype=jnp.int32))
    return (given_len, given_off, start_by_seq)

def buffer_layout(lengths_dev, start_dev, rows_total):
    seq_count = lengths_dev.shape[0]
    lengths_dev = lengths_dev.astype(jnp.int32)
    end_rows = jnp.cumsum(lengths_dev, dtype=jnp.int32)
    offsets = (end_rows - lengths_dev).astype(jnp.int32)
    row_ids = jnp.arange(rows_total, dtype=jnp.int32)
    holder = lax.optimization_barrier(jnp.sum((row_ids[:, None] >= end_rows[None, :]).astype(jnp.int32), axis=1, dtype=jnp.int32))
    one_hot = (holder[:, None] == jnp.arange(seq_count, dtype=jnp.int32)[None, :]).astype(jnp.int32)
    position = (row_ids - lax.optimization_barrier(jnp.sum(one_hot * offsets[None, :], axis=1, dtype=jnp.int32))).astype(jnp.int32)
    source = (lax.optimization_barrier(jnp.sum(one_hot * start_dev.astype(jnp.int32)[None, :], axis=1, dtype=jnp.int32)) + position).astype(jnp.int32)
    return (holder, position, source)

def visible(holder, position, first_row, last_row, key_reach):
    period = SEG + SUMM
    query_seq = holder[first_row:last_row, None]
    key_seq = holder[None, :key_reach]
    query_part = position[first_row:last_row, None] // period
    key_part = position[None, :key_reach] // period
    summary = position[None, :key_reach] % period >= SEG
    query_row = jnp.arange(first_row, last_row, dtype=jnp.int32)[:, None]
    key_row = jnp.arange(key_reach, dtype=jnp.int32)[None, :]
    same_part = (query_part == key_part) & (key_row <= query_row)
    earlier = (key_part < query_part) & summary
    return (query_seq == key_seq) & (same_part | earlier)

def layer_forward(inputs, params, allowed):
    query_weight, key_weight, value_weight, out_weight, query_bias, value_bias, out_bias, up_weight, up_bias, down_weight, down_bias, attn_gain, attn_shift, mlp_gain, mlp_shift = params
    row_count = inputs.shape[0]
    score_scale = float(HEAD_DIM) ** (-0.5)
    first_in = low_back(low(norm_rows(inputs, attn_gain, attn_shift)))
    queries = low(low_back(exact_dot(first_in, query_weight)) + query_bias)
    keys_all = low(low_back(exact_dot(first_in, key_weight)))
    values_all = low(low_back(exact_dot(first_in, value_weight)) + value_bias)
    queries = queries.reshape(row_count, HEADS, HEAD_DIM)
    keys_all = keys_all.reshape(row_count, HEADS, HEAD_DIM)
    values_all = values_all.reshape(row_count, HEADS, HEAD_DIM)
    scores = jnp.einsum('qhd,khd->hqk', queries, keys_all, precision=lax.Precision.HIGHEST) * score_scale
    scores = low_back(scores)
    seen = allowed[None]
    row_top = lax.optimization_barrier(jnp.max(jnp.where(seen, scores, MASKED), axis=-1, keepdims=True))
    centered = jnp.where(seen, scores - row_top, jnp.zeros_like(scores))
    exp_terms = jnp.where(seen, jnp.exp(centered), jnp.zeros_like(scores))
    attn_prob = low(exp_terms / lax.optimization_barrier(jnp.sum(exp_terms, axis=-1, keepdims=True)))
    mixed_heads = jnp.einsum('hqk,khd->qhd', attn_prob, values_all, precision=lax.Precision.HIGHEST)
    mixed_heads = low_back(low(mixed_heads.reshape(row_count, HEADS * HEAD_DIM)))
    resid = inputs + low_back(exact_dot(mixed_heads, out_weight)) + out_bias
    second_in = low_back(low(norm_rows(low(resid), mlp_gain, mlp_shift)))
    hidden_pre = low_back(exact_dot(second_in, up_weight)) + up_bias
    hidden = low(gelu_tanh(hidden_pre))
    return resid + exact_dot(hidden, down_weight) + down_bias

def reference(tokens, cotangent, lengths, dealing, query_weight, key_weight, value_weight, out_weight, query_bias, value_bias, out_bias, up_weight, up_bias, down_weight, down_bias, attn_gain, attn_shift, mlp_gain, mlp_shift):
    params = tuple((array.astype(jnp.float32) for array in (query_weight, key_weight, value_weight, out_weight, query_bias, value_bias, out_bias, up_weight, up_bias, down_weight, down_bias, attn_gain, attn_shift, mlp_gain, mlp_shift)))
    micro_count = tokens.shape[0]
    groups = lengths.shape[1]
    seq_dev = lengths.shape[2]
    rows_total = tokens.shape[1] // groups
    labels = jnp.arange(micro_count * groups, dtype=jnp.int32)
    lengths_int = lengths.astype(jnp.int32)
    dealing_int = dealing.astype(jnp.int32)

    def one_group(totals, label):
        micro_step = (label // groups).astype(jnp.int32)
        device = (label % groups).astype(jnp.int32)
        lengths_mb = lax.dynamic_index_in_dim(lengths_int, micro_step, 0, keepdims=False)
        dealing_mb = lax.dynamic_index_in_dim(dealing_int, micro_step, 0, keepdims=False)
        given_len, given_off, start_by_seq = given_layout(lengths_mb, dealing_mb)
        lengths_dev = lax.dynamic_index_in_dim(lengths_mb, device, 0, keepdims=False).astype(jnp.int32)
        start_dev = lax.dynamic_slice_in_dim(start_by_seq, (device * seq_dev).astype(jnp.int32), seq_dev)
        holder, position, source = buffer_layout(lengths_dev, start_dev, rows_total)
        token_mb = lax.dynamic_index_in_dim(tokens, micro_step, 0, keepdims=False)
        cot_mb = lax.dynamic_index_in_dim(cotangent, micro_step, 0, keepdims=False)
        inputs = jnp.take(token_mb, source, axis=0).astype(jnp.float32)
        grad_rows = jnp.take(cot_mb, source, axis=0).astype(jnp.float32)
        allowed = visible(holder, position, 0, rows_total, rows_total)

        def forward(values, weights):
            return layer_forward(values, weights, allowed)
        result, pullback = jax.vjp(forward, inputs, params)
        input_back, weight_grads = pullback(grad_rows)
        totals = tuple((held + added.astype(jnp.float32) for held, added in zip(totals, weight_grads)))
        return (totals, (result.astype(jnp.bfloat16), input_back.astype(jnp.bfloat16), source.astype(jnp.int32)))
    zero_grads = tuple((jnp.zeros(array.shape, jnp.float32) for array in params))
    totals, (results, back_rows, sources) = lax.scan(one_group, zero_grads, labels)
    micro_ids = (labels // groups).astype(jnp.int32)[:, None]
    layer_out = jnp.zeros(tokens.shape, jnp.bfloat16).at[micro_ids, sources].set(results)
    input_grad = jnp.zeros(tokens.shape, jnp.bfloat16).at[micro_ids, sources].set(back_rows)
    return (layer_out, input_grad, totals[0], totals[1], totals[2], totals[3], totals[4], totals[5], totals[6], totals[7], totals[8], totals[9], totals[10], totals[11], totals[12], totals[13], totals[14])
```

```python
import functools

import jax
import jax.numpy as jnp
from jax import lax
from jax.experimental import pallas as pl
from jax.experimental.pallas import tpu as pltpu
from jax.sharding import Mesh
from jax.sharding import PartitionSpec as P


HEAD_DIM = 64
SEG = 512
SUMM = 50
NBLK = 2


NORM_EPS = 1e-05
MASKED = -1e30


def gelu_tanh(values):
    return jax.nn.gelu(values, approximate=True)


def matmul(left_array, right_array):
    return jnp.dot(left_array, right_array, preferred_element_type=jnp.float32)


def cross_rows(left_array, right_array):
    return lax.dot_general(
        left_array, right_array, (((0,), (0,)), ((), ())), preferred_element_type=jnp.float32
    )


def times_transpose(left_array, right_array):
    return lax.dot_general(
        left_array, right_array, (((1,), (1,)), ((), ())), preferred_element_type=jnp.float32
    )


def normalize(values):
    center = jnp.mean(values, axis=1, keepdims=True)
    shifted = values - center
    spread = jnp.mean(shifted * shifted, axis=1, keepdims=True)
    inverse = lax.rsqrt(spread + NORM_EPS)
    return (shifted * inverse, inverse)


def norm_backward(grad_in, normed, inverse, gain_row):
    gain_grad = jnp.sum(grad_in * normed, axis=0)
    shift_grad = jnp.sum(grad_in, axis=0)
    scaled = grad_in * gain_row
    first_mean = jnp.mean(scaled, axis=1, keepdims=True)
    second_mean = jnp.mean(scaled * normed, axis=1, keepdims=True)
    return (inverse * (scaled - first_mean - normed * second_mean), gain_grad, shift_grad)


def running_sum(counts):
    size = counts.shape[-1]
    places = jnp.arange(size, dtype=jnp.int32)
    upto = (places[:, None] <= places[None, :]).astype(jnp.int32)
    return jnp.sum(counts[..., :, None] * upto, axis=-2, dtype=jnp.int32)


def given_layout(lengths_mb, dealing_mb):
    seq_count = dealing_mb.shape[0]
    labels = jnp.arange(seq_count, dtype=jnp.int32)
    flat_lengths = lengths_mb.reshape(seq_count)
    one_hot = (dealing_mb[:, None] == labels[None, :]).astype(jnp.int32)
    given_len = jnp.sum(one_hot * flat_lengths[None, :], axis=1, dtype=jnp.int32)
    given_off = running_sum(given_len) - given_len
    start_by_seq = jnp.sum(one_hot * given_off[:, None], axis=0, dtype=jnp.int32)
    return (given_len, given_off, start_by_seq)


def buffer_layout(lengths_dev, start_dev, rows_total):
    seq_count = lengths_dev.shape[0]
    end_rows = running_sum(lengths_dev)
    offsets = end_rows - lengths_dev
    row_ids = jnp.arange(rows_total, dtype=jnp.int32)
    holder = jnp.sum(
        (row_ids[:, None] >= end_rows[None, :]).astype(jnp.int32), axis=1, dtype=jnp.int32
    )
    one_hot = (holder[:, None] == jnp.arange(seq_count, dtype=jnp.int32)[None, :]).astype(jnp.int32)
    position = row_ids - jnp.sum(one_hot * offsets[None, :], axis=1, dtype=jnp.int32)
    source = jnp.sum(one_hot * start_dev[None, :], axis=1, dtype=jnp.int32) + position
    return (holder, position, source)


def visible(holder, position, first_row, last_row, key_reach):
    period = SEG + SUMM
    query_seq = holder[first_row:last_row, None]
    key_seq = holder[None, :key_reach]
    query_part = position[first_row:last_row, None] // period
    key_part = position[None, :key_reach] // period
    summary = position[None, :key_reach] % period >= SEG
    query_row = jnp.arange(first_row, last_row, dtype=jnp.int32)[:, None]
    key_row = jnp.arange(key_reach, dtype=jnp.int32)[None, :]
    same_part = (query_part == key_part) & (key_row <= query_row)
    earlier = (key_part < query_part) & summary
    return (query_seq == key_seq) & (same_part | earlier)


def block_scores(queries, keys_all, allowed, score_scale):
    scores = (
        jnp.einsum("qhd,khd->hqk", queries, keys_all, preferred_element_type=jnp.float32)
        * score_scale
    )
    return jnp.where(allowed[None], scores, MASKED)


def shards(
    tokens,
    cotangent,
    lengths,
    dealing,
    query_weight,
    key_weight,
    value_weight,
    out_weight,
    query_bias,
    value_bias,
    out_bias,
    up_weight,
    up_bias,
    down_weight,
    down_bias,
    attn_gain,
    attn_shift,
    mlp_gain,
    mlp_shift,
):
    micro_count = tokens.shape[0]
    tok_rows = tokens.shape[1]
    col_width = tokens.shape[2]
    seq_dev = lengths.shape[2]
    heads_here = query_weight.shape[1] // HEAD_DIM
    head_cols = heads_here * HEAD_DIM
    block_rows = tok_rows // NBLK
    score_scale = HEAD_DIM ** (-0.5)
    device = lax.axis_index("dp")
    column = lax.axis_index("tensor")
    gain_one = attn_gain.astype(jnp.float32)
    shift_one = attn_shift.astype(jnp.float32)
    gain_two = mlp_gain.astype(jnp.float32)
    shift_two = mlp_shift.astype(jnp.float32)
    query_bias_f = query_bias.astype(jnp.float32)
    value_bias_f = value_bias.astype(jnp.float32)
    up_bias_f = up_bias.astype(jnp.float32)
    out_bias_cols = lax.dynamic_slice_in_dim(
        out_bias.astype(jnp.float32), column * col_width, col_width
    )
    down_bias_cols = lax.dynamic_slice_in_dim(
        down_bias.astype(jnp.float32), column * col_width, col_width
    )
    query_w_grad = jnp.zeros(query_weight.shape, jnp.float32)
    key_w_grad = jnp.zeros(key_weight.shape, jnp.float32)
    value_w_grad = jnp.zeros(value_weight.shape, jnp.float32)
    out_w_grad = jnp.zeros(out_weight.shape, jnp.float32)
    query_b_grad = jnp.zeros(query_bias.shape, jnp.float32)
    value_b_grad = jnp.zeros(value_bias.shape, jnp.float32)
    out_b_grad = jnp.zeros(out_bias.shape, jnp.float32)
    up_w_grad = jnp.zeros(up_weight.shape, jnp.float32)
    up_b_grad = jnp.zeros(up_bias.shape, jnp.float32)
    down_w_grad = jnp.zeros(down_weight.shape, jnp.float32)
    down_b_grad = jnp.zeros(down_bias.shape, jnp.float32)
    gain_one_grad = jnp.zeros(attn_gain.shape, jnp.float32)
    shift_one_grad = jnp.zeros(attn_shift.shape, jnp.float32)
    gain_two_grad = jnp.zeros(mlp_gain.shape, jnp.float32)
    shift_two_grad = jnp.zeros(mlp_shift.shape, jnp.float32)
    layer_parts = []
    grad_parts = []
    for micro_step in range(micro_count):
        lengths_mb = lengths[micro_step]
        dealing_mb = dealing[micro_step]
        given_len, given_off, start_by_seq = given_layout(lengths_mb, dealing_mb)
        lengths_dev = lax.dynamic_index_in_dim(lengths_mb, device, 0, keepdims=False)
        start_dev = lax.dynamic_slice_in_dim(start_by_seq, device * seq_dev, seq_dev)
        holder, position, source = buffer_layout(lengths_dev, start_dev, tok_rows)
        blank_rows = jnp.zeros((tok_rows, col_width), jnp.bfloat16)
        pieces = (
            lax.all_gather(tokens[micro_step], "dp", axis=0, tiled=True),
            lax.all_gather(cotangent[micro_step], "dp", axis=0, tiled=True),
        )
        span_rows = pieces[0].shape[0]
        inside = ((source >= 0) & (source < span_rows))[:, None]
        fetch_at = jnp.clip(source, 0, span_rows - 1)
        tok_buf = jnp.where(inside, jnp.take(pieces[0], fetch_at, axis=0), blank_rows)
        cot_buf = jnp.where(inside, jnp.take(pieces[1], fetch_at, axis=0), blank_rows)
        tok_full, cot_full = (
            lax.all_gather(tok_buf, "tensor", axis=1, tiled=True),
            lax.all_gather(cot_buf, "tensor", axis=1, tiled=True),
        )
        normed_one, inverse_one = normalize(tok_full.astype(jnp.float32))
        first_in = (normed_one * gain_one + shift_one).astype(jnp.bfloat16)
        queries = (
            (matmul(first_in, query_weight) + query_bias_f)
            .astype(jnp.bfloat16)
            .reshape(tok_rows, heads_here, HEAD_DIM)
        )
        keys_here = (
            matmul(first_in, key_weight)
            .astype(jnp.bfloat16)
            .reshape(tok_rows, heads_here, HEAD_DIM)
        )
        values_here = (
            (matmul(first_in, value_weight) + value_bias_f)
            .astype(jnp.bfloat16)
            .reshape(tok_rows, heads_here, HEAD_DIM)
        )
        outputs = []
        row_tops = []
        row_totals = []
        for block_index in range(NBLK):
            row_lower = block_index * block_rows
            row_upper = row_lower + block_rows
            allowed = visible(holder, position, row_lower, row_upper, row_upper)
            scores = block_scores(
                queries[row_lower:row_upper], keys_here[:row_upper], allowed, score_scale
            )
            row_top = jnp.max(scores, axis=2, keepdims=True)
            exp_terms = jnp.exp(scores - row_top)
            row_total = jnp.sum(exp_terms, axis=2, keepdims=True)
            attn_prob = exp_terms / row_total
            outputs.append(
                jnp.einsum(
                    "hqk,khd->qhd",
                    attn_prob.astype(jnp.bfloat16),
                    values_here[:row_upper],
                    preferred_element_type=jnp.float32,
                )
            )
            row_tops.append(row_top)
            row_totals.append(row_total)
        mixed_heads = (
            jnp.concatenate(outputs, axis=0).reshape(tok_rows, head_cols).astype(jnp.bfloat16)
        )
        attn_cols = lax.psum_scatter(
            matmul(mixed_heads, out_weight), "tensor", scatter_dimension=1, tiled=True
        )
        resid_cols = tok_buf.astype(jnp.float32) + attn_cols + out_bias_cols
        resid_full = lax.all_gather(resid_cols.astype(jnp.bfloat16), "tensor", axis=1, tiled=True)
        normed_two, inverse_two = normalize(resid_full.astype(jnp.float32))
        second_in = (normed_two * gain_two + shift_two).astype(jnp.bfloat16)
        hidden_pre = matmul(second_in, up_weight) + up_bias_f
        hidden_act, gelu_pull = jax.vjp(gelu_tanh, hidden_pre)
        hidden = hidden_act.astype(jnp.bfloat16)
        mlp_cols = lax.psum_scatter(
            matmul(hidden, down_weight).astype(jnp.bfloat16),
            "tensor",
            scatter_dimension=1,
            tiled=True,
        ).astype(jnp.float32)
        layer_cols = (resid_cols + mlp_cols + down_bias_cols).astype(jnp.bfloat16)
        grad_out = cot_full.astype(jnp.float32)
        down_w_grad = down_w_grad + cross_rows(hidden, cot_full)
        down_b_grad = down_b_grad + jnp.sum(grad_out, axis=0)
        hidden_grad = gelu_pull(times_transpose(cot_full, down_weight))[0]
        up_b_grad = up_b_grad + jnp.sum(hidden_grad, axis=0)
        hidden_low = hidden_grad.astype(jnp.bfloat16)
        up_w_grad = up_w_grad + cross_rows(second_in, hidden_low)
        second_cols = lax.psum_scatter(
            times_transpose(hidden_low, up_weight), "tensor", scatter_dimension=1, tiled=True
        )
        second_grad = lax.all_gather(
            second_cols.astype(jnp.bfloat16), "tensor", axis=1, tiled=True
        ).astype(jnp.float32)
        resid_back, gain_part, shift_part = norm_backward(
            second_grad, normed_two, inverse_two, gain_two
        )
        gain_two_grad = gain_two_grad + gain_part
        shift_two_grad = shift_two_grad + shift_part
        resid_grad = grad_out + resid_back
        out_b_grad = out_b_grad + jnp.sum(resid_grad, axis=0)
        attn_low = resid_grad.astype(jnp.bfloat16)
        out_w_grad = out_w_grad + cross_rows(mixed_heads, attn_low)
        mixed_grad = (
            times_transpose(attn_low, out_weight)
            .astype(jnp.bfloat16)
            .reshape(tok_rows, heads_here, HEAD_DIM)
        )
        query_parts = []
        key_acc = jnp.zeros((tok_rows, heads_here, HEAD_DIM), jnp.float32)
        value_acc = jnp.zeros((tok_rows, heads_here, HEAD_DIM), jnp.float32)
        for block_index in range(NBLK):
            row_lower = block_index * block_rows
            row_upper = row_lower + block_rows
            allowed = visible(holder, position, row_lower, row_upper, row_upper)
            scores = block_scores(
                queries[row_lower:row_upper], keys_here[:row_upper], allowed, score_scale
            )
            attn_prob = jnp.exp(scores - row_tops[block_index]) / row_totals[block_index]
            grad_block = mixed_grad[row_lower:row_upper]
            prob_grad = jnp.einsum(
                "qhd,khd->hqk",
                grad_block,
                values_here[:row_upper],
                preferred_element_type=jnp.float32,
            )
            inner_sum = jnp.sum(attn_prob * prob_grad, axis=2, keepdims=True)
            score_grad = (attn_prob * (prob_grad - inner_sum)).astype(jnp.bfloat16)
            query_parts.append(
                jnp.einsum(
                    "hqk,khd->qhd",
                    score_grad,
                    keys_here[:row_upper],
                    preferred_element_type=jnp.float32,
                )
                * score_scale
            )
            pad_rows = ((0, tok_rows - row_upper), (0, 0), (0, 0))
            key_acc = key_acc + jnp.pad(
                jnp.einsum(
                    "hqk,qhd->khd",
                    score_grad,
                    queries[row_lower:row_upper],
                    preferred_element_type=jnp.float32,
                )
                * score_scale,
                pad_rows,
            )
            value_acc = value_acc + jnp.pad(
                jnp.einsum(
                    "hqk,qhd->khd",
                    attn_prob.astype(jnp.bfloat16),
                    grad_block,
                    preferred_element_type=jnp.float32,
                ),
                pad_rows,
            )
        query_grad = jnp.concatenate(query_parts, axis=0).reshape(tok_rows, head_cols)
        key_grad = key_acc.reshape(tok_rows, head_cols)
        value_grad = value_acc.reshape(tok_rows, head_cols)
        query_b_grad = query_b_grad + jnp.sum(query_grad, axis=0)
        value_b_grad = value_b_grad + jnp.sum(value_grad, axis=0)
        query_low = query_grad.astype(jnp.bfloat16)
        key_low = key_grad.astype(jnp.bfloat16)
        value_low = value_grad.astype(jnp.bfloat16)
        query_w_grad = query_w_grad + cross_rows(first_in, query_low)
        key_w_grad = key_w_grad + cross_rows(first_in, key_low)
        value_w_grad = value_w_grad + cross_rows(first_in, value_low)
        first_part = (
            times_transpose(query_low, query_weight)
            + times_transpose(key_low, key_weight)
            + times_transpose(value_low, value_weight)
        )
        first_cols = lax.psum_scatter(first_part, "tensor", scatter_dimension=1, tiled=True)
        first_grad = lax.all_gather(
            first_cols.astype(jnp.bfloat16), "tensor", axis=1, tiled=True
        ).astype(jnp.float32)
        input_back, gain_part, shift_part = norm_backward(
            first_grad, normed_one, inverse_one, gain_one
        )
        gain_one_grad = gain_one_grad + gain_part
        shift_one_grad = shift_one_grad + shift_part
        input_cols = lax.dynamic_slice_in_dim(
            resid_grad + input_back, column * col_width, col_width, axis=1
        ).astype(jnp.bfloat16)
        packed = jnp.concatenate([layer_cols, input_cols], axis=1)
        given_end = given_off + given_len
        dest_off = (running_sum(lengths_mb) - lengths_mb).reshape(-1)
        labels = jnp.arange(dealing_mb.shape[0], dtype=jnp.int32)
        give_row_ids = jnp.arange(tok_rows * lax.axis_size("dp"), dtype=jnp.int32)
        owner_seq = jnp.sum(
            (give_row_ids[:, None] >= given_end[None, :]).astype(jnp.int32), axis=1, dtype=jnp.int32
        )
        one_hot = (owner_seq[:, None] == labels[None, :]).astype(jnp.int32)
        within = give_row_ids - jnp.sum(one_hot * given_off[None, :], axis=1, dtype=jnp.int32)
        seq_label = jnp.sum(one_hot * dealing_mb[None, :], axis=1, dtype=jnp.int32)
        seq_hot = (seq_label[:, None] == labels[None, :]).astype(jnp.int32)
        buffer_row = jnp.sum(seq_hot * dest_off[None, :], axis=1, dtype=jnp.int32) + within
        owner_dev = seq_label // seq_dev
        is_mine = owner_dev == device
        fetched = jnp.take(packed, jnp.clip(buffer_row, 0, tok_rows - 1), axis=0).astype(
            jnp.float32
        )
        returned = lax.psum_scatter(
            jnp.where(is_mine[:, None], fetched, 0.0).astype(jnp.bfloat16),
            "dp",
            scatter_dimension=0,
            tiled=True,
        ).astype(jnp.float32)
        layer_parts.append(returned[:, :col_width].astype(jnp.bfloat16))
        grad_parts.append(returned[:, col_width:].astype(jnp.bfloat16))
    (
        query_w_grad,
        key_w_grad,
        value_w_grad,
        out_w_grad,
        query_b_grad,
        value_b_grad,
        out_b_grad,
        gain_one_grad,
        shift_one_grad,
        up_w_grad,
        up_b_grad,
        down_w_grad,
        down_b_grad,
        gain_two_grad,
        shift_two_grad,
    ) = lax.psum(
        (
            query_w_grad,
            key_w_grad,
            value_w_grad,
            out_w_grad,
            query_b_grad,
            value_b_grad,
            out_b_grad,
            gain_one_grad,
            shift_one_grad,
            up_w_grad,
            up_b_grad,
            down_w_grad,
            down_b_grad,
            gain_two_grad,
            shift_two_grad,
        ),
        "dp",
    )
    layer_out = jnp.stack(layer_parts, axis=0)
    input_grad = jnp.stack(grad_parts, axis=0)
    return (
        layer_out,
        input_grad,
        query_w_grad,
        key_w_grad,
        value_w_grad,
        out_w_grad,
        query_b_grad,
        value_b_grad,
        out_b_grad,
        up_w_grad,
        up_b_grad,
        down_w_grad,
        down_b_grad,
        gain_one_grad,
        shift_one_grad,
        gain_two_grad,
        shift_two_grad,
    )


def general_layer(mesh):
    in_specs = (
        P(None, "dp", "tensor"),
        P(None, "dp", "tensor"),
        P(),
        P(),
        P(None, "tensor"),
        P(None, "tensor"),
        P(None, "tensor"),
        P("tensor", None),
        P("tensor"),
        P("tensor"),
        P(),
        P(None, "tensor"),
        P("tensor"),
        P("tensor", None),
        P(),
        P(),
        P(),
        P(),
        P(),
    )
    out_specs = (
        P(None, "dp", "tensor"),
        P(None, "dp", "tensor"),
        P(None, "tensor"),
        P(None, "tensor"),
        P(None, "tensor"),
        P("tensor", None),
        P("tensor"),
        P("tensor"),
        P(),
        P(None, "tensor"),
        P("tensor"),
        P("tensor", None),
        P(),
        P(),
        P(),
        P(),
        P(),
    )
    return jax.shard_map(shards, mesh=mesh, in_specs=in_specs, out_specs=out_specs, check_vma=False)


ROWS = 1024
QBLK = 256
PAIR = 128


def slot_of(block, rank):
    piece = jnp.bitwise_xor(block, rank)
    return jnp.bitwise_or(piece >> 1, (piece & 1) << 1)


def rows_of(block, rank):
    return pl.ds(pl.multiple_of(slot_of(block, rank) * QBLK, QBLK), QBLK)


def fill_bias(bias_ref, key_info_ref, query_info_ref):
    for block in range(ROWS // QBLK):
        reach = (block + 1) * QBLK
        cols = pl.ds(block * QBLK, QBLK)
        key_part = key_info_ref[pl.ds(0, reach), 0:1]
        key_summary = key_info_ref[pl.ds(0, reach), 1:2]
        query_part = query_info_ref[0:1, cols]
        query_seq = query_info_ref[1:2, cols]
        key_row = lax.broadcasted_iota(jnp.int32, (reach, QBLK), 0)
        query_row = lax.broadcasted_iota(jnp.int32, (reach, QBLK), 1) + block * QBLK
        seen = (key_row <= query_row) & ((key_part == query_part) | (key_summary == query_seq))
        bias_ref[pl.ds(0, reach), cols] = jnp.where(seen, 0.0, MASKED)


def nt_dot(left, right):
    return lax.dot_general(left, right, (((1,), (1,)), ((), ())), preferred_element_type=jnp.float32)


def nn_dot(left, right):
    return jnp.dot(left, right, preferred_element_type=jnp.float32)


def head_lanes(block, head):
    lane = lax.broadcasted_iota(jnp.int32, block.shape, 1)
    inside = (lane >= head * HEAD_DIM) & (lane < (head + 1) * HEAD_DIM)
    return jnp.where(inside, block, jnp.zeros_like(block))


def attend_kernel(
    rank_ref, query_ref, key_ref, value_ref, key_info_ref, query_info_ref, out_ref, bias_ref, keys, value_t
):
    rank = rank_ref[0]

    @pl.when(pl.program_id(0) == 0)
    def _():
        fill_bias(bias_ref, key_info_ref, query_info_ref)

    for block in range(ROWS // QBLK):
        here = rows_of(block, rank)
        keys[pl.ds(block * QBLK, QBLK), :] = key_ref[here, :]
        value_t[:, pl.ds(block * QBLK, QBLK)] = value_ref[here, :].T
    for block in range(ROWS // QBLK):
        reach = (block + 1) * QBLK
        here = rows_of(block, rank)
        queries = query_ref[here, :] * jnp.bfloat16(HEAD_DIM**-0.5)
        bias = bias_ref[pl.ds(0, reach), pl.ds(block * QBLK, QBLK)]
        parts = []
        for head in range(2):
            scores = nt_dot(keys[pl.ds(0, reach), :], head_lanes(queries, head)) + bias
            top = jnp.max(scores, axis=0, keepdims=True)
            terms = jnp.exp(scores - top)
            total = jnp.sum(terms, axis=0, keepdims=True)
            heads_t = nn_dot(
                value_t[pl.ds(head * HEAD_DIM, HEAD_DIM), pl.ds(0, reach)], terms.astype(jnp.bfloat16)
            )
            parts.append(heads_t / total)
        out_ref[here, :] = jnp.concatenate(parts, axis=0).T.astype(out_ref.dtype)


def attend(qkv, rank, key_info, query_info):
    pairs = qkv.shape[1] // (3 * PAIR)
    cells = ROWS * ROWS * 5 // 8
    return pl.pallas_call(
        attend_kernel,
        grid_spec=pltpu.PrefetchScalarGridSpec(
            num_scalar_prefetch=1,
            grid=(pairs,),
            in_specs=[
                pl.BlockSpec((ROWS, PAIR), lambda i, r: (0, i)),
                pl.BlockSpec((ROWS, PAIR), lambda i, r: (0, pairs + i)),
                pl.BlockSpec((ROWS, PAIR), lambda i, r: (0, 2 * pairs + i)),
                pl.BlockSpec((ROWS, 2), lambda i, r: (0, 0)),
                pl.BlockSpec((2, ROWS), lambda i, r: (0, 0)),
            ],
            out_specs=pl.BlockSpec((ROWS, PAIR), lambda i, r: (0, i)),
            scratch_shapes=[
                pltpu.VMEM((ROWS, ROWS), jnp.float32),
                pltpu.VMEM((ROWS, PAIR), jnp.bfloat16),
                pltpu.VMEM((PAIR, ROWS), jnp.bfloat16),
            ],
        ),
        out_shape=jax.ShapeDtypeStruct((ROWS, pairs * PAIR), jnp.bfloat16),
        compiler_params=pltpu.CompilerParams(vmem_limit_bytes=24 << 20),
        cost_estimate=pl.CostEstimate(
            flops=2 * 2 * 2 * pairs * cells * 256, bytes_accessed=ROWS * pairs * PAIR * 8, transcendentals=2 * pairs * cells
        ),
        name="attend",
    )(rank, qkv, qkv, qkv, key_info, query_info)


def attend_back_kernel(
    rank_ref,
    query_ref,
    key_ref,
    value_ref,
    grad_ref,
    key_info_ref,
    query_info_ref,
    query_out,
    key_out,
    value_out,
    sums_out,
    bias_ref,
    keys,
    values,
    key_t,
    key_acc,
    value_acc,
):
    rank = rank_ref[0]
    scale = HEAD_DIM**-0.5

    @pl.when(pl.program_id(0) == 0)
    def _():
        fill_bias(bias_ref, key_info_ref, query_info_ref)

    for block in range(ROWS // QBLK):
        here = rows_of(block, rank)
        there = pl.ds(block * QBLK, QBLK)
        keys[there, :] = key_ref[here, :]
        values[there, :] = value_ref[here, :]
        key_t[:, there] = key_ref[here, :].T
    query_sum = jnp.zeros((1, PAIR), jnp.float32)
    for block in reversed(range(ROWS // QBLK)):
        reach = (block + 1) * QBLK
        here = rows_of(block, rank)
        upto = pl.ds(0, reach)
        queries = query_ref[here, :] * jnp.bfloat16(scale)
        grads = grad_ref[here, :]
        bias = bias_ref[upto, pl.ds(block * QBLK, QBLK)]
        parts = []
        key_add = None
        value_add = None
        for head in range(2):
            query_h = head_lanes(queries, head)
            grad_h = head_lanes(grads, head)
            scores = nt_dot(keys[upto, :], query_h) + bias
            top = jnp.max(scores, axis=0, keepdims=True)
            terms = jnp.exp(scores - top)
            prob = terms * (1.0 / jnp.sum(terms, axis=0, keepdims=True))
            prob_grad = nt_dot(values[upto, :], grad_h)
            inner = jnp.sum(prob * prob_grad, axis=0, keepdims=True)
            score_grad = (prob * (prob_grad - inner)).astype(jnp.bfloat16)
            value_part = nn_dot(prob.astype(jnp.bfloat16), grad_h)
            key_part = nn_dot(score_grad, query_h)
            value_add = value_part if value_add is None else value_add + value_part
            key_add = key_part if key_add is None else key_add + key_part
            parts.append(nn_dot(key_t[pl.ds(head * HEAD_DIM, HEAD_DIM), upto], score_grad))
        if block == ROWS // QBLK - 1:
            key_acc[...] = key_add
            value_acc[...] = value_add
        else:
            key_acc[upto, :] += key_add
            value_acc[upto, :] += value_add
        query_grad = jnp.concatenate(parts, axis=0).T * scale
        query_sum = query_sum + jnp.sum(query_grad, axis=0, keepdims=True)
        query_out[here, :] = query_grad.astype(query_out.dtype)
    for block in range(ROWS // QBLK):
        here = rows_of(block, rank)
        there = pl.ds(block * QBLK, QBLK)
        key_out[here, :] = key_acc[there, :].astype(key_out.dtype)
        value_out[here, :] = value_acc[there, :].astype(value_out.dtype)
    value_sum = jnp.sum(value_acc[...], axis=0, keepdims=True)
    row = lax.broadcasted_iota(jnp.int32, (8, PAIR), 0)
    sums_out[...] = jnp.where(row == 0, query_sum, jnp.where(row == 1, value_sum, 0.0))


def attend_back(qkv, grads, rank, key_info, query_info):
    pairs = qkv.shape[1] // (3 * PAIR)
    cells = ROWS * ROWS * 5 // 8
    block = (ROWS, PAIR)
    wide = jax.ShapeDtypeStruct((ROWS, pairs * PAIR), jnp.bfloat16)
    return pl.pallas_call(
        attend_back_kernel,
        grid_spec=pltpu.PrefetchScalarGridSpec(
            num_scalar_prefetch=1,
            grid=(pairs,),
            in_specs=[
                pl.BlockSpec(block, lambda i, r: (0, i)),
                pl.BlockSpec(block, lambda i, r: (0, pairs + i)),
                pl.BlockSpec(block, lambda i, r: (0, 2 * pairs + i)),
                pl.BlockSpec(block, lambda i, r: (0, i)),
                pl.BlockSpec((ROWS, 2), lambda i, r: (0, 0)),
                pl.BlockSpec((2, ROWS), lambda i, r: (0, 0)),
            ],
            out_specs=[
                pl.BlockSpec(block, lambda i, r: (0, i)),
                pl.BlockSpec(block, lambda i, r: (0, i)),
                pl.BlockSpec(block, lambda i, r: (0, i)),
                pl.BlockSpec((8, PAIR), lambda i, r: (0, i)),
            ],
            scratch_shapes=[
                pltpu.VMEM((ROWS, ROWS), jnp.float32),
                pltpu.VMEM(block, jnp.bfloat16),
                pltpu.VMEM(block, jnp.bfloat16),
                pltpu.VMEM((PAIR, ROWS), jnp.bfloat16),
                pltpu.VMEM(block, jnp.float32),
                pltpu.VMEM(block, jnp.float32),
            ],
        ),
        out_shape=[wide, wide, wide, jax.ShapeDtypeStruct((8, pairs * PAIR), jnp.float32)],
        compiler_params=pltpu.CompilerParams(vmem_limit_bytes=28 << 20),
        cost_estimate=pl.CostEstimate(
            flops=2 * 5 * 2 * pairs * cells * 256,
            bytes_accessed=ROWS * pairs * PAIR * 14,
            transcendentals=2 * pairs * cells,
        ),
        name="attend_back",
    )(rank, qkv, qkv, qkv, grads, key_info, query_info)


SWAP = [(0, 1), (1, 0)]
PLANE = ("y", "x", "core")
EVERY = ("z", "y", "x", "core")
MICRO = 2
SLOTS = 72


def swap_along(array, axis):
    return lax.ppermute(array, axis, SWAP)


def pass_on(array):
    size = lax.axis_size("z")
    return lax.ppermute(array, "z", [(i, (i + 1) % size) for i in range(size)])


def gather_team(rows):
    other = swap_along(rows, "x")
    near = jnp.concatenate([rows, other], axis=0)
    far = swap_along(near, "core")
    return jnp.concatenate([near, far], axis=0)


def scatter_team(partial):
    half = partial.shape[0] // 2
    quarter = half // 2
    got = swap_along(partial[half:].astype(jnp.bfloat16), "core")
    kept = partial[:half].astype(jnp.float32) + got.astype(jnp.float32)
    got = swap_along(kept[quarter:].astype(jnp.bfloat16), "x")
    return kept[:quarter] + got.astype(jnp.float32)


def gather_weight(mine):
    held = [mine]
    for _ in range(lax.axis_size("z") - 1):
        held.append(pass_on(held[-1]))
    return (held, [swap_along(piece, "y") for piece in held[1:]])


def reduce_weight(grad):
    depth = lax.axis_size("z")
    half = grad.shape[0] // 2
    piece = half // depth
    got = swap_along(grad[half:], "y")
    parts = [
        grad[k * piece : (k + 1) * piece].astype(jnp.float32)
        + got[k * piece : (k + 1) * piece].astype(jnp.float32)
        for k in range(depth)
    ]
    total = parts[1].astype(jnp.bfloat16)
    for k in list(range(2, depth)) + [0]:
        total = (parts[k] + pass_on(total).astype(jnp.float32)).astype(jnp.bfloat16)
    return total


def gather_plane(piece):
    half = piece.shape[0] // 2
    by_x = swap_along(piece, "x")
    by_y = swap_along(piece, "y")
    corner_top = swap_along(by_y[:half], "x")
    corner_low = swap_along(by_x[half:], "y")
    near = jnp.concatenate([piece, by_x, by_y, corner_top, corner_low], axis=0)
    far = swap_along(near, "core")
    size = piece.shape[0]
    found = []
    for core_flip, array in ((0, near), (1, far)):
        for index, (x_flip, y_flip) in enumerate(((0, 0), (1, 0), (0, 1), (1, 1))):
            code = 4 * x_flip + 2 * core_flip + y_flip
            found.append((code, array[index * size : (index + 1) * size]))
    return found


def total_all(vector):
    for axis in ("core", "x", "y"):
        vector = vector + swap_along(vector, axis)
    size = lax.axis_size("z")
    for step in (1, 2):
        vector = vector + lax.ppermute(vector, "z", [(i, i ^ step) for i in range(size)])
    return vector


def held_before(bound, residue, parts):
    return (bound + (parts - 1) - residue) // parts


def piece_tables(lengths, starts, quarter_low, quarter_rows, residue, parts):
    ends = running_sum(lengths)
    firsts = ends - lengths
    shift = starts - firsts
    low = jnp.maximum(firsts, quarter_low)
    high = jnp.minimum(ends, quarter_low + quarter_rows)
    begin = held_before(low + shift, residue, parts)
    count = jnp.where(high > low, held_before(high + shift, residue, parts) - begin, 0)
    return (begin, count, shift)


def slot_lookup(begin, count, value_of):
    base = running_sum(count) - count
    slot = jnp.arange(SLOTS, dtype=jnp.int32)
    inside = (slot >= base[..., None]) & (slot < (base + count)[..., None])
    held = begin[..., None] + slot - base[..., None]
    return jnp.sum(jnp.where(inside, value_of(held) + 1, 0), axis=-2, dtype=jnp.int32) - 1


def one_hot(wanted, count, dtype=jnp.bfloat16):
    return (wanted[:, None] == jnp.arange(count, dtype=jnp.int32)[None, :]).astype(dtype)


def layer(
    tokens,
    cotangent,
    lengths,
    dealing,
    query_weight,
    key_weight,
    value_weight,
    out_weight,
    query_bias,
    value_bias,
    out_bias,
    up_weight,
    up_bias,
    down_weight,
    down_bias,
    attn_gain,
    attn_shift,
    mlp_gain,
    mlp_shift,
):
    tok_rows = tokens.shape[1]
    col_width = tokens.shape[2]
    width = out_weight.shape[1]
    seq_dev = lengths.shape[2]
    depth = lax.axis_size("z")
    parts = lax.axis_size("y") * 4
    own_rows = tok_rows // 4
    y, x, core, z = (lax.axis_index(name) for name in ("y", "x", "core", "z"))
    team = 2 * x + core
    eighth = 2 * team + y
    residue = 4 * y + team
    group = 2 * z + y

    given_off = []
    for micro_step in range(MICRO):
        given_off.append(given_layout(lengths[micro_step], dealing[micro_step])[2])
    starts = jnp.stack(given_off).reshape(lengths.shape)
    quarter_low = (jnp.arange(4, dtype=jnp.int32) * own_rows)[None, None, :, None]
    begin, count, _ = piece_tables(
        lengths[:, :, None, :], starts[:, :, None, :], quarter_low, own_rows, residue, parts
    )
    micro_ids = jnp.arange(MICRO, dtype=jnp.int32)[:, None, None, None]
    begin = jnp.transpose(begin + micro_ids * tok_rows, (1, 2, 0, 3)).reshape(-1, MICRO * seq_dev)
    count = jnp.transpose(count, (1, 2, 0, 3)).reshape(-1, MICRO * seq_dev)
    send_row = slot_lookup(begin, count, lambda held: held).reshape(-1)

    my_lengths = lax.dynamic_index_in_dim(lengths, group, 1, keepdims=False)
    my_starts = lax.dynamic_index_in_dim(starts, group, 1, keepdims=False)
    residues = jnp.arange(parts, dtype=jnp.int32)[:, None, None]
    my_begin, my_count, my_shift = piece_tables(
        my_lengths[None], my_starts[None], team * own_rows, own_rows, residues, parts
    )
    flat = (parts, MICRO * seq_dev)
    row_shift = (
        my_shift + team * own_rows - jnp.arange(MICRO, dtype=jnp.int32)[None, :, None] * own_rows
    )
    row_shift = jnp.broadcast_to(row_shift, my_count.shape).reshape(flat)
    own_row = slot_lookup(
        my_begin.reshape(flat),
        my_count.reshape(flat),
        lambda held: held * parts + residues - row_shift[..., None],
    ).reshape(-1)
    spread_hot = one_hot(send_row, MICRO * tok_rows)
    spread_hot_t = one_hot(send_row, MICRO * tok_rows).T
    settle_hot = (
        own_row[None, :] == jnp.arange(MICRO * own_rows, dtype=jnp.int32)[:, None]
    ).astype(jnp.bfloat16)
    settle_hot_t = one_hot(own_row, MICRO * own_rows)

    def deal(array):
        spread = array.reshape(MICRO, tok_rows // parts, parts, col_width)
        spread = lax.all_to_all(spread, PLANE, split_axis=2, concat_axis=1, tiled=True)
        spread = spread.reshape(MICRO * tok_rows, col_width)
        sent = matmul(spread_hot, spread).astype(jnp.bfloat16)
        got = lax.all_to_all(sent, EVERY, split_axis=0, concat_axis=0, tiled=True)
        got = got.reshape(depth, parts * SLOTS, col_width)
        columns = [matmul(settle_hot, got[k]).astype(jnp.bfloat16) for k in range(depth)]
        return jnp.concatenate(columns, axis=1)

    def undeal(array):
        sent = [
            matmul(settle_hot_t, array[:, k * col_width : (k + 1) * col_width]).astype(jnp.bfloat16)
            for k in range(depth)
        ]
        sent = jnp.concatenate(sent, axis=0)
        got = lax.all_to_all(sent, EVERY, split_axis=0, concat_axis=0, tiled=True)
        held = matmul(spread_hot_t, got).astype(jnp.bfloat16)
        held = held.reshape(MICRO, tok_rows, 1, col_width)
        back = lax.all_to_all(held, PLANE, split_axis=1, concat_axis=2, tiled=True)
        return back.reshape(MICRO, tok_rows, col_width)

    head_rows = HEAD_DIM
    team_cols = query_weight.shape[1] // 4
    team_units = up_weight.shape[1] // 4
    half_units = team_units // 2

    def team_slice(array, axis):
        return lax.dynamic_slice_in_dim(array, team * (array.shape[axis] // 4), array.shape[axis] // 4, axis)

    def halves(array):
        size = array.shape[0] // 2
        return (
            lax.dynamic_slice_in_dim(array, y * size, size, 0),
            lax.dynamic_slice_in_dim(array, (1 - y) * size, size, 0),
        )

    attn_parts = [
        halves(team_slice(array, 1).T) for array in (query_weight, key_weight, value_weight)
    ] + [halves(team_slice(out_weight, 0))]
    attn_mine = jnp.concatenate([part[0] for part in attn_parts], axis=0)
    attn_other = jnp.concatenate([part[1] for part in attn_parts], axis=0)
    up_mine, up_other = halves(team_slice(up_weight, 1).T)
    down_mine, down_other = halves(team_slice(down_weight, 0))

    bias_pack = jnp.concatenate([query_bias, value_bias, up_bias]).astype(jnp.float32).reshape(-1, 128)
    bias_held = [bias_pack]
    for _ in range(depth - 1):
        bias_held.append(pass_on(bias_held[-1]))
    bias_held = [bias.reshape(-1) for bias in bias_held]

    def bias_of(offset, size):
        return jnp.concatenate(
            [
                lax.dynamic_slice_in_dim(bias, offset + (2 * team + half) * size, size)
                for half in (y, 1 - y)
                for bias in bias_held
            ]
        )

    shard_heads = query_weight.shape[1]
    query_b = bias_of(0, HEAD_DIM)
    value_b = bias_of(shard_heads, HEAD_DIM)
    up_b = bias_of(2 * shard_heads, half_units)
    qkv_b = jnp.concatenate([query_b, jnp.zeros_like(query_b), value_b])

    tok = deal(tokens)
    attn_held, attn_got = gather_weight(attn_mine)
    attn_all = attn_held + [attn_other] + attn_got
    qkv_w = jnp.concatenate(
        [piece[k * head_rows : (k + 1) * head_rows] for k in range(3) for piece in attn_all], axis=0
    )
    out_w = jnp.concatenate([piece[3 * head_rows :] for piece in attn_all], axis=0)
    cot = deal(cotangent)
    up_held, up_got = gather_weight(up_mine)
    up_w = jnp.concatenate(up_held + [up_other] + up_got, axis=0)
    down_held, down_got = gather_weight(down_mine)
    down_w = jnp.concatenate(down_held + [down_other] + down_got, axis=0)

    gain_one, shift_one, gain_two, shift_two, out_b, down_b = (
        array.astype(jnp.float32)
        for array in (attn_gain, attn_shift, mlp_gain, mlp_shift, out_bias, down_bias)
    )

    rank = jnp.full((1,), team, jnp.int32)
    infos = []
    for micro_step in range(MICRO):
        holder, position, _ = buffer_layout(my_lengths[micro_step], my_starts[micro_step], tok_rows)
        segment = holder * tok_rows + position // (SEG + SUMM)
        summary = jnp.where(position % (SEG + SUMM) >= SEG, holder, -1)
        infos.append((jnp.stack([segment, summary], axis=1), jnp.stack([segment, holder], axis=0)))

    layer_rows = []
    input_rows = []
    kept = []
    for m in range(MICRO):
        rows = tok[m * own_rows : (m + 1) * own_rows].astype(jnp.float32)
        cot_rows = cot[m * own_rows : (m + 1) * own_rows]
        normed_one, inverse_one = normalize(rows)
        first_in = gather_team((normed_one * gain_one + shift_one).astype(jnp.bfloat16))
        qkv = (times_transpose(first_in, qkv_w) + qkv_b).astype(jnp.bfloat16)
        mixed = attend(qkv, rank, *infos[m])
        resid = rows + scatter_team(matmul(mixed, out_w)) + out_b
        normed_two, inverse_two = normalize(resid.astype(jnp.bfloat16).astype(jnp.float32))
        second_in = gather_team((normed_two * gain_two + shift_two).astype(jnp.bfloat16))
        cot_all = gather_team(cot_rows)
        hidden_pre = times_transpose(second_in, up_w) + up_b
        hidden_act, gelu_pull = jax.vjp(gelu_tanh, hidden_pre)
        hidden = hidden_act.astype(jnp.bfloat16)
        hidden_grad = gelu_pull(times_transpose(cot_all, down_w))[0]
        hidden_low = hidden_grad.astype(jnp.bfloat16)
        layer_rows.append((resid + scatter_team(matmul(hidden, down_w)) + down_b).astype(jnp.bfloat16))
        second_grad = scatter_team(matmul(hidden_low, up_w)).astype(jnp.bfloat16).astype(jnp.float32)
        back, gain_two_part, shift_two_part = norm_backward(second_grad, normed_two, inverse_two, gain_two)
        resid_grad = cot_rows.astype(jnp.float32) + back
        attn_low = gather_team(resid_grad.astype(jnp.bfloat16))
        mixed_grad = times_transpose(attn_low, out_w).astype(jnp.bfloat16)
        query_low, key_low, value_low, sums = attend_back(qkv, mixed_grad, rank, *infos[m])
        qkv_low = jnp.concatenate([query_low, key_low, value_low], axis=1)
        first_grad = scatter_team(matmul(qkv_low, qkv_w)).astype(jnp.bfloat16).astype(jnp.float32)
        back, gain_one_part, shift_one_part = norm_backward(first_grad, normed_one, inverse_one, gain_one)
        input_rows.append((resid_grad + back).astype(jnp.bfloat16))
        kept.append(
            dict(
                up=cross_rows(hidden_low, second_in),
                down=cross_rows(hidden, cot_all),
                out=cross_rows(mixed, attn_low),
                qkv=cross_rows(qkv_low, first_in),
                query_b=sums[0],
                value_b=sums[1],
                up_b=jnp.sum(hidden_grad, axis=0),
                vectors=(
                    jnp.sum(resid_grad, axis=0),
                    jnp.sum(cot_rows.astype(jnp.float32), axis=0),
                    gain_one_part,
                    shift_one_part,
                    gain_two_part,
                    shift_two_part,
                ),
            )
        )

    layer_out = undeal(jnp.concatenate(layer_rows, axis=0))

    def both(name):
        return (kept[0][name] + kept[1][name]).astype(jnp.bfloat16)

    def into(pieces, rows_per, start, size):
        shard = jnp.zeros((8 * size, width), jnp.bfloat16)
        for code, piece in pieces:
            at = jnp.bitwise_xor(eighth, code)
            shard = lax.dynamic_update_slice(shard, piece[start : start + size], (at * size, 0))
        return shard.astype(jnp.float32)

    down_grad = into(gather_plane(reduce_weight(both("down"))), half_units, 0, half_units)
    up_grad = into(gather_plane(reduce_weight(both("up"))), half_units, 0, half_units).T
    qkv_grad = both("qkv")
    out_grad = both("out")
    heads = qkv_grad.shape[0] // 3
    attn_grad = jnp.concatenate(
        [
            array[k * head_rows : (k + 1) * head_rows]
            for k in range(2 * depth)
            for array in (qkv_grad[:heads], qkv_grad[heads : 2 * heads], qkv_grad[2 * heads :], out_grad)
        ],
        axis=0,
    )
    attn_pieces = gather_plane(reduce_weight(attn_grad))
    query_grad, key_grad, value_grad, out_w_grad = (
        into(attn_pieces, 4 * head_rows, k * head_rows, head_rows) for k in range(4)
    )

    def place(vector, shard_size, size):
        whole = jnp.zeros((depth * shard_size,), jnp.float32)
        for index in range(2 * depth):
            half = y if index < depth else 1 - y
            owner = lax.rem(z - index % depth + depth, depth)
            whole = lax.dynamic_update_slice(
                whole,
                vector[index * size : (index + 1) * size],
                (owner * shard_size + (2 * team + half) * size,),
            )
        return whole

    small = [kept[0][name] + kept[1][name] for name in ("query_b", "value_b", "up_b")]
    vectors = [
        place(small[0], shard_heads, HEAD_DIM),
        place(small[1], shard_heads, HEAD_DIM),
        place(small[2], up_weight.shape[1], half_units),
    ] + [kept[0]["vectors"][k] + kept[1]["vectors"][k] for k in range(6)]
    sizes = [vector.shape[0] for vector in vectors]
    packed = total_all(jnp.concatenate(vectors).reshape(-1, 128)).reshape(-1)
    pieces = []
    offset = 0
    for size in sizes:
        pieces.append(packed[offset : offset + size])
        offset += size
    query_b_grad, value_b_grad, up_b_grad, out_b_grad, down_b_grad, *norm_grads = pieces

    def own_shard(vector):
        size = vector.shape[0] // depth
        return lax.dynamic_slice_in_dim(vector, z * size, size)

    input_grad = undeal(jnp.concatenate(input_rows, axis=0))
    return (
        layer_out,
        input_grad,
        query_grad.T,
        key_grad.T,
        value_grad.T,
        out_w_grad,
        own_shard(query_b_grad),
        own_shard(value_b_grad),
        out_b_grad,
        up_grad,
        own_shard(up_b_grad),
        down_grad,
        down_b_grad,
        *norm_grads,
    )


def team_layer(mesh):
    axes = ("y", "x", "core", "z")
    inner = Mesh(mesh.devices.reshape(2, 2, 2, 4), axes)
    rows = P(None, PLANE, "z")
    in_specs = (
        rows, rows, P(), P(), P(None, "z"), P(None, "z"), P(None, "z"), P("z", None), P("z"), P("z"),
        P(), P(None, "z"), P("z"), P("z", None), P(), P(), P(), P(), P(),
    )
    out_specs = (
        rows, rows, P(None, "z"), P(None, "z"), P(None, "z"), P("z", None), P("z"), P("z"),
        P(), P(None, "z"), P("z"), P("z", None), P(), P(), P(), P(), P(),
    )
    return jax.shard_map(layer, mesh=inner, in_specs=in_specs, out_specs=out_specs, check_vma=False)


def solution(mesh):
    if dict(mesh.shape) == {"dp": 8, "tensor": 4}:
        return team_layer(mesh)
    return general_layer(mesh)
```

```python
import functools

import jax
import jax.numpy as jnp
from jax import lax
from jax.experimental import pallas as pl
from jax.experimental.pallas import tpu as pltpu
from jax.sharding import Mesh
from jax.sharding import PartitionSpec as P


HEAD_DIM = 64
SEG = 512
SUMM = 50
NBLK = 2


NORM_EPS = 1e-05
MASKED = -1e30


def gelu_tanh(values):
    return jax.nn.gelu(values, approximate=True)


def matmul(left_array, right_array):
    return jnp.dot(left_array, right_array, preferred_element_type=jnp.float32)


def cross_rows(left_array, right_array):
    return lax.dot_general(
        left_array, right_array, (((0,), (0,)), ((), ())), preferred_element_type=jnp.float32
    )


def times_transpose(left_array, right_array):
    return lax.dot_general(
        left_array, right_array, (((1,), (1,)), ((), ())), preferred_element_type=jnp.float32
    )


def normalize(values):
    center = jnp.mean(values, axis=1, keepdims=True)
    shifted = values - center
    spread = jnp.mean(shifted * shifted, axis=1, keepdims=True)
    inverse = lax.rsqrt(spread + NORM_EPS)
    return (shifted * inverse, inverse)


def norm_backward(grad_in, normed, inverse, gain_row):
    gain_grad = jnp.sum(grad_in * normed, axis=0)
    shift_grad = jnp.sum(grad_in, axis=0)
    scaled = grad_in * gain_row
    first_mean = jnp.mean(scaled, axis=1, keepdims=True)
    second_mean = jnp.mean(scaled * normed, axis=1, keepdims=True)
    return (inverse * (scaled - first_mean - normed * second_mean), gain_grad, shift_grad)


def running_sum(counts):
    size = counts.shape[-1]
    places = jnp.arange(size, dtype=jnp.int32)
    upto = (places[:, None] <= places[None, :]).astype(jnp.int32)
    return jnp.sum(counts[..., :, None] * upto, axis=-2, dtype=jnp.int32)


def given_layout(lengths_mb, dealing_mb):
    seq_count = dealing_mb.shape[0]
    labels = jnp.arange(seq_count, dtype=jnp.int32)
    flat_lengths = lengths_mb.reshape(seq_count)
    one_hot = (dealing_mb[:, None] == labels[None, :]).astype(jnp.int32)
    given_len = jnp.sum(one_hot * flat_lengths[None, :], axis=1, dtype=jnp.int32)
    given_off = running_sum(given_len) - given_len
    start_by_seq = jnp.sum(one_hot * given_off[:, None], axis=0, dtype=jnp.int32)
    return (given_len, given_off, start_by_seq)


def buffer_layout(lengths_dev, start_dev, rows_total):
    seq_count = lengths_dev.shape[0]
    end_rows = running_sum(lengths_dev)
    offsets = end_rows - lengths_dev
    row_ids = jnp.arange(rows_total, dtype=jnp.int32)
    holder = jnp.sum(
        (row_ids[:, None] >= end_rows[None, :]).astype(jnp.int32), axis=1, dtype=jnp.int32
    )
    one_hot = (holder[:, None] == jnp.arange(seq_count, dtype=jnp.int32)[None, :]).astype(jnp.int32)
    position = row_ids - jnp.sum(one_hot * offsets[None, :], axis=1, dtype=jnp.int32)
    source = jnp.sum(one_hot * start_dev[None, :], axis=1, dtype=jnp.int32) + position
    return (holder, position, source)


def visible(holder, position, first_row, last_row, key_reach):
    period = SEG + SUMM
    query_seq = holder[first_row:last_row, None]
    key_seq = holder[None, :key_reach]
    query_part = position[first_row:last_row, None] // period
    key_part = position[None, :key_reach] // period
    summary = position[None, :key_reach] % period >= SEG
    query_row = jnp.arange(first_row, last_row, dtype=jnp.int32)[:, None]
    key_row = jnp.arange(key_reach, dtype=jnp.int32)[None, :]
    same_part = (query_part == key_part) & (key_row <= query_row)
    earlier = (key_part < query_part) & summary
    return (query_seq == key_seq) & (same_part | earlier)


def block_scores(queries, keys_all, allowed, score_scale):
    scores = (
        jnp.einsum("qhd,khd->hqk", queries, keys_all, preferred_element_type=jnp.float32)
        * score_scale
    )
    return jnp.where(allowed[None], scores, MASKED)


def shards(
    tokens,
    cotangent,
    lengths,
    dealing,
    query_weight,
    key_weight,
    value_weight,
    out_weight,
    query_bias,
    value_bias,
    out_bias,
    up_weight,
    up_bias,
    down_weight,
    down_bias,
    attn_gain,
    attn_shift,
    mlp_gain,
    mlp_shift,
):
    micro_count = tokens.shape[0]
    tok_rows = tokens.shape[1]
    col_width = tokens.shape[2]
    seq_dev = lengths.shape[2]
    heads_here = query_weight.shape[1] // HEAD_DIM
    head_cols = heads_here * HEAD_DIM
    block_rows = tok_rows // NBLK
    score_scale = HEAD_DIM ** (-0.5)
    device = lax.axis_index("dp")
    column = lax.axis_index("tensor")
    gain_one = attn_gain.astype(jnp.float32)
    shift_one = attn_shift.astype(jnp.float32)
    gain_two = mlp_gain.astype(jnp.float32)
    shift_two = mlp_shift.astype(jnp.float32)
    query_bias_f = query_bias.astype(jnp.float32)
    value_bias_f = value_bias.astype(jnp.float32)
    up_bias_f = up_bias.astype(jnp.float32)
    out_bias_cols = lax.dynamic_slice_in_dim(
        out_bias.astype(jnp.float32), column * col_width, col_width
    )
    down_bias_cols = lax.dynamic_slice_in_dim(
        down_bias.astype(jnp.float32), column * col_width, col_width
    )
    query_w_grad = jnp.zeros(query_weight.shape, jnp.float32)
    key_w_grad = jnp.zeros(key_weight.shape, jnp.float32)
    value_w_grad = jnp.zeros(value_weight.shape, jnp.float32)
    out_w_grad = jnp.zeros(out_weight.shape, jnp.float32)
    query_b_grad = jnp.zeros(query_bias.shape, jnp.float32)
    value_b_grad = jnp.zeros(value_bias.shape, jnp.float32)
    out_b_grad = jnp.zeros(out_bias.shape, jnp.float32)
    up_w_grad = jnp.zeros(up_weight.shape, jnp.float32)
    up_b_grad = jnp.zeros(up_bias.shape, jnp.float32)
    down_w_grad = jnp.zeros(down_weight.shape, jnp.float32)
    down_b_grad = jnp.zeros(down_bias.shape, jnp.float32)
    gain_one_grad = jnp.zeros(attn_gain.shape, jnp.float32)
    shift_one_grad = jnp.zeros(attn_shift.shape, jnp.float32)
    gain_two_grad = jnp.zeros(mlp_gain.shape, jnp.float32)
    shift_two_grad = jnp.zeros(mlp_shift.shape, jnp.float32)
    layer_parts = []
    grad_parts = []
    for micro_step in range(micro_count):
        lengths_mb = lengths[micro_step]
        dealing_mb = dealing[micro_step]
        given_len, given_off, start_by_seq = given_layout(lengths_mb, dealing_mb)
        lengths_dev = lax.dynamic_index_in_dim(lengths_mb, device, 0, keepdims=False)
        start_dev = lax.dynamic_slice_in_dim(start_by_seq, device * seq_dev, seq_dev)
        holder, position, source = buffer_layout(lengths_dev, start_dev, tok_rows)
        blank_rows = jnp.zeros((tok_rows, col_width), jnp.bfloat16)
        pieces = (
            lax.all_gather(tokens[micro_step], "dp", axis=0, tiled=True),
            lax.all_gather(cotangent[micro_step], "dp", axis=0, tiled=True),
        )
        span_rows = pieces[0].shape[0]
        inside = ((source >= 0) & (source < span_rows))[:, None]
        fetch_at = jnp.clip(source, 0, span_rows - 1)
        tok_buf = jnp.where(inside, jnp.take(pieces[0], fetch_at, axis=0), blank_rows)
        cot_buf = jnp.where(inside, jnp.take(pieces[1], fetch_at, axis=0), blank_rows)
        tok_full, cot_full = (
            lax.all_gather(tok_buf, "tensor", axis=1, tiled=True),
            lax.all_gather(cot_buf, "tensor", axis=1, tiled=True),
        )
        normed_one, inverse_one = normalize(tok_full.astype(jnp.float32))
        first_in = (normed_one * gain_one + shift_one).astype(jnp.bfloat16)
        queries = (
            (matmul(first_in, query_weight) + query_bias_f)
            .astype(jnp.bfloat16)
            .reshape(tok_rows, heads_here, HEAD_DIM)
        )
        keys_here = (
            matmul(first_in, key_weight)
            .astype(jnp.bfloat16)
            .reshape(tok_rows, heads_here, HEAD_DIM)
        )
        values_here = (
            (matmul(first_in, value_weight) + value_bias_f)
            .astype(jnp.bfloat16)
            .reshape(tok_rows, heads_here, HEAD_DIM)
        )
        outputs = []
        row_tops = []
        row_totals = []
        for block_index in range(NBLK):
            row_lower = block_index * block_rows
            row_upper = row_lower + block_rows
            allowed = visible(holder, position, row_lower, row_upper, row_upper)
            scores = block_scores(
                queries[row_lower:row_upper], keys_here[:row_upper], allowed, score_scale
            )
            row_top = jnp.max(scores, axis=2, keepdims=True)
            exp_terms = jnp.exp(scores - row_top)
            row_total = jnp.sum(exp_terms, axis=2, keepdims=True)
            attn_prob = exp_terms / row_total
            outputs.append(
                jnp.einsum(
                    "hqk,khd->qhd",
                    attn_prob.astype(jnp.bfloat16),
                    values_here[:row_upper],
                    preferred_element_type=jnp.float32,
                )
            )
            row_tops.append(row_top)
            row_totals.append(row_total)
        mixed_heads = (
            jnp.concatenate(outputs, axis=0).reshape(tok_rows, head_cols).astype(jnp.bfloat16)
        )
        attn_cols = lax.psum_scatter(
            matmul(mixed_heads, out_weight), "tensor", scatter_dimension=1, tiled=True
        )
        resid_cols = tok_buf.astype(jnp.float32) + attn_cols + out_bias_cols
        resid_full = lax.all_gather(resid_cols.astype(jnp.bfloat16), "tensor", axis=1, tiled=True)
        normed_two, inverse_two = normalize(resid_full.astype(jnp.float32))
        second_in = (normed_two * gain_two + shift_two).astype(jnp.bfloat16)
        hidden_pre = matmul(second_in, up_weight) + up_bias_f
        hidden_act, gelu_pull = jax.vjp(gelu_tanh, hidden_pre)
        hidden = hidden_act.astype(jnp.bfloat16)
        mlp_cols = lax.psum_scatter(
            matmul(hidden, down_weight).astype(jnp.bfloat16),
            "tensor",
            scatter_dimension=1,
            tiled=True,
        ).astype(jnp.float32)
        layer_cols = (resid_cols + mlp_cols + down_bias_cols).astype(jnp.bfloat16)
        grad_out = cot_full.astype(jnp.float32)
        down_w_grad = down_w_grad + cross_rows(hidden, cot_full)
        down_b_grad = down_b_grad + jnp.sum(grad_out, axis=0)
        hidden_grad = gelu_pull(times_transpose(cot_full, down_weight))[0]
        up_b_grad = up_b_grad + jnp.sum(hidden_grad, axis=0)
        hidden_low = hidden_grad.astype(jnp.bfloat16)
        up_w_grad = up_w_grad + cross_rows(second_in, hidden_low)
        second_cols = lax.psum_scatter(
            times_transpose(hidden_low, up_weight), "tensor", scatter_dimension=1, tiled=True
        )
        second_grad = lax.all_gather(
            second_cols.astype(jnp.bfloat16), "tensor", axis=1, tiled=True
        ).astype(jnp.float32)
        resid_back, gain_part, shift_part = norm_backward(
            second_grad, normed_two, inverse_two, gain_two
        )
        gain_two_grad = gain_two_grad + gain_part
        shift_two_grad = shift_two_grad + shift_part
        resid_grad = grad_out + resid_back
        out_b_grad = out_b_grad + jnp.sum(resid_grad, axis=0)
        attn_low = resid_grad.astype(jnp.bfloat16)
        out_w_grad = out_w_grad + cross_rows(mixed_heads, attn_low)
        mixed_grad = (
            times_transpose(attn_low, out_weight)
            .astype(jnp.bfloat16)
            .reshape(tok_rows, heads_here, HEAD_DIM)
        )
        query_parts = []
        key_acc = jnp.zeros((tok_rows, heads_here, HEAD_DIM), jnp.float32)
        value_acc = jnp.zeros((tok_rows, heads_here, HEAD_DIM), jnp.float32)
        for block_index in range(NBLK):
            row_lower = block_index * block_rows
            row_upper = row_lower + block_rows
            allowed = visible(holder, position, row_lower, row_upper, row_upper)
            scores = block_scores(
                queries[row_lower:row_upper], keys_here[:row_upper], allowed, score_scale
            )
            attn_prob = jnp.exp(scores - row_tops[block_index]) / row_totals[block_index]
            grad_block = mixed_grad[row_lower:row_upper]
            prob_grad = jnp.einsum(
                "qhd,khd->hqk",
                grad_block,
                values_here[:row_upper],
                preferred_element_type=jnp.float32,
            )
            inner_sum = jnp.sum(attn_prob * prob_grad, axis=2, keepdims=True)
            score_grad = (attn_prob * (prob_grad - inner_sum)).astype(jnp.bfloat16)
            query_parts.append(
                jnp.einsum(
                    "hqk,khd->qhd",
                    score_grad,
                    keys_here[:row_upper],
                    preferred_element_type=jnp.float32,
                )
                * score_scale
            )
            pad_rows = ((0, tok_rows - row_upper), (0, 0), (0, 0))
            key_acc = key_acc + jnp.pad(
                jnp.einsum(
                    "hqk,qhd->khd",
                    score_grad,
                    queries[row_lower:row_upper],
                    preferred_element_type=jnp.float32,
                )
                * score_scale,
                pad_rows,
            )
            value_acc = value_acc + jnp.pad(
                jnp.einsum(
                    "hqk,qhd->khd",
                    attn_prob.astype(jnp.bfloat16),
                    grad_block,
                    preferred_element_type=jnp.float32,
                ),
                pad_rows,
            )
        query_grad = jnp.concatenate(query_parts, axis=0).reshape(tok_rows, head_cols)
        key_grad = key_acc.reshape(tok_rows, head_cols)
        value_grad = value_acc.reshape(tok_rows, head_cols)
        query_b_grad = query_b_grad + jnp.sum(query_grad, axis=0)
        value_b_grad = value_b_grad + jnp.sum(value_grad, axis=0)
        query_low = query_grad.astype(jnp.bfloat16)
        key_low = key_grad.astype(jnp.bfloat16)
        value_low = value_grad.astype(jnp.bfloat16)
        query_w_grad = query_w_grad + cross_rows(first_in, query_low)
        key_w_grad = key_w_grad + cross_rows(first_in, key_low)
        value_w_grad = value_w_grad + cross_rows(first_in, value_low)
        first_part = (
            times_transpose(query_low, query_weight)
            + times_transpose(key_low, key_weight)
            + times_transpose(value_low, value_weight)
        )
        first_cols = lax.psum_scatter(first_part, "tensor", scatter_dimension=1, tiled=True)
        first_grad = lax.all_gather(
            first_cols.astype(jnp.bfloat16), "tensor", axis=1, tiled=True
        ).astype(jnp.float32)
        input_back, gain_part, shift_part = norm_backward(
            first_grad, normed_one, inverse_one, gain_one
        )
        gain_one_grad = gain_one_grad + gain_part
        shift_one_grad = shift_one_grad + shift_part
        input_cols = lax.dynamic_slice_in_dim(
            resid_grad + input_back, column * col_width, col_width, axis=1
        ).astype(jnp.bfloat16)
        packed = jnp.concatenate([layer_cols, input_cols], axis=1)
        given_end = given_off + given_len
        dest_off = (running_sum(lengths_mb) - lengths_mb).reshape(-1)
        labels = jnp.arange(dealing_mb.shape[0], dtype=jnp.int32)
        give_row_ids = jnp.arange(tok_rows * lax.axis_size("dp"), dtype=jnp.int32)
        owner_seq = jnp.sum(
            (give_row_ids[:, None] >= given_end[None, :]).astype(jnp.int32), axis=1, dtype=jnp.int32
        )
        one_hot = (owner_seq[:, None] == labels[None, :]).astype(jnp.int32)
        within = give_row_ids - jnp.sum(one_hot * given_off[None, :], axis=1, dtype=jnp.int32)
        seq_label = jnp.sum(one_hot * dealing_mb[None, :], axis=1, dtype=jnp.int32)
        seq_hot = (seq_label[:, None] == labels[None, :]).astype(jnp.int32)
        buffer_row = jnp.sum(seq_hot * dest_off[None, :], axis=1, dtype=jnp.int32) + within
        owner_dev = seq_label // seq_dev
        is_mine = owner_dev == device
        fetched = jnp.take(packed, jnp.clip(buffer_row, 0, tok_rows - 1), axis=0).astype(
            jnp.float32
        )
        returned = lax.psum_scatter(
            jnp.where(is_mine[:, None], fetched, 0.0).astype(jnp.bfloat16),
            "dp",
            scatter_dimension=0,
            tiled=True,
        ).astype(jnp.float32)
        layer_parts.append(returned[:, :col_width].astype(jnp.bfloat16))
        grad_parts.append(returned[:, col_width:].astype(jnp.bfloat16))
    (
        query_w_grad,
        key_w_grad,
        value_w_grad,
        out_w_grad,
        query_b_grad,
        value_b_grad,
        out_b_grad,
        gain_one_grad,
        shift_one_grad,
        up_w_grad,
        up_b_grad,
        down_w_grad,
        down_b_grad,
        gain_two_grad,
        shift_two_grad,
    ) = lax.psum(
        (
            query_w_grad,
            key_w_grad,
            value_w_grad,
            out_w_grad,
            query_b_grad,
            value_b_grad,
            out_b_grad,
            gain_one_grad,
            shift_one_grad,
            up_w_grad,
            up_b_grad,
            down_w_grad,
            down_b_grad,
            gain_two_grad,
            shift_two_grad,
        ),
        "dp",
    )
    layer_out = jnp.stack(layer_parts, axis=0)
    input_grad = jnp.stack(grad_parts, axis=0)
    return (
        layer_out,
        input_grad,
        query_w_grad,
        key_w_grad,
        value_w_grad,
        out_w_grad,
        query_b_grad,
        value_b_grad,
        out_b_grad,
        up_w_grad,
        up_b_grad,
        down_w_grad,
        down_b_grad,
        gain_one_grad,
        shift_one_grad,
        gain_two_grad,
        shift_two_grad,
    )


def general_layer(mesh):
    in_specs = (
        P(None, "dp", "tensor"),
        P(None, "dp", "tensor"),
        P(),
        P(),
        P(None, "tensor"),
        P(None, "tensor"),
        P(None, "tensor"),
        P("tensor", None),
        P("tensor"),
        P("tensor"),
        P(),
        P(None, "tensor"),
        P("tensor"),
        P("tensor", None),
        P(),
        P(),
        P(),
        P(),
        P(),
    )
    out_specs = (
        P(None, "dp", "tensor"),
        P(None, "dp", "tensor"),
        P(None, "tensor"),
        P(None, "tensor"),
        P(None, "tensor"),
        P("tensor", None),
        P("tensor"),
        P("tensor"),
        P(),
        P(None, "tensor"),
        P("tensor"),
        P("tensor", None),
        P(),
        P(),
        P(),
        P(),
        P(),
    )
    return jax.shard_map(shards, mesh=mesh, in_specs=in_specs, out_specs=out_specs, check_vma=False)


ROWS = 1024
QBLK = 256
PAIR = 128


def slot_of(block, rank):
    piece = jnp.bitwise_xor(block, rank)
    return jnp.bitwise_or(piece >> 1, (piece & 1) << 1)


def rows_of(block, rank):
    return pl.ds(pl.multiple_of(slot_of(block, rank) * QBLK, QBLK), QBLK)


def fill_bias(bias_ref, key_info_ref, query_info_ref):
    for block in range(ROWS // QBLK):
        reach = (block + 1) * QBLK
        cols = pl.ds(block * QBLK, QBLK)
        key_part = key_info_ref[pl.ds(0, reach), 0:1]
        key_summary = key_info_ref[pl.ds(0, reach), 1:2]
        query_part = query_info_ref[0:1, cols]
        query_seq = query_info_ref[1:2, cols]
        key_row = lax.broadcasted_iota(jnp.int32, (reach, QBLK), 0)
        query_row = lax.broadcasted_iota(jnp.int32, (reach, QBLK), 1) + block * QBLK
        seen = (key_row <= query_row) & ((key_part == query_part) | (key_summary == query_seq))
        bias_ref[pl.ds(0, reach), cols] = jnp.where(seen, 0.0, MASKED)


def nt_dot(left, right):
    return lax.dot_general(left, right, (((1,), (1,)), ((), ())), preferred_element_type=jnp.float32)


def nn_dot(left, right):
    return jnp.dot(left, right, preferred_element_type=jnp.float32)


def head_lanes(block, head):
    lane = lax.broadcasted_iota(jnp.int32, block.shape, 1)
    inside = (lane >= head * HEAD_DIM) & (lane < (head + 1) * HEAD_DIM)
    return jnp.where(inside, block, jnp.zeros_like(block))


def attend_kernel(
    rank_ref, query_ref, key_ref, value_ref, key_info_ref, query_info_ref, out_ref, bias_ref, keys, value_t
):
    rank = rank_ref[0]

    @pl.when(pl.program_id(0) == 0)
    def _():
        fill_bias(bias_ref, key_info_ref, query_info_ref)

    for block in range(ROWS // QBLK):
        here = rows_of(block, rank)
        keys[pl.ds(block * QBLK, QBLK), :] = key_ref[here, :]
        value_t[:, pl.ds(block * QBLK, QBLK)] = value_ref[here, :].T
    for block in range(ROWS // QBLK):
        reach = (block + 1) * QBLK
        here = rows_of(block, rank)
        queries = query_ref[here, :] * jnp.bfloat16(HEAD_DIM**-0.5)
        bias = bias_ref[pl.ds(0, reach), pl.ds(block * QBLK, QBLK)]
        parts = []
        for head in range(2):
            scores = nt_dot(keys[pl.ds(0, reach), :], head_lanes(queries, head)) + bias
            top = jnp.max(scores, axis=0, keepdims=True)
            terms = jnp.exp(scores - top)
            total = jnp.sum(terms, axis=0, keepdims=True)
            heads_t = nn_dot(
                value_t[pl.ds(head * HEAD_DIM, HEAD_DIM), pl.ds(0, reach)], terms.astype(jnp.bfloat16)
            )
            parts.append(heads_t / total)
        out_ref[here, :] = jnp.concatenate(parts, axis=0).T.astype(out_ref.dtype)


def attend(qkv, rank, key_info, query_info):
    pairs = qkv.shape[1] // (3 * PAIR)
    cells = ROWS * ROWS * 5 // 8
    return pl.pallas_call(
        attend_kernel,
        grid_spec=pltpu.PrefetchScalarGridSpec(
            num_scalar_prefetch=1,
            grid=(pairs,),
            in_specs=[
                pl.BlockSpec((ROWS, PAIR), lambda i, r: (0, i)),
                pl.BlockSpec((ROWS, PAIR), lambda i, r: (0, pairs + i)),
                pl.BlockSpec((ROWS, PAIR), lambda i, r: (0, 2 * pairs + i)),
                pl.BlockSpec((ROWS, 2), lambda i, r: (0, 0)),
                pl.BlockSpec((2, ROWS), lambda i, r: (0, 0)),
            ],
            out_specs=pl.BlockSpec((ROWS, PAIR), lambda i, r: (0, i)),
            scratch_shapes=[
                pltpu.VMEM((ROWS, ROWS), jnp.float32),
                pltpu.VMEM((ROWS, PAIR), jnp.bfloat16),
                pltpu.VMEM((PAIR, ROWS), jnp.bfloat16),
            ],
        ),
        out_shape=jax.ShapeDtypeStruct((ROWS, pairs * PAIR), jnp.bfloat16),
        compiler_params=pltpu.CompilerParams(vmem_limit_bytes=24 << 20),
        cost_estimate=light(),
        name="attend",
    )(rank, qkv, qkv, qkv, key_info, query_info)


def attend_back_kernel(
    rank_ref,
    query_ref,
    key_ref,
    value_ref,
    grad_ref,
    key_info_ref,
    query_info_ref,
    query_out,
    key_out,
    value_out,
    sums_out,
    bias_ref,
    keys,
    values,
    key_t,
    key_acc,
    value_acc,
):
    rank = rank_ref[0]
    scale = HEAD_DIM**-0.5

    @pl.when(pl.program_id(0) == 0)
    def _():
        fill_bias(bias_ref, key_info_ref, query_info_ref)

    for block in range(ROWS // QBLK):
        here = rows_of(block, rank)
        there = pl.ds(block * QBLK, QBLK)
        keys[there, :] = key_ref[here, :]
        values[there, :] = value_ref[here, :]
        key_t[:, there] = key_ref[here, :].T
    query_sum = jnp.zeros((1, PAIR), jnp.float32)
    for block in reversed(range(ROWS // QBLK)):
        reach = (block + 1) * QBLK
        here = rows_of(block, rank)
        upto = pl.ds(0, reach)
        queries = query_ref[here, :] * jnp.bfloat16(scale)
        grads = grad_ref[here, :]
        bias = bias_ref[upto, pl.ds(block * QBLK, QBLK)]
        parts = []
        key_add = None
        value_add = None
        for head in range(2):
            query_h = head_lanes(queries, head)
            grad_h = head_lanes(grads, head)
            scores = nt_dot(keys[upto, :], query_h) + bias
            top = jnp.max(scores, axis=0, keepdims=True)
            terms = jnp.exp(scores - top)
            prob = terms * (1.0 / jnp.sum(terms, axis=0, keepdims=True))
            prob_grad = nt_dot(values[upto, :], grad_h)
            inner = jnp.sum(prob * prob_grad, axis=0, keepdims=True)
            score_grad = (prob * (prob_grad - inner)).astype(jnp.bfloat16)
            value_part = nn_dot(prob.astype(jnp.bfloat16), grad_h)
            key_part = nn_dot(score_grad, query_h)
            value_add = value_part if value_add is None else value_add + value_part
            key_add = key_part if key_add is None else key_add + key_part
            parts.append(nn_dot(key_t[pl.ds(head * HEAD_DIM, HEAD_DIM), upto], score_grad))
        if block == ROWS // QBLK - 1:
            key_acc[...] = key_add
            value_acc[...] = value_add
        else:
            key_acc[upto, :] += key_add
            value_acc[upto, :] += value_add
        query_grad = jnp.concatenate(parts, axis=0).T * scale
        query_sum = query_sum + jnp.sum(query_grad, axis=0, keepdims=True)
        query_out[here, :] = query_grad.astype(query_out.dtype)
    for block in range(ROWS // QBLK):
        here = rows_of(block, rank)
        there = pl.ds(block * QBLK, QBLK)
        key_out[here, :] = key_acc[there, :].astype(key_out.dtype)
        value_out[here, :] = value_acc[there, :].astype(value_out.dtype)
    value_sum = jnp.sum(value_acc[...], axis=0, keepdims=True)
    row = lax.broadcasted_iota(jnp.int32, (8, PAIR), 0)
    sums_out[...] = jnp.where(row == 0, query_sum, jnp.where(row == 1, value_sum, 0.0))


def attend_back(qkv, grads, rank, key_info, query_info):
    pairs = qkv.shape[1] // (3 * PAIR)
    cells = ROWS * ROWS * 5 // 8
    block = (ROWS, PAIR)
    wide = jax.ShapeDtypeStruct((ROWS, pairs * PAIR), jnp.bfloat16)
    return pl.pallas_call(
        attend_back_kernel,
        grid_spec=pltpu.PrefetchScalarGridSpec(
            num_scalar_prefetch=1,
            grid=(pairs,),
            in_specs=[
                pl.BlockSpec(block, lambda i, r: (0, i)),
                pl.BlockSpec(block, lambda i, r: (0, pairs + i)),
                pl.BlockSpec(block, lambda i, r: (0, 2 * pairs + i)),
                pl.BlockSpec(block, lambda i, r: (0, i)),
                pl.BlockSpec((ROWS, 2), lambda i, r: (0, 0)),
                pl.BlockSpec((2, ROWS), lambda i, r: (0, 0)),
            ],
            out_specs=[
                pl.BlockSpec(block, lambda i, r: (0, i)),
                pl.BlockSpec(block, lambda i, r: (0, i)),
                pl.BlockSpec(block, lambda i, r: (0, i)),
                pl.BlockSpec((8, PAIR), lambda i, r: (0, i)),
            ],
            scratch_shapes=[
                pltpu.VMEM((ROWS, ROWS), jnp.float32),
                pltpu.VMEM(block, jnp.bfloat16),
                pltpu.VMEM(block, jnp.bfloat16),
                pltpu.VMEM((PAIR, ROWS), jnp.bfloat16),
                pltpu.VMEM(block, jnp.float32),
                pltpu.VMEM(block, jnp.float32),
            ],
        ),
        out_shape=[wide, wide, wide, jax.ShapeDtypeStruct((8, pairs * PAIR), jnp.float32)],
        compiler_params=pltpu.CompilerParams(vmem_limit_bytes=28 << 20),
        cost_estimate=light(),
        name="attend_back",
    )(rank, qkv, qkv, qkv, grads, key_info, query_info)


WIDE = 512
VMEM_BYTES = 56 << 20


def light(flops=1 << 20):
    return pl.CostEstimate(flops=flops, bytes_accessed=1 << 12, transcendentals=0)


def settings():
    return pltpu.CompilerParams(vmem_limit_bytes=VMEM_BYTES)


def whole(shape):
    return pl.BlockSpec(shape, lambda i: (0,) * len(shape))


def project_kernel(near_ref, far_ref, weight_ref, bias_ref, out_ref):
    rows = near_ref.shape[0]
    bias = bias_ref[...]
    out_ref[pl.ds(0, rows), :] = (nt_dot(near_ref[...], weight_ref[...]) + bias).astype(out_ref.dtype)
    out_ref[pl.ds(rows, rows), :] = (nt_dot(far_ref[...], weight_ref[...]) + bias).astype(out_ref.dtype)


def project(near, far, weight, bias):
    rows, depth = near.shape
    cols = weight.shape[0]
    return pl.pallas_call(
        project_kernel,
        grid=(cols // WIDE,),
        in_specs=[
            whole((rows, depth)),
            whole((rows, depth)),
            pl.BlockSpec((WIDE, depth), lambda i: (i, 0)),
            pl.BlockSpec((1, WIDE), lambda i: (0, i)),
        ],
        out_specs=pl.BlockSpec((2 * rows, WIDE), lambda i: (0, i)),
        out_shape=jax.ShapeDtypeStruct((2 * rows, cols), jnp.bfloat16),
        compiler_params=settings(),
        cost_estimate=light(),
        name="project",
    )(near, far, weight, bias)


def expand_kernel(near_ref, far_ref, weight_ref, bias_ref, hidden_ref, slope_ref):
    rows = near_ref.shape[0]
    bias = bias_ref[...]
    for part, ref in enumerate((near_ref, far_ref)):
        at = pl.ds(part * rows, rows)
        pre = nt_dot(ref[...], weight_ref[...]) + bias
        cube = 0.044715 * pre * pre
        bend = jnp.tanh((0.7978845608028654 * pre) * (1.0 + cube))
        half = 0.5 + 0.5 * bend
        inner = 0.7978845608028654 + (3.0 * 0.7978845608028654) * cube
        hidden_ref[at, :] = (pre * half).astype(jnp.bfloat16)
        slope_ref[at, :] = (half + (pre * half) * ((1.0 - bend) * inner)).astype(jnp.bfloat16)


def expand(near, far, weight, bias):
    rows, depth = near.shape
    cols = weight.shape[0]
    out = jax.ShapeDtypeStruct((2 * rows, cols), jnp.bfloat16)
    return pl.pallas_call(
        expand_kernel,
        grid=(cols // WIDE,),
        in_specs=[
            whole((rows, depth)),
            whole((rows, depth)),
            pl.BlockSpec((WIDE, depth), lambda i: (i, 0)),
            pl.BlockSpec((1, WIDE), lambda i: (0, i)),
        ],
        out_specs=[pl.BlockSpec((2 * rows, WIDE), lambda i: (0, i))] * 2,
        out_shape=[out, out],
        compiler_params=settings(),
        cost_estimate=light(),
        name="expand",
    )(near, far, weight, bias)


def expand_back_kernel(near_ref, far_ref, weight_ref, slope_ref, low_ref, sums_ref):
    rows = near_ref.shape[0]
    total = jnp.zeros((1, low_ref.shape[1]), jnp.float32)
    for part, ref in enumerate((near_ref, far_ref)):
        at = pl.ds(part * rows, rows)
        grad = nt_dot(ref[...], weight_ref[...]) * slope_ref[at, :].astype(jnp.float32)
        total = total + jnp.sum(grad, axis=0, keepdims=True)
        low_ref[at, :] = grad.astype(jnp.bfloat16)
    sums_ref[...] = jnp.broadcast_to(total, sums_ref.shape)


def expand_back(near, far, weight, slope):
    rows, depth = near.shape
    cols = weight.shape[0]
    return pl.pallas_call(
        expand_back_kernel,
        grid=(cols // WIDE,),
        in_specs=[
            whole((rows, depth)),
            whole((rows, depth)),
            pl.BlockSpec((WIDE, depth), lambda i: (i, 0)),
            pl.BlockSpec((2 * rows, WIDE), lambda i: (0, i)),
        ],
        out_specs=[pl.BlockSpec((2 * rows, WIDE), lambda i: (0, i)), pl.BlockSpec((8, WIDE), lambda i: (0, i))],
        out_shape=[
            jax.ShapeDtypeStruct((2 * rows, cols), jnp.bfloat16),
            jax.ShapeDtypeStruct((8, cols), jnp.float32),
        ],
        compiler_params=settings(),
        cost_estimate=light(),
        name="expand_back",
    )(near, far, weight, slope)


def partial_kernel(left_ref, weight_ref, near_ref, far_ref):
    rows = near_ref.shape[0]
    far_ref[...] = nn_dot(left_ref[pl.ds(rows, rows), :], weight_ref[...]).astype(far_ref.dtype)
    near_ref[...] = nn_dot(left_ref[pl.ds(0, rows), :], weight_ref[...])


def partial_sums(left, weight):
    rows, depth = left.shape
    cols = weight.shape[1]
    half = rows // 2
    return pl.pallas_call(
        partial_kernel,
        grid=(cols // WIDE,),
        in_specs=[whole((rows, depth)), pl.BlockSpec((depth, WIDE), lambda i: (0, i))],
        out_specs=[pl.BlockSpec((half, WIDE), lambda i: (0, i))] * 2,
        out_shape=[
            jax.ShapeDtypeStruct((half, cols), jnp.float32),
            jax.ShapeDtypeStruct((half, cols), jnp.bfloat16),
        ],
        compiler_params=settings(),
        cost_estimate=light(),
        name="partial_sums",
    )(left, weight)


def tn_dot(left, right):
    return lax.dot_general(left, right, (((0,), (0,)), ((), ())), preferred_element_type=jnp.float32)


def cross_kernel(left_a, near_a, far_a, left_b, near_b, far_b, out_ref):
    rows = near_a.shape[0]
    top, low = pl.ds(0, rows), pl.ds(rows, rows)
    total = tn_dot(left_a[top, :], near_a[...]) + tn_dot(left_a[low, :], far_a[...])
    total = total + tn_dot(left_b[top, :], near_b[...]) + tn_dot(left_b[low, :], far_b[...])
    out_ref[...] = total.astype(out_ref.dtype)


def cross_sums(left_a, right_a, left_b, right_b, start, size):
    rows = left_a.shape[0]
    cols = right_a[0].shape[1]
    tall = 256
    first = start // tall
    left_spec = pl.BlockSpec((rows, tall), lambda i: (0, first + i))
    right_spec = whole((rows // 2, cols))
    return pl.pallas_call(
        cross_kernel,
        grid=(size // tall,),
        in_specs=[left_spec, right_spec, right_spec] * 2,
        out_specs=pl.BlockSpec((tall, cols), lambda i: (i, 0)),
        out_shape=jax.ShapeDtypeStruct((size, cols), jnp.bfloat16),
        compiler_params=settings(),
        cost_estimate=light(),
        name="cross_sums",
    )(left_a, *right_a, left_b, *right_b)


def flip_kernel(first_ref, weight_ref, out_ref):
    out_ref[...] = weight_ref[...].T


def flipped(weight, first, count):
    depth = weight.shape[0]
    return pl.pallas_call(
        flip_kernel,
        grid_spec=pltpu.PrefetchScalarGridSpec(
            num_scalar_prefetch=1,
            grid=(count,),
            in_specs=[pl.BlockSpec((depth, 128), lambda i, first: (0, first[0] + i))],
            out_specs=pl.BlockSpec((128, depth), lambda i, first: (i, 0)),
        ),
        out_shape=jax.ShapeDtypeStruct((count * 128, depth), weight.dtype),
        compiler_params=settings(),
        cost_estimate=light(),
        name="flipped",
    )(first.reshape(1).astype(jnp.int32), weight)


def attn_pack_kernel(
    place_ref, query_ref, key_ref, value_ref, out_w_ref, bias_mine, bias_other, mine_ref, other_ref
):
    half = place_ref[1]
    mine_ref[pl.ds(4 * HEAD_DIM, 8), :] = bias_mine[...]
    other_ref[pl.ds(4 * HEAD_DIM, 8), :] = bias_other[...]
    for which, ref in enumerate((mine_ref, other_ref)):
        rows = pl.ds(pl.multiple_of(jnp.where(which == 0, half, 1 - half) * HEAD_DIM, HEAD_DIM), HEAD_DIM)
        ref[pl.ds(3 * HEAD_DIM, HEAD_DIM), :] = out_w_ref[rows, :]
    for index, source in enumerate((query_ref, key_ref, value_ref)):
        flat = source[...].T
        low, high = flat[:HEAD_DIM, :], flat[HEAD_DIM:, :]
        at = pl.ds(index * HEAD_DIM, HEAD_DIM)
        mine_ref[at, :] = jnp.where(half == 0, low, high)
        other_ref[at, :] = jnp.where(half == 0, high, low)


def attn_pack(query_weight, key_weight, value_weight, out_weight, bias_mine, bias_other, team, half):
    depth = query_weight.shape[0]
    out = jax.ShapeDtypeStruct((4 * HEAD_DIM + 8, depth), query_weight.dtype)
    column = pl.BlockSpec((depth, 128), lambda i, place: (0, place[0]))
    full = pl.BlockSpec((4 * HEAD_DIM + 8, depth), lambda i, place: (0, 0))
    bias = pl.BlockSpec((8, depth), lambda i, place: (0, 0))
    return pl.pallas_call(
        attn_pack_kernel,
        grid_spec=pltpu.PrefetchScalarGridSpec(
            num_scalar_prefetch=1,
            grid=(1,),
            in_specs=[column, column, column, pl.BlockSpec((128, depth), lambda i, place: (place[0], 0)), bias, bias],
            out_specs=[full, full],
        ),
        out_shape=[out, out],
        compiler_params=settings(),
        cost_estimate=light(),
        name="attn_pack",
    )(jnp.stack([team, half]).astype(jnp.int32), query_weight, key_weight, value_weight, out_weight, bias_mine, bias_other)


def pick_kernel(index_ref, rows_ref, out_ref):
    wanted = index_ref[...]
    place = lax.broadcasted_iota(jnp.int32, (wanted.shape[0], rows_ref.shape[0]), 1)
    hot = jnp.where(place == wanted, 1.0, 0.0).astype(jnp.bfloat16)
    out_ref[...] = nn_dot(hot, rows_ref[...]).astype(out_ref.dtype)


def pick_rows(index, rows, tall):
    count = index.shape[0]
    cols = rows.shape[1]
    return pl.pallas_call(
        pick_kernel,
        grid=(count // tall,),
        in_specs=[pl.BlockSpec((tall, 1), lambda i: (i, 0)), whole(rows.shape)],
        out_specs=pl.BlockSpec((tall, cols), lambda i: (i, 0)),
        out_shape=jax.ShapeDtypeStruct((count, cols), rows.dtype),
        compiler_params=settings(),
        cost_estimate=light(),
        name="pick_rows",
    )(index[:, None], rows)


def drop_kernel(index_ref, rows_ref, out_ref):
    wanted = index_ref[...]
    tall = out_ref.shape[0]
    place = lax.broadcasted_iota(jnp.int32, (tall, rows_ref.shape[0]), 0) + pl.program_id(0) * tall
    hot = jnp.where(place == wanted, 1.0, 0.0).astype(jnp.bfloat16)
    out_ref[...] = nn_dot(hot, rows_ref[...]).astype(out_ref.dtype)


def drop_rows(index, rows, count, tall):
    cols = rows.shape[1]
    return pl.pallas_call(
        drop_kernel,
        grid=(count // tall,),
        in_specs=[whole((1, index.shape[0])), whole(rows.shape)],
        out_specs=pl.BlockSpec((tall, cols), lambda i: (i, 0)),
        out_shape=jax.ShapeDtypeStruct((count, cols), rows.dtype),
        compiler_params=settings(),
        cost_estimate=light(),
        name="drop_rows",
    )(index[None, :], rows)


def settle_kernel(index_ref, boxes_ref, out_ref):
    wanted = index_ref[...]
    place = lax.broadcasted_iota(jnp.int32, (out_ref.shape[0], boxes_ref.shape[1]), 0)
    hot = jnp.where(place == wanted, 1.0, 0.0).astype(jnp.bfloat16)
    out_ref[...] = nn_dot(hot, boxes_ref[0]).astype(out_ref.dtype)


def settle_rows(index, boxes, count):
    depth, slots, cols = boxes.shape
    return pl.pallas_call(
        settle_kernel,
        grid=(depth,),
        in_specs=[whole((1, slots)), pl.BlockSpec((1, slots, cols), lambda i: (i, 0, 0))],
        out_specs=pl.BlockSpec((count, cols), lambda i: (0, i)),
        out_shape=jax.ShapeDtypeStruct((count, depth * cols), boxes.dtype),
        compiler_params=settings(),
        cost_estimate=light(),
        name="settle_rows",
    )(index[None, :], boxes)


def unsettle_kernel(index_ref, rows_ref, out_ref):
    wanted = index_ref[...]
    place = lax.broadcasted_iota(jnp.int32, (wanted.shape[0], rows_ref.shape[0]), 1)
    hot = jnp.where(place == wanted, 1.0, 0.0).astype(jnp.bfloat16)
    out_ref[0] = nn_dot(hot, rows_ref[...]).astype(out_ref.dtype)


def unsettle_rows(index, rows, depth):
    slots = index.shape[0]
    count = rows.shape[0]
    cols = rows.shape[1] // depth
    return pl.pallas_call(
        unsettle_kernel,
        grid=(depth,),
        in_specs=[whole((slots, 1)), pl.BlockSpec((count, cols), lambda i: (0, i))],
        out_specs=pl.BlockSpec((1, slots, cols), lambda i: (i, 0, 0)),
        out_shape=jax.ShapeDtypeStruct((depth, slots, cols), rows.dtype),
        compiler_params=settings(),
        cost_estimate=light(),
        name="unsettle_rows",
    )(index[:, None], rows)


def code_of(place, own):
    return jnp.bitwise_xor(place, own)


def piece_of(code):
    return ((code >> 2) & 1) + 2 * (code & 1)


def stack_kernel(own_ref, near_ref, far_ref, out_ref):
    code = code_of(pl.program_id(0), own_ref[0])
    block = jnp.where((code & 2) == 0, near_ref[...], far_ref[...])
    out_ref[...] = block.astype(out_ref.dtype)


def stack_kernel_t(own_ref, near_ref, far_ref, out_ref):
    code = code_of(pl.program_id(0), own_ref[0])
    block = jnp.where((code & 2) == 0, near_ref[...], far_ref[...])
    out_ref[...] = block.T.astype(out_ref.dtype)


def stack_pieces(near, far, own, transposed):
    tall = near.shape[0] // 4
    cols = near.shape[1]
    spec = pl.BlockSpec((tall, cols), lambda i, own: (piece_of(code_of(i, own[0])), 0))
    return pl.pallas_call(
        stack_kernel_t if transposed else stack_kernel,
        grid_spec=pltpu.PrefetchScalarGridSpec(
            num_scalar_prefetch=1,
            grid=(8,),
            in_specs=[spec, spec],
            out_specs=pl.BlockSpec((cols, tall), lambda i, own: (0, i))
            if transposed
            else pl.BlockSpec((tall, cols), lambda i, own: (i, 0)),
        ),
        out_shape=jax.ShapeDtypeStruct((cols, 8 * tall) if transposed else (8 * tall, cols), jnp.float32),
        compiler_params=settings(),
        cost_estimate=light(),
        name="stack_pieces",
    )(own, near, far)


def stack_heads_kernel(flips, own_ref, near_low, far_low, near_high, far_high, *outs):
    code = code_of(2 * pl.program_id(0), own_ref[0])
    take_near = (code & 2) == 0
    low = jnp.where(take_near, near_low[...], far_low[...])
    high = jnp.where(take_near, near_high[...], far_high[...])
    for index, ref in enumerate(outs):
        at = slice(index * HEAD_DIM, (index + 1) * HEAD_DIM)
        both = jnp.concatenate([low[at], high[at]], axis=0)
        ref[...] = (both.T if flips[index] else both).astype(ref.dtype)


def stack_heads(near, far, own, flips):
    tall = near.shape[0] // 4
    cols = near.shape[1]
    low = pl.BlockSpec((tall, cols), lambda i, own: (piece_of(code_of(2 * i, own[0])), 0))
    high = pl.BlockSpec((tall, cols), lambda i, own: (piece_of(code_of(2 * i + 1, own[0])), 0))
    column = pl.BlockSpec((cols, 128), lambda i, own: (0, i))
    row = pl.BlockSpec((128, cols), lambda i, own: (i, 0))
    tall_out = jax.ShapeDtypeStruct((cols, 512), jnp.float32)
    flat_out = jax.ShapeDtypeStruct((512, cols), jnp.float32)
    return pl.pallas_call(
        functools.partial(stack_heads_kernel, flips),
        grid_spec=pltpu.PrefetchScalarGridSpec(
            num_scalar_prefetch=1,
            grid=(4,),
            in_specs=[low, low, high, high],
            out_specs=[column if flip else row for flip in flips],
        ),
        out_shape=[tall_out if flip else flat_out for flip in flips],
        compiler_params=settings(),
        cost_estimate=light(),
        name="stack_heads",
    )(own, near, far, near, far)


def add_rows_kernel(*refs):
    total = refs[0][...].astype(jnp.float32)
    for ref in refs[1:-1]:
        total = total + ref[...].astype(jnp.float32)
    refs[-1][...] = total.astype(refs[-1].dtype)


def add_pieces(near, got, moved, index):
    tall = near.shape[0] // 4
    cols = near.shape[1]
    at = pl.BlockSpec((tall, cols), lambda i: (index, 0))
    return pl.pallas_call(
        add_rows_kernel,
        grid=(1,),
        in_specs=[at, at] + [whole((tall, cols))] * len(moved),
        out_specs=whole((tall, cols)),
        out_shape=jax.ShapeDtypeStruct((tall, cols), near.dtype),
        compiler_params=settings(),
        cost_estimate=light(),
        name="add_pieces",
    )(near, got, *moved)


def add_rows(near, got, index):
    return add_pieces(near, got, (), index)


def add_three(near, got, moved, index):
    return add_pieces(near, got, (moved,), index)


def add_four(near, got, first, second, index):
    return add_pieces(near, got, (first, second), index)


def partial_three_kernel(query_ref, key_ref, value_ref, weight_ref, near_ref, far_ref):
    rows = near_ref.shape[0]
    depth = query_ref.shape[1]
    for at, out in ((pl.ds(rows, rows), far_ref), (pl.ds(0, rows), near_ref)):
        total = nn_dot(query_ref[at, :], weight_ref[pl.ds(0, depth), :])
        total = total + nn_dot(key_ref[at, :], weight_ref[pl.ds(depth, depth), :])
        total = total + nn_dot(value_ref[at, :], weight_ref[pl.ds(2 * depth, depth), :])
        out[...] = total.astype(out.dtype)


def partial_three(query, key, value, weight):
    rows, depth = query.shape
    cols = weight.shape[1]
    half = rows // 2
    return pl.pallas_call(
        partial_three_kernel,
        grid=(cols // WIDE,),
        in_specs=[whole((rows, depth))] * 3 + [pl.BlockSpec((3 * depth, WIDE), lambda i: (0, i))],
        out_specs=[pl.BlockSpec((half, WIDE), lambda i: (0, i))] * 2,
        out_shape=[
            jax.ShapeDtypeStruct((half, cols), jnp.float32),
            jax.ShapeDtypeStruct((half, cols), jnp.bfloat16),
        ],
        compiler_params=settings(),
        cost_estimate=light(),
        name="partial_three",
    )(query, key, value, weight)


SWAP = [(0, 1), (1, 0)]
PLANE = ("y", "x", "core")
EVERY = ("z", "y", "x", "core")
MICRO = 2
SLOTS = 72


def after(value, *others):
    return lax.optimization_barrier((value, *others))[0]


class Order:

    def __init__(self):
        self.last = ()

    def take(self, value):
        return lax.optimization_barrier((value, self.last))[0]

    def mark(self, value):
        self.last = value
        return value

    def step(self, value):
        return self.mark(self.take(value))


def swap_along(array, axis):
    return lax.ppermute(array, axis, SWAP)


def shift(array, step):
    size = lax.axis_size("z")
    return lax.ppermute(array, "z", [(i, (i + step) % size) for i in range(size)])


def joined(arrays):
    return jnp.concatenate(arrays, axis=0)


def plane_start(piece):
    return (piece, swap_along(piece, "x"), swap_along(piece, "y"))


def plane_middle(started, order):
    piece, by_x, by_y = started
    half = piece.shape[0] // 2
    by_x, by_y = order.step((by_x, by_y))
    return (piece, by_x, by_y, swap_along(by_y[:half], "x"), swap_along(by_x[half:], "y"))


def plane_end(started, order):
    piece, by_x, by_y, corner_top, corner_low = started
    near = order.mark(joined([piece, by_x, by_y, *order.take((corner_top, corner_low))]))
    return (near, swap_along(near, "core"))


def total_all(vector):
    for axis in ("core", "x", "y"):
        vector = vector + swap_along(vector, axis)
    size = lax.axis_size("z")
    for step in (1, 2):
        vector = vector + lax.ppermute(vector, "z", [(i, i ^ step) for i in range(size)])
    return vector


def held_before(bound, residue, parts):
    return (bound + (parts - 1) - residue) // parts


def piece_tables(lengths, starts, quarter_low, quarter_rows, residue, parts):
    ends = running_sum(lengths)
    firsts = ends - lengths
    shift = starts - firsts
    low = jnp.maximum(firsts, quarter_low)
    high = jnp.minimum(ends, quarter_low + quarter_rows)
    begin = held_before(low + shift, residue, parts)
    count = jnp.where(high > low, held_before(high + shift, residue, parts) - begin, 0)
    return (begin, count, shift)


def slot_lookup(begin, count, value_of):
    base = running_sum(count) - count
    slot = jnp.arange(SLOTS, dtype=jnp.int32)
    inside = (slot >= base[..., None]) & (slot < (base + count)[..., None])
    held = begin[..., None] + slot - base[..., None]
    return jnp.sum(jnp.where(inside, value_of(held) + 1, 0), axis=-2, dtype=jnp.int32) - 1


def layer(
    tokens,
    cotangent,
    lengths,
    dealing,
    query_weight,
    key_weight,
    value_weight,
    out_weight,
    query_bias,
    value_bias,
    out_bias,
    up_weight,
    up_bias,
    down_weight,
    down_bias,
    attn_gain,
    attn_shift,
    mlp_gain,
    mlp_shift,
):
    tok_rows = tokens.shape[1]
    col_width = tokens.shape[2]
    width = out_weight.shape[1]
    seq_dev = lengths.shape[2]
    depth = lax.axis_size("z")
    parts = lax.axis_size("y") * 4
    own_rows = tok_rows // 4
    y, x, core, z = (lax.axis_index(name) for name in ("y", "x", "core", "z"))
    team = 2 * x + core
    eighth = 2 * team + y
    residue = 4 * y + team
    group = 2 * z + y

    given_off = []
    for micro_step in range(MICRO):
        given_off.append(given_layout(lengths[micro_step], dealing[micro_step])[2])
    starts = jnp.stack(given_off).reshape(lengths.shape)
    quarter_low = (jnp.arange(4, dtype=jnp.int32) * own_rows)[None, None, :, None]
    begin, count, _ = piece_tables(
        lengths[:, :, None, :], starts[:, :, None, :], quarter_low, own_rows, residue, parts
    )
    micro_ids = jnp.arange(MICRO, dtype=jnp.int32)[:, None, None, None]
    begin = jnp.transpose(begin + micro_ids * tok_rows, (1, 2, 0, 3)).reshape(-1, MICRO * seq_dev)
    count = jnp.transpose(count, (1, 2, 0, 3)).reshape(-1, MICRO * seq_dev)
    send_row = slot_lookup(begin, count, lambda held: held).reshape(-1)

    my_lengths = lax.dynamic_index_in_dim(lengths, group, 1, keepdims=False)
    my_starts = lax.dynamic_index_in_dim(starts, group, 1, keepdims=False)
    residues = jnp.arange(parts, dtype=jnp.int32)[:, None, None]
    my_begin, my_count, my_shift = piece_tables(
        my_lengths[None], my_starts[None], team * own_rows, own_rows, residues, parts
    )
    flat = (parts, MICRO * seq_dev)
    row_shift = (
        my_shift + team * own_rows - jnp.arange(MICRO, dtype=jnp.int32)[None, :, None] * own_rows
    )
    row_shift = jnp.broadcast_to(row_shift, my_count.shape).reshape(flat)
    own_row = slot_lookup(
        my_begin.reshape(flat),
        my_count.reshape(flat),
        lambda held: held * parts + residues - row_shift[..., None],
    ).reshape(-1)
    head_rows = HEAD_DIM
    half_units = up_weight.shape[1] // 8

    shard_heads = query_weight.shape[1]

    def bias_rows(half):
        row = jnp.concatenate(
            [
                lax.dynamic_slice_in_dim(bias, (2 * team + half) * size, size)
                for bias, size in ((query_bias, HEAD_DIM), (value_bias, HEAD_DIM), (up_bias, half_units))
            ]
        )
        return jnp.pad(row[None, :], ((0, 7), (0, width - row.shape[0])))

    attn_mine, attn_other = attn_pack(
        query_weight, key_weight, value_weight, out_weight, bias_rows(y), bias_rows(1 - y), team, y
    )
    blocks = half_units // 128
    up_mine = flipped(up_weight, (2 * team + y) * blocks, blocks)
    up_other = flipped(up_weight, (2 * team + 1 - y) * blocks, blocks)
    down_mine = lax.dynamic_slice_in_dim(down_weight, (2 * team + y) * half_units, half_units, 0)
    down_other = lax.dynamic_slice_in_dim(down_weight, (2 * team + 1 - y) * half_units, half_units, 0)

    order = Order()

    def spread_out(array):
        spread = array.reshape(MICRO, tok_rows // parts, parts, col_width)
        spread = lax.all_to_all(spread, PLANE, split_axis=2, concat_axis=1, tiled=True)
        return spread.reshape(MICRO * tok_rows, col_width)

    def box_exchange(sent):
        return lax.all_to_all(sent, EVERY, split_axis=0, concat_axis=0, tiled=True)

    def boxes(spread):
        return pick_rows(send_row, spread, 384)

    def settle(got):
        return settle_rows(own_row, got.reshape(depth, parts * SLOTS, col_width), MICRO * own_rows)

    gain_one, shift_one, gain_two, shift_two, out_b, down_b = (
        array.astype(jnp.float32)
        for array in (attn_gain, attn_shift, mlp_gain, mlp_shift, out_bias, down_bias)
    )

    rank = jnp.full((1,), team, jnp.int32)
    infos = []
    for micro_step in range(MICRO):
        holder, position, _ = buffer_layout(my_lengths[micro_step], my_starts[micro_step], tok_rows)
        segment = holder * tok_rows + position // (SEG + SUMM)
        summary = jnp.where(position % (SEG + SUMM) >= SEG, holder, -1)
        infos.append((jnp.stack([segment, summary], axis=1), jnp.stack([segment, holder], axis=0)))

    def up_down(piece):
        piece = order.take(piece)
        return (shift(piece, 1), shift(piece, -1))

    def onward(piece):
        piece = order.step(piece)
        return (piece, shift(piece, 1), swap_along(piece, "y"))

    def swapped(piece):
        piece = order.step(piece)
        return (piece, swap_along(piece, "y"))

    def team_start(rows):
        return (rows, swap_along(rows, "x"))

    def team_middle(started):
        own, by_x = started
        near = order.mark(joined([own, order.take(by_x)]))
        return (near, swap_along(near, "core"))

    def team_end(started):
        near, far = started
        return (near, order.step(far))

    def sum_start(left, weight):
        near, far = order.mark(partial_sums(order.take(left), weight))
        return (near, swap_along(far, "core"))

    def sum_middle(started):
        kept, got = started
        quarter = kept.shape[0] // 2
        kept = kept + order.take(got).astype(jnp.float32)
        moving = order.mark(kept[quarter:].astype(jnp.bfloat16))
        return (kept[:quarter], swap_along(moving, "x"))

    def sum_end(started):
        kept, got = started
        return kept + order.take(got).astype(jnp.float32)

    def unsettle(array):
        return unsettle_rows(own_row, array, depth).reshape(-1, col_width)

    def unbox(got):
        return drop_rows(send_row, got, MICRO * tok_rows, 256)

    def spread_back(held):
        held = held.reshape(MICRO, tok_rows, 1, col_width)
        back = lax.all_to_all(held, PLANE, split_axis=1, concat_axis=2, tiled=True)
        return back.reshape(MICRO, tok_rows, col_width)

    order.mark(attn_mine)
    attn_1, attn_3 = up_down(attn_mine)
    tok_spread = spread_out(tokens)
    tok_sent = order.mark(boxes(order.take(tok_spread)))
    tok_got = box_exchange(tok_sent)
    attn_1, attn_2, attn_y1 = onward(attn_1)
    attn_3, attn_y3 = swapped(attn_3)
    attn_2, attn_y2 = swapped(attn_2)
    tok = order.mark(settle(order.take(tok_got)))
    up_1, up_3 = up_down(up_mine)
    cot_spread = spread_out(after(cotangent, tok))

    def normed_rows(rows, gain, shift_by):
        normed, inverse = normalize(rows)
        return (normed, inverse, order.mark((normed * gain + shift_by).astype(jnp.bfloat16)))

    rows_a = tok[:own_rows].astype(jnp.float32)
    rows_b = tok[own_rows:].astype(jnp.float32)
    normed_one_a, inverse_one_a, first_a = normed_rows(order.take(rows_a), gain_one, shift_one)
    first_a = team_start(first_a)
    normed_one_b, inverse_one_b, first_b = normed_rows(order.take(rows_b), gain_one, shift_one)
    first_b = team_start(first_b)
    attn_all = [attn_mine, attn_1, attn_2, attn_3, attn_other, *order.take((attn_y1, attn_y2, attn_y3))]
    qkv_w = joined([piece[k * head_rows : (k + 1) * head_rows] for k in range(3) for piece in attn_all])
    out_w = joined([piece[3 * head_rows : 4 * head_rows] for piece in attn_all])
    order.mark((qkv_w, out_w))
    bias_all = [piece[4 * head_rows].astype(jnp.float32) for piece in attn_all]
    query_b = joined([bias[:head_rows] for bias in bias_all])
    value_b = joined([bias[head_rows : 2 * head_rows] for bias in bias_all])
    up_b = joined([bias[2 * head_rows : 2 * head_rows + half_units] for bias in bias_all])[None, :]
    qkv_b = joined([query_b, jnp.zeros_like(query_b), value_b])[None, :]
    no_b = jnp.zeros((1, out_w.shape[0]), jnp.float32)

    first_a = team_end(team_middle(first_a))
    qkv_a = order.mark(project(*order.take(first_a), qkv_w, qkv_b))
    up_1, up_2, up_y1 = onward(up_1)
    mixed_a = order.mark(attend(order.take(qkv_a), rank, *infos[0]))
    first_b = team_middle(first_b)
    sum_a1 = sum_start(mixed_a, out_w)
    first_b = team_end(first_b)
    qkv_b_ = order.mark(project(*order.take(first_b), qkv_w, qkv_b))
    sum_a1 = sum_middle(sum_a1)
    up_3, up_y3 = swapped(up_3)
    down_1, down_3 = up_down(down_mine)
    mixed_b = order.mark(attend(order.take(qkv_b_), rank, *infos[1]))
    up_2, up_y2 = swapped(up_2)
    sum_b1 = sum_start(mixed_b, out_w)
    resid_a = rows_a + sum_end(sum_a1) + out_b
    normed_two_a, inverse_two_a, second_a = normed_rows(
        resid_a.astype(jnp.bfloat16).astype(jnp.float32), gain_two, shift_two
    )
    second_a = team_start(second_a)
    sum_b1 = sum_middle(sum_b1)
    cot_sent = order.mark(boxes(order.take(cot_spread)))
    down_1, down_2, down_y1 = onward(down_1)
    up_w = order.mark(joined([up_mine, up_1, up_2, up_3, up_other, *order.take((up_y1, up_y2, up_y3))]))
    second_a = team_end(team_middle(second_a))
    down_3, down_y3 = swapped(down_3)
    cot_got = box_exchange(order.take(cot_sent))

    hidden_a, slope_a = order.mark(expand(*order.take(second_a), up_w, up_b))
    resid_b = rows_b + sum_end(sum_b1) + out_b
    normed_two_b, inverse_two_b, second_b = normed_rows(
        resid_b.astype(jnp.bfloat16).astype(jnp.float32), gain_two, shift_two
    )
    second_b = team_start(second_b)
    down_2, down_y2 = swapped(down_2)
    second_b = team_middle(second_b)
    cot = order.mark(settle(order.take(cot_got)))
    cot_own = cot.reshape(MICRO, own_rows, width)
    second_b = team_end(second_b)
    cot_parts = [team_start(cot_own[m]) for m in range(MICRO)]
    hidden_b, slope_b = order.mark(expand(*order.take(second_b), up_w, up_b))
    down_w = order.mark(
        joined([down_mine, down_1, down_2, down_3, down_other, *order.take((down_y1, down_y2, down_y3))])
    )
    sum_a4 = sum_start(hidden_a, down_w)
    cot_parts[0] = team_middle(cot_parts[0])
    sum_b4 = sum_start(hidden_b, down_w)
    cot_parts[1] = team_middle(cot_parts[1])
    cot_a = team_end(cot_parts[0])
    cot_own_a, cot_own_b = cot_own[0].astype(jnp.float32), cot_own[1].astype(jnp.float32)

    low_a, up_sum_a = order.mark(expand_back(*order.take(cot_a), down_w, slope_a))
    cot_b = team_end(cot_parts[1])
    sum_a2 = sum_start(low_a, up_w)
    sum_a4 = sum_middle(sum_a4)
    low_b, up_sum_b = order.mark(expand_back(*order.take(cot_b), down_w, slope_b))
    up_sum_a, up_sum_b = up_sum_a[0], up_sum_b[0]
    sum_a2 = sum_middle(sum_a2)
    sum_b2 = sum_start(low_b, up_w)
    sum_b4 = sum_middle(sum_b4)

    def cross_half(left_a, right_a, left_b, right_b, half):
        size = left_a.shape[1] // 2
        return order.mark(cross_sums(order.take(left_a), right_a, left_b, right_b, half * size, size))

    down_far = cross_half(hidden_a, cot_a, hidden_b, cot_b, 1)
    down_swap = swap_along(down_far, "y")
    sum_b2 = sum_middle(sum_b2)

    def second_back(started, normed_two, inverse_two, cot_rows):
        grad = sum_end(started).astype(jnp.bfloat16).astype(jnp.float32)
        back, gain_part, shift_part = norm_backward(grad, normed_two, inverse_two, gain_two)
        resid_grad = cot_rows + back
        low = order.mark(resid_grad.astype(jnp.bfloat16))
        return (resid_grad, low, gain_part, shift_part)

    resid_grad_a, attn_low_a, gain_two_a, shift_two_a = second_back(
        sum_a2, normed_two_a, inverse_two_a, cot_own_a
    )
    attn_low_a = team_start(attn_low_a)
    down_near = cross_half(hidden_a, cot_a, hidden_b, cot_b, 0)
    layer_a = (resid_a + sum_end(sum_a4) + down_b).astype(jnp.bfloat16)
    layer_b = (resid_b + sum_end(sum_b4) + down_b).astype(jnp.bfloat16)
    layer_sent = order.mark(unsettle(order.take(joined([layer_a, layer_b]))))
    layer_got = box_exchange(layer_sent)
    up_far = cross_half(low_a, second_a, low_b, second_b, 1)
    up_swap = swap_along(up_far, "y")
    resid_grad_b, attn_low_b, gain_two_b, shift_two_b = second_back(
        sum_b2, normed_two_b, inverse_two_b, cot_own_b
    )
    attn_low_b = team_start(attn_low_b)
    attn_low_a = team_end(team_middle(attn_low_a))

    def attn_back(attn_low, qkv, m):
        mixed_grad = order.mark(project(*order.take(attn_low), out_w, no_b))
        return order.mark(attend_back(qkv, order.take(mixed_grad), rank, *infos[m]))

    def sum_start_three(lefts, weight):
        near, far = order.mark(partial_three(*order.take(lefts), weight))
        return (near, swap_along(far, "core"))

    *lows_a, sums_a = attn_back(attn_low_a, qkv_a, 0)
    attn_low_b = team_middle(attn_low_b)
    sum_a3 = sum_start_three(lows_a, qkv_w)
    attn_low_b = team_end(attn_low_b)
    up_near = cross_half(low_a, second_a, low_b, second_b, 0)
    layer_held = order.mark(unbox(order.take(layer_got)))
    layer_out = spread_back(layer_held)

    def ring_start(near, got):
        piece = near.shape[0] // depth
        got = order.take(got)
        far_2 = order.mark(add_rows(near, got, 2))
        move = shift(far_2, 1)
        far_1 = order.mark(add_rows(near, order.take(got), 1))
        back = shift(far_1, -1)
        return (near, got, move, back)

    def ring_middle(started):
        near, got, move, back = started
        far_3 = order.mark(add_three(near, got, order.take(move), 3))
        return (near, got, shift(far_3, 1), back)

    def ring_end(started):
        near, got, move, back = started
        move, back = order.take((move, back))
        return order.mark(add_four(near, got, move, back, 0))

    sum_a3 = sum_middle(sum_a3)
    down_ring = ring_start(down_near, down_swap)
    *lows_b, sums_b = attn_back(attn_low_b, qkv_b_, 1)
    down_ring = ring_middle(down_ring)
    sum_b3 = sum_start_three(lows_b, qkv_w)

    def first_back(started, normed_one, inverse_one, resid_grad):
        grad = sum_end(started).astype(jnp.bfloat16).astype(jnp.float32)
        back, gain_part, shift_part = norm_backward(grad, normed_one, inverse_one, gain_one)
        return (order.mark((resid_grad + back).astype(jnp.bfloat16)), gain_part, shift_part)

    def by_piece(arrays):
        rows = head_rows
        return order.mark(joined([a[k * rows : (k + 1) * rows] for k in range(depth) for a in arrays]))

    def cross_heads(index, half):
        left_a, right_a, left_b, right_b = (
            (lows_a[index], first_a, lows_b[index], first_b)
            if index < 3
            else (mixed_a, attn_low_a, mixed_b, attn_low_b)
        )
        return cross_half(left_a, right_a, left_b, right_b, half)

    one_far = by_piece([cross_heads(0, 1), cross_heads(1, 1)])
    one_swap = swap_along(one_far, "y")
    sum_b3 = sum_middle(sum_b3)
    input_a, gain_one_a, shift_one_a = first_back(sum_a3, normed_one_a, inverse_one_a, resid_grad_a)
    two_far = by_piece([cross_heads(2, 1), cross_heads(3, 1)])
    two_swap = swap_along(two_far, "y")
    down_total = ring_end(down_ring)
    up_ring = ring_start(up_near, up_swap)
    one_near = by_piece([cross_heads(0, 0), cross_heads(1, 0)])
    input_b, gain_one_b, shift_one_b = first_back(sum_b3, normed_one_b, inverse_one_b, resid_grad_b)
    input_sent = order.mark(unsettle(order.take(joined([input_a, input_b]))))
    input_got = box_exchange(input_sent)
    two_near = by_piece([cross_heads(2, 0), cross_heads(3, 0)])
    up_ring = ring_middle(up_ring)
    one_ring = ring_start(one_near, one_swap)
    down_plane = plane_start(down_total)
    up_total = ring_end(up_ring)
    down_plane = plane_middle(down_plane, order)
    one_ring = ring_middle(one_ring)
    up_plane = plane_start(up_total)
    own = jnp.full((1,), eighth, jnp.int32)
    two_ring = ring_start(two_near, two_swap)
    down_plane = plane_end(down_plane, order)
    down_grad = order.mark(stack_pieces(*order.take(down_plane), own, False))
    one_total = ring_end(one_ring)
    one_plane = plane_start(one_total)
    input_held = order.mark(unbox(order.take(input_got)))
    input_grad = spread_back(input_held)
    two_ring = ring_middle(two_ring)
    up_plane = plane_middle(up_plane, order)
    up_plane = plane_end(up_plane, order)
    one_plane = plane_middle(one_plane, order)
    up_grad = order.mark(stack_pieces(*order.take(up_plane), own, True))
    two_total = ring_end(two_ring)
    two_plane = plane_start(two_total)
    one_plane = plane_end(one_plane, order)
    two_plane = plane_middle(two_plane, order)
    query_grad, key_grad = order.mark(stack_heads(*order.take(one_plane), own, (True, True)))
    two_plane = plane_end(two_plane, order)
    value_grad, out_w_grad = order.mark(stack_heads(*order.take(two_plane), own, (True, False)))
    kept = []
    for sums, up_sum, resid_grad, cot_rows, norms in (
        (sums_a, up_sum_a, resid_grad_a, cot_own_a, (gain_one_a, shift_one_a, gain_two_a, shift_two_a)),
        (sums_b, up_sum_b, resid_grad_b, cot_own_b, (gain_one_b, shift_one_b, gain_two_b, shift_two_b)),
    ):
        kept.append(
            dict(
                query_b=sums[0],
                value_b=sums[1],
                up_b=up_sum,
                vectors=(jnp.sum(resid_grad, axis=0), jnp.sum(cot_rows, axis=0)) + norms,
            )
        )

    def place(vector, shard_size, size):
        whole = jnp.zeros((depth * shard_size,), jnp.float32)
        for index in range(2 * depth):
            half = y if index < depth else 1 - y
            owner = lax.rem(z - index % depth + depth, depth)
            whole = lax.dynamic_update_slice(
                whole,
                vector[index * size : (index + 1) * size],
                (owner * shard_size + (2 * team + half) * size,),
            )
        return whole

    small = [kept[0][name] + kept[1][name] for name in ("query_b", "value_b", "up_b")]
    vectors = [
        place(small[0], shard_heads, HEAD_DIM),
        place(small[1], shard_heads, HEAD_DIM),
        place(small[2], up_weight.shape[1], half_units),
    ] + [kept[0]["vectors"][k] + kept[1]["vectors"][k] for k in range(6)]
    sizes = [vector.shape[0] for vector in vectors]
    packed = total_all(jnp.concatenate(vectors).reshape(-1, 128)).reshape(-1)
    pieces = []
    offset = 0
    for size in sizes:
        pieces.append(packed[offset : offset + size])
        offset += size
    query_b_grad, value_b_grad, up_b_grad, out_b_grad, down_b_grad, *norm_grads = pieces

    def own_shard(vector):
        size = vector.shape[0] // depth
        return lax.dynamic_slice_in_dim(vector, z * size, size)

    return (
        layer_out,
        input_grad,
        query_grad,
        key_grad,
        value_grad,
        out_w_grad,
        own_shard(query_b_grad),
        own_shard(value_b_grad),
        out_b_grad,
        up_grad,
        own_shard(up_b_grad),
        down_grad,
        down_b_grad,
        *norm_grads,
    )


def team_layer(mesh):
    axes = ("y", "x", "core", "z")
    inner = Mesh(mesh.devices.reshape(2, 2, 2, 4), axes)
    rows = P(None, PLANE, "z")
    in_specs = (
        rows, rows, P(), P(), P(None, "z"), P(None, "z"), P(None, "z"), P("z", None), P("z"), P("z"),
        P(), P(None, "z"), P("z"), P("z", None), P(), P(), P(), P(), P(),
    )
    out_specs = (
        rows, rows, P(None, "z"), P(None, "z"), P(None, "z"), P("z", None), P("z"), P("z"),
        P(), P(None, "z"), P("z"), P("z", None), P(), P(), P(), P(), P(),
    )
    return jax.shard_map(layer, mesh=inner, in_specs=in_specs, out_specs=out_specs, check_vma=False)


def solution(mesh):
    if dict(mesh.shape) == {"dp": 8, "tensor": 4}:
        return team_layer(mesh)
    return general_layer(mesh)
```

```python
import functools

import jax
import jax.numpy as jnp
from jax import lax
from jax.experimental import pallas as pl
from jax.experimental.pallas import tpu as pltpu
from jax.sharding import Mesh
from jax.sharding import PartitionSpec as P


HEAD_DIM = 64
SEG = 512
SUMM = 50
NBLK = 2


NORM_EPS = 1e-05
MASKED = -1e30


def gelu_tanh(values):
    return jax.nn.gelu(values, approximate=True)


def matmul(left_array, right_array):
    return jnp.dot(left_array, right_array, preferred_element_type=jnp.float32)


def cross_rows(left_array, right_array):
    return lax.dot_general(
        left_array, right_array, (((0,), (0,)), ((), ())), preferred_element_type=jnp.float32
    )


def times_transpose(left_array, right_array):
    return lax.dot_general(
        left_array, right_array, (((1,), (1,)), ((), ())), preferred_element_type=jnp.float32
    )


def normalize(values):
    center = jnp.mean(values, axis=1, keepdims=True)
    shifted = values - center
    spread = jnp.mean(shifted * shifted, axis=1, keepdims=True)
    inverse = lax.rsqrt(spread + NORM_EPS)
    return (shifted * inverse, inverse)


def norm_backward(grad_in, normed, inverse, gain_row):
    gain_grad = jnp.sum(grad_in * normed, axis=0)
    shift_grad = jnp.sum(grad_in, axis=0)
    scaled = grad_in * gain_row
    first_mean = jnp.mean(scaled, axis=1, keepdims=True)
    second_mean = jnp.mean(scaled * normed, axis=1, keepdims=True)
    return (inverse * (scaled - first_mean - normed * second_mean), gain_grad, shift_grad)


def running_sum(counts):
    size = counts.shape[-1]
    places = jnp.arange(size, dtype=jnp.int32)
    upto = (places[:, None] <= places[None, :]).astype(jnp.int32)
    return jnp.sum(counts[..., :, None] * upto, axis=-2, dtype=jnp.int32)


def given_layout(lengths_mb, dealing_mb):
    seq_count = dealing_mb.shape[0]
    labels = jnp.arange(seq_count, dtype=jnp.int32)
    flat_lengths = lengths_mb.reshape(seq_count)
    one_hot = (dealing_mb[:, None] == labels[None, :]).astype(jnp.int32)
    given_len = jnp.sum(one_hot * flat_lengths[None, :], axis=1, dtype=jnp.int32)
    given_off = running_sum(given_len) - given_len
    start_by_seq = jnp.sum(one_hot * given_off[:, None], axis=0, dtype=jnp.int32)
    return (given_len, given_off, start_by_seq)


def buffer_layout(lengths_dev, start_dev, rows_total):
    seq_count = lengths_dev.shape[0]
    end_rows = running_sum(lengths_dev)
    offsets = end_rows - lengths_dev
    row_ids = jnp.arange(rows_total, dtype=jnp.int32)
    holder = jnp.sum(
        (row_ids[:, None] >= end_rows[None, :]).astype(jnp.int32), axis=1, dtype=jnp.int32
    )
    one_hot = (holder[:, None] == jnp.arange(seq_count, dtype=jnp.int32)[None, :]).astype(jnp.int32)
    position = row_ids - jnp.sum(one_hot * offsets[None, :], axis=1, dtype=jnp.int32)
    source = jnp.sum(one_hot * start_dev[None, :], axis=1, dtype=jnp.int32) + position
    return (holder, position, source)


def visible(holder, position, first_row, last_row, key_reach):
    period = SEG + SUMM
    query_seq = holder[first_row:last_row, None]
    key_seq = holder[None, :key_reach]
    query_part = position[first_row:last_row, None] // period
    key_part = position[None, :key_reach] // period
    summary = position[None, :key_reach] % period >= SEG
    query_row = jnp.arange(first_row, last_row, dtype=jnp.int32)[:, None]
    key_row = jnp.arange(key_reach, dtype=jnp.int32)[None, :]
    same_part = (query_part == key_part) & (key_row <= query_row)
    earlier = (key_part < query_part) & summary
    return (query_seq == key_seq) & (same_part | earlier)


def block_scores(queries, keys_all, allowed, score_scale):
    scores = (
        jnp.einsum("qhd,khd->hqk", queries, keys_all, preferred_element_type=jnp.float32)
        * score_scale
    )
    return jnp.where(allowed[None], scores, MASKED)


def shards(
    tokens,
    cotangent,
    lengths,
    dealing,
    query_weight,
    key_weight,
    value_weight,
    out_weight,
    query_bias,
    value_bias,
    out_bias,
    up_weight,
    up_bias,
    down_weight,
    down_bias,
    attn_gain,
    attn_shift,
    mlp_gain,
    mlp_shift,
):
    micro_count = tokens.shape[0]
    tok_rows = tokens.shape[1]
    col_width = tokens.shape[2]
    seq_dev = lengths.shape[2]
    heads_here = query_weight.shape[1] // HEAD_DIM
    head_cols = heads_here * HEAD_DIM
    block_rows = tok_rows // NBLK
    score_scale = HEAD_DIM ** (-0.5)
    device = lax.axis_index("dp")
    column = lax.axis_index("tensor")
    gain_one = attn_gain.astype(jnp.float32)
    shift_one = attn_shift.astype(jnp.float32)
    gain_two = mlp_gain.astype(jnp.float32)
    shift_two = mlp_shift.astype(jnp.float32)
    query_bias_f = query_bias.astype(jnp.float32)
    value_bias_f = value_bias.astype(jnp.float32)
    up_bias_f = up_bias.astype(jnp.float32)
    out_bias_cols = lax.dynamic_slice_in_dim(
        out_bias.astype(jnp.float32), column * col_width, col_width
    )
    down_bias_cols = lax.dynamic_slice_in_dim(
        down_bias.astype(jnp.float32), column * col_width, col_width
    )
    query_w_grad = jnp.zeros(query_weight.shape, jnp.float32)
    key_w_grad = jnp.zeros(key_weight.shape, jnp.float32)
    value_w_grad = jnp.zeros(value_weight.shape, jnp.float32)
    out_w_grad = jnp.zeros(out_weight.shape, jnp.float32)
    query_b_grad = jnp.zeros(query_bias.shape, jnp.float32)
    value_b_grad = jnp.zeros(value_bias.shape, jnp.float32)
    out_b_grad = jnp.zeros(out_bias.shape, jnp.float32)
    up_w_grad = jnp.zeros(up_weight.shape, jnp.float32)
    up_b_grad = jnp.zeros(up_bias.shape, jnp.float32)
    down_w_grad = jnp.zeros(down_weight.shape, jnp.float32)
    down_b_grad = jnp.zeros(down_bias.shape, jnp.float32)
    gain_one_grad = jnp.zeros(attn_gain.shape, jnp.float32)
    shift_one_grad = jnp.zeros(attn_shift.shape, jnp.float32)
    gain_two_grad = jnp.zeros(mlp_gain.shape, jnp.float32)
    shift_two_grad = jnp.zeros(mlp_shift.shape, jnp.float32)
    layer_parts = []
    grad_parts = []
    for micro_step in range(micro_count):
        lengths_mb = lengths[micro_step]
        dealing_mb = dealing[micro_step]
        given_len, given_off, start_by_seq = given_layout(lengths_mb, dealing_mb)
        lengths_dev = lax.dynamic_index_in_dim(lengths_mb, device, 0, keepdims=False)
        start_dev = lax.dynamic_slice_in_dim(start_by_seq, device * seq_dev, seq_dev)
        holder, position, source = buffer_layout(lengths_dev, start_dev, tok_rows)
        blank_rows = jnp.zeros((tok_rows, col_width), jnp.bfloat16)
        pieces = (
            lax.all_gather(tokens[micro_step], "dp", axis=0, tiled=True),
            lax.all_gather(cotangent[micro_step], "dp", axis=0, tiled=True),
        )
        span_rows = pieces[0].shape[0]
        inside = ((source >= 0) & (source < span_rows))[:, None]
        fetch_at = jnp.clip(source, 0, span_rows - 1)
        tok_buf = jnp.where(inside, jnp.take(pieces[0], fetch_at, axis=0), blank_rows)
        cot_buf = jnp.where(inside, jnp.take(pieces[1], fetch_at, axis=0), blank_rows)
        tok_full, cot_full = (
            lax.all_gather(tok_buf, "tensor", axis=1, tiled=True),
            lax.all_gather(cot_buf, "tensor", axis=1, tiled=True),
        )
        normed_one, inverse_one = normalize(tok_full.astype(jnp.float32))
        first_in = (normed_one * gain_one + shift_one).astype(jnp.bfloat16)
        queries = (
            (matmul(first_in, query_weight) + query_bias_f)
            .astype(jnp.bfloat16)
            .reshape(tok_rows, heads_here, HEAD_DIM)
        )
        keys_here = (
            matmul(first_in, key_weight)
            .astype(jnp.bfloat16)
            .reshape(tok_rows, heads_here, HEAD_DIM)
        )
        values_here = (
            (matmul(first_in, value_weight) + value_bias_f)
            .astype(jnp.bfloat16)
            .reshape(tok_rows, heads_here, HEAD_DIM)
        )
        outputs = []
        row_tops = []
        row_totals = []
        for block_index in range(NBLK):
            row_lower = block_index * block_rows
            row_upper = row_lower + block_rows
            allowed = visible(holder, position, row_lower, row_upper, row_upper)
            scores = block_scores(
                queries[row_lower:row_upper], keys_here[:row_upper], allowed, score_scale
            )
            row_top = jnp.max(scores, axis=2, keepdims=True)
            exp_terms = jnp.exp(scores - row_top)
            row_total = jnp.sum(exp_terms, axis=2, keepdims=True)
            attn_prob = exp_terms / row_total
            outputs.append(
                jnp.einsum(
                    "hqk,khd->qhd",
                    attn_prob.astype(jnp.bfloat16),
                    values_here[:row_upper],
                    preferred_element_type=jnp.float32,
                )
            )
            row_tops.append(row_top)
            row_totals.append(row_total)
        mixed_heads = (
            jnp.concatenate(outputs, axis=0).reshape(tok_rows, head_cols).astype(jnp.bfloat16)
        )
        attn_cols = lax.psum_scatter(
            matmul(mixed_heads, out_weight), "tensor", scatter_dimension=1, tiled=True
        )
        resid_cols = tok_buf.astype(jnp.float32) + attn_cols + out_bias_cols
        resid_full = lax.all_gather(resid_cols.astype(jnp.bfloat16), "tensor", axis=1, tiled=True)
        normed_two, inverse_two = normalize(resid_full.astype(jnp.float32))
        second_in = (normed_two * gain_two + shift_two).astype(jnp.bfloat16)
        hidden_pre = matmul(second_in, up_weight) + up_bias_f
        hidden_act, gelu_pull = jax.vjp(gelu_tanh, hidden_pre)
        hidden = hidden_act.astype(jnp.bfloat16)
        mlp_cols = lax.psum_scatter(
            matmul(hidden, down_weight).astype(jnp.bfloat16),
            "tensor",
            scatter_dimension=1,
            tiled=True,
        ).astype(jnp.float32)
        layer_cols = (resid_cols + mlp_cols + down_bias_cols).astype(jnp.bfloat16)
        grad_out = cot_full.astype(jnp.float32)
        down_w_grad = down_w_grad + cross_rows(hidden, cot_full)
        down_b_grad = down_b_grad + jnp.sum(grad_out, axis=0)
        hidden_grad = gelu_pull(times_transpose(cot_full, down_weight))[0]
        up_b_grad = up_b_grad + jnp.sum(hidden_grad, axis=0)
        hidden_low = hidden_grad.astype(jnp.bfloat16)
        up_w_grad = up_w_grad + cross_rows(second_in, hidden_low)
        second_cols = lax.psum_scatter(
            times_transpose(hidden_low, up_weight), "tensor", scatter_dimension=1, tiled=True
        )
        second_grad = lax.all_gather(
            second_cols.astype(jnp.bfloat16), "tensor", axis=1, tiled=True
        ).astype(jnp.float32)
        resid_back, gain_part, shift_part = norm_backward(
            second_grad, normed_two, inverse_two, gain_two
        )
        gain_two_grad = gain_two_grad + gain_part
        shift_two_grad = shift_two_grad + shift_part
        resid_grad = grad_out + resid_back
        out_b_grad = out_b_grad + jnp.sum(resid_grad, axis=0)
        attn_low = resid_grad.astype(jnp.bfloat16)
        out_w_grad = out_w_grad + cross_rows(mixed_heads, attn_low)
        mixed_grad = (
            times_transpose(attn_low, out_weight)
            .astype(jnp.bfloat16)
            .reshape(tok_rows, heads_here, HEAD_DIM)
        )
        query_parts = []
        key_acc = jnp.zeros((tok_rows, heads_here, HEAD_DIM), jnp.float32)
        value_acc = jnp.zeros((tok_rows, heads_here, HEAD_DIM), jnp.float32)
        for block_index in range(NBLK):
            row_lower = block_index * block_rows
            row_upper = row_lower + block_rows
            allowed = visible(holder, position, row_lower, row_upper, row_upper)
            scores = block_scores(
                queries[row_lower:row_upper], keys_here[:row_upper], allowed, score_scale
            )
            attn_prob = jnp.exp(scores - row_tops[block_index]) / row_totals[block_index]
            grad_block = mixed_grad[row_lower:row_upper]
            prob_grad = jnp.einsum(
                "qhd,khd->hqk",
                grad_block,
                values_here[:row_upper],
                preferred_element_type=jnp.float32,
            )
            inner_sum = jnp.sum(attn_prob * prob_grad, axis=2, keepdims=True)
            score_grad = (attn_prob * (prob_grad - inner_sum)).astype(jnp.bfloat16)
            query_parts.append(
                jnp.einsum(
                    "hqk,khd->qhd",
                    score_grad,
                    keys_here[:row_upper],
                    preferred_element_type=jnp.float32,
                )
                * score_scale
            )
            pad_rows = ((0, tok_rows - row_upper), (0, 0), (0, 0))
            key_acc = key_acc + jnp.pad(
                jnp.einsum(
                    "hqk,qhd->khd",
                    score_grad,
                    queries[row_lower:row_upper],
                    preferred_element_type=jnp.float32,
                )
                * score_scale,
                pad_rows,
            )
            value_acc = value_acc + jnp.pad(
                jnp.einsum(
                    "hqk,qhd->khd",
                    attn_prob.astype(jnp.bfloat16),
                    grad_block,
                    preferred_element_type=jnp.float32,
                ),
                pad_rows,
            )
        query_grad = jnp.concatenate(query_parts, axis=0).reshape(tok_rows, head_cols)
        key_grad = key_acc.reshape(tok_rows, head_cols)
        value_grad = value_acc.reshape(tok_rows, head_cols)
        query_b_grad = query_b_grad + jnp.sum(query_grad, axis=0)
        value_b_grad = value_b_grad + jnp.sum(value_grad, axis=0)
        query_low = query_grad.astype(jnp.bfloat16)
        key_low = key_grad.astype(jnp.bfloat16)
        value_low = value_grad.astype(jnp.bfloat16)
        query_w_grad = query_w_grad + cross_rows(first_in, query_low)
        key_w_grad = key_w_grad + cross_rows(first_in, key_low)
        value_w_grad = value_w_grad + cross_rows(first_in, value_low)
        first_part = (
            times_transpose(query_low, query_weight)
            + times_transpose(key_low, key_weight)
            + times_transpose(value_low, value_weight)
        )
        first_cols = lax.psum_scatter(first_part, "tensor", scatter_dimension=1, tiled=True)
        first_grad = lax.all_gather(
            first_cols.astype(jnp.bfloat16), "tensor", axis=1, tiled=True
        ).astype(jnp.float32)
        input_back, gain_part, shift_part = norm_backward(
            first_grad, normed_one, inverse_one, gain_one
        )
        gain_one_grad = gain_one_grad + gain_part
        shift_one_grad = shift_one_grad + shift_part
        input_cols = lax.dynamic_slice_in_dim(
            resid_grad + input_back, column * col_width, col_width, axis=1
        ).astype(jnp.bfloat16)
        packed = jnp.concatenate([layer_cols, input_cols], axis=1)
        given_end = given_off + given_len
        dest_off = (running_sum(lengths_mb) - lengths_mb).reshape(-1)
        labels = jnp.arange(dealing_mb.shape[0], dtype=jnp.int32)
        give_row_ids = jnp.arange(tok_rows * lax.axis_size("dp"), dtype=jnp.int32)
        owner_seq = jnp.sum(
            (give_row_ids[:, None] >= given_end[None, :]).astype(jnp.int32), axis=1, dtype=jnp.int32
        )
        one_hot = (owner_seq[:, None] == labels[None, :]).astype(jnp.int32)
        within = give_row_ids - jnp.sum(one_hot * given_off[None, :], axis=1, dtype=jnp.int32)
        seq_label = jnp.sum(one_hot * dealing_mb[None, :], axis=1, dtype=jnp.int32)
        seq_hot = (seq_label[:, None] == labels[None, :]).astype(jnp.int32)
        buffer_row = jnp.sum(seq_hot * dest_off[None, :], axis=1, dtype=jnp.int32) + within
        owner_dev = seq_label // seq_dev
        is_mine = owner_dev == device
        fetched = jnp.take(packed, jnp.clip(buffer_row, 0, tok_rows - 1), axis=0).astype(
            jnp.float32
        )
        returned = lax.psum_scatter(
            jnp.where(is_mine[:, None], fetched, 0.0).astype(jnp.bfloat16),
            "dp",
            scatter_dimension=0,
            tiled=True,
        ).astype(jnp.float32)
        layer_parts.append(returned[:, :col_width].astype(jnp.bfloat16))
        grad_parts.append(returned[:, col_width:].astype(jnp.bfloat16))
    (
        query_w_grad,
        key_w_grad,
        value_w_grad,
        out_w_grad,
        query_b_grad,
        value_b_grad,
        out_b_grad,
        gain_one_grad,
        shift_one_grad,
        up_w_grad,
        up_b_grad,
        down_w_grad,
        down_b_grad,
        gain_two_grad,
        shift_two_grad,
    ) = lax.psum(
        (
            query_w_grad,
            key_w_grad,
            value_w_grad,
            out_w_grad,
            query_b_grad,
            value_b_grad,
            out_b_grad,
            gain_one_grad,
            shift_one_grad,
            up_w_grad,
            up_b_grad,
            down_w_grad,
            down_b_grad,
            gain_two_grad,
            shift_two_grad,
        ),
        "dp",
    )
    layer_out = jnp.stack(layer_parts, axis=0)
    input_grad = jnp.stack(grad_parts, axis=0)
    return (
        layer_out,
        input_grad,
        query_w_grad,
        key_w_grad,
        value_w_grad,
        out_w_grad,
        query_b_grad,
        value_b_grad,
        out_b_grad,
        up_w_grad,
        up_b_grad,
        down_w_grad,
        down_b_grad,
        gain_one_grad,
        shift_one_grad,
        gain_two_grad,
        shift_two_grad,
    )


def general_layer(mesh):
    in_specs = (
        P(None, "dp", "tensor"),
        P(None, "dp", "tensor"),
        P(),
        P(),
        P(None, "tensor"),
        P(None, "tensor"),
        P(None, "tensor"),
        P("tensor", None),
        P("tensor"),
        P("tensor"),
        P(),
        P(None, "tensor"),
        P("tensor"),
        P("tensor", None),
        P(),
        P(),
        P(),
        P(),
        P(),
    )
    out_specs = (
        P(None, "dp", "tensor"),
        P(None, "dp", "tensor"),
        P(None, "tensor"),
        P(None, "tensor"),
        P(None, "tensor"),
        P("tensor", None),
        P("tensor"),
        P("tensor"),
        P(),
        P(None, "tensor"),
        P("tensor"),
        P("tensor", None),
        P(),
        P(),
        P(),
        P(),
        P(),
    )
    return jax.shard_map(shards, mesh=mesh, in_specs=in_specs, out_specs=out_specs, check_vma=False)


ROWS = 1024
QBLK = 256
PAIR = 128


def slot_of(block, rank):
    piece = jnp.bitwise_xor(block, rank)
    return jnp.bitwise_or(piece >> 1, (piece & 1) << 1)


def rows_of(block, rank):
    return pl.ds(pl.multiple_of(slot_of(block, rank) * QBLK, QBLK), QBLK)


def fill_bias(bias_ref, key_info_ref, query_info_ref):
    for block in range(ROWS // QBLK):
        reach = (block + 1) * QBLK
        cols = pl.ds(block * QBLK, QBLK)
        key_part = key_info_ref[pl.ds(0, reach), 0:1]
        key_summary = key_info_ref[pl.ds(0, reach), 1:2]
        query_part = query_info_ref[0:1, cols]
        query_seq = query_info_ref[1:2, cols]
        key_row = lax.broadcasted_iota(jnp.int32, (reach, QBLK), 0)
        query_row = lax.broadcasted_iota(jnp.int32, (reach, QBLK), 1) + block * QBLK
        seen = (key_row <= query_row) & ((key_part == query_part) | (key_summary == query_seq))
        bias_ref[pl.ds(0, reach), cols] = jnp.where(seen, 0.0, MASKED)


def nt_dot(left, right):
    return lax.dot_general(left, right, (((1,), (1,)), ((), ())), preferred_element_type=jnp.float32)


def nn_dot(left, right):
    return jnp.dot(left, right, preferred_element_type=jnp.float32)


def head_lanes(block, head):
    lane = lax.broadcasted_iota(jnp.int32, block.shape, 1)
    inside = (lane >= head * HEAD_DIM) & (lane < (head + 1) * HEAD_DIM)
    return jnp.where(inside, block, jnp.zeros_like(block))


def attend_kernel(
    rank_ref, query_ref, key_ref, value_ref, key_info_ref, query_info_ref, out_ref, bias_ref, keys, value_t
):
    rank = rank_ref[0]

    @pl.when(pl.program_id(0) == 0)
    def _():
        fill_bias(bias_ref, key_info_ref, query_info_ref)

    for block in range(ROWS // QBLK):
        here = rows_of(block, rank)
        keys[pl.ds(block * QBLK, QBLK), :] = key_ref[here, :]
        value_t[:, pl.ds(block * QBLK, QBLK)] = value_ref[here, :].T
    for block in range(ROWS // QBLK):
        reach = (block + 1) * QBLK
        here = rows_of(block, rank)
        queries = query_ref[here, :] * jnp.bfloat16(HEAD_DIM**-0.5)
        bias = bias_ref[pl.ds(0, reach), pl.ds(block * QBLK, QBLK)]
        parts = []
        for head in range(2):
            scores = nt_dot(keys[pl.ds(0, reach), :], head_lanes(queries, head)) + bias
            top = jnp.max(scores, axis=0, keepdims=True)
            terms = jnp.exp(scores - top)
            total = jnp.sum(terms, axis=0, keepdims=True)
            heads_t = nn_dot(
                value_t[pl.ds(head * HEAD_DIM, HEAD_DIM), pl.ds(0, reach)], terms.astype(jnp.bfloat16)
            )
            parts.append(heads_t / total)
        out_ref[here, :] = jnp.concatenate(parts, axis=0).T.astype(out_ref.dtype)


def attend(qkv, rank, key_info, query_info):
    pairs = qkv.shape[1] // (3 * PAIR)
    cells = ROWS * ROWS * 5 // 8
    return pl.pallas_call(
        attend_kernel,
        grid_spec=pltpu.PrefetchScalarGridSpec(
            num_scalar_prefetch=1,
            grid=(pairs,),
            in_specs=[
                pl.BlockSpec((ROWS, PAIR), lambda i, r: (0, i)),
                pl.BlockSpec((ROWS, PAIR), lambda i, r: (0, pairs + i)),
                pl.BlockSpec((ROWS, PAIR), lambda i, r: (0, 2 * pairs + i)),
                pl.BlockSpec((ROWS, 2), lambda i, r: (0, 0)),
                pl.BlockSpec((2, ROWS), lambda i, r: (0, 0)),
            ],
            out_specs=pl.BlockSpec((ROWS, PAIR), lambda i, r: (0, i)),
            scratch_shapes=[
                pltpu.VMEM((ROWS, ROWS), jnp.float32),
                pltpu.VMEM((ROWS, PAIR), jnp.bfloat16),
                pltpu.VMEM((PAIR, ROWS), jnp.bfloat16),
            ],
        ),
        out_shape=jax.ShapeDtypeStruct((ROWS, pairs * PAIR), jnp.bfloat16),
        compiler_params=pltpu.CompilerParams(vmem_limit_bytes=24 << 20),
        cost_estimate=light(),
        name="attend",
    )(rank, qkv, qkv, qkv, key_info, query_info)


def attend_back_kernel(
    rank_ref,
    query_ref,
    key_ref,
    value_ref,
    grad_ref,
    key_info_ref,
    query_info_ref,
    query_out,
    key_out,
    value_out,
    sums_out,
    bias_ref,
    keys,
    values,
    key_t,
    key_acc,
    value_acc,
):
    rank = rank_ref[0]
    scale = HEAD_DIM**-0.5

    @pl.when(pl.program_id(0) == 0)
    def _():
        fill_bias(bias_ref, key_info_ref, query_info_ref)

    for block in range(ROWS // QBLK):
        here = rows_of(block, rank)
        there = pl.ds(block * QBLK, QBLK)
        keys[there, :] = key_ref[here, :]
        values[there, :] = value_ref[here, :]
        key_t[:, there] = key_ref[here, :].T
    query_sum = jnp.zeros((1, PAIR), jnp.float32)
    for block in reversed(range(ROWS // QBLK)):
        reach = (block + 1) * QBLK
        here = rows_of(block, rank)
        upto = pl.ds(0, reach)
        queries = query_ref[here, :] * jnp.bfloat16(scale)
        grads = grad_ref[here, :]
        bias = bias_ref[upto, pl.ds(block * QBLK, QBLK)]
        parts = []
        key_add = None
        value_add = None
        for head in range(2):
            query_h = head_lanes(queries, head)
            grad_h = head_lanes(grads, head)
            scores = nt_dot(keys[upto, :], query_h) + bias
            top = jnp.max(scores, axis=0, keepdims=True)
            terms = jnp.exp(scores - top)
            prob = terms * (1.0 / jnp.sum(terms, axis=0, keepdims=True))
            prob_grad = nt_dot(values[upto, :], grad_h)
            inner = jnp.sum(prob * prob_grad, axis=0, keepdims=True)
            score_grad = (prob * (prob_grad - inner)).astype(jnp.bfloat16)
            value_part = nn_dot(prob.astype(jnp.bfloat16), grad_h)
            key_part = nn_dot(score_grad, query_h)
            value_add = value_part if value_add is None else value_add + value_part
            key_add = key_part if key_add is None else key_add + key_part
            parts.append(nn_dot(key_t[pl.ds(head * HEAD_DIM, HEAD_DIM), upto], score_grad))
        if block == ROWS // QBLK - 1:
            key_acc[...] = key_add
            value_acc[...] = value_add
        else:
            key_acc[upto, :] += key_add
            value_acc[upto, :] += value_add
        query_grad = jnp.concatenate(parts, axis=0).T * scale
        query_sum = query_sum + jnp.sum(query_grad, axis=0, keepdims=True)
        query_out[here, :] = query_grad.astype(query_out.dtype)
    for block in range(ROWS // QBLK):
        here = rows_of(block, rank)
        there = pl.ds(block * QBLK, QBLK)
        key_out[here, :] = key_acc[there, :].astype(key_out.dtype)
        value_out[here, :] = value_acc[there, :].astype(value_out.dtype)
    value_sum = jnp.sum(value_acc[...], axis=0, keepdims=True)
    row = lax.broadcasted_iota(jnp.int32, (8, PAIR), 0)
    sums_out[...] = jnp.where(row == 0, query_sum, jnp.where(row == 1, value_sum, 0.0))


def attend_back(qkv, grads, rank, key_info, query_info):
    pairs = qkv.shape[1] // (3 * PAIR)
    cells = ROWS * ROWS * 5 // 8
    block = (ROWS, PAIR)
    wide = jax.ShapeDtypeStruct((ROWS, pairs * PAIR), jnp.bfloat16)
    return pl.pallas_call(
        attend_back_kernel,
        grid_spec=pltpu.PrefetchScalarGridSpec(
            num_scalar_prefetch=1,
            grid=(pairs,),
            in_specs=[
                pl.BlockSpec(block, lambda i, r: (0, i)),
                pl.BlockSpec(block, lambda i, r: (0, pairs + i)),
                pl.BlockSpec(block, lambda i, r: (0, 2 * pairs + i)),
                pl.BlockSpec(block, lambda i, r: (0, i)),
                pl.BlockSpec((ROWS, 2), lambda i, r: (0, 0)),
                pl.BlockSpec((2, ROWS), lambda i, r: (0, 0)),
            ],
            out_specs=[
                pl.BlockSpec(block, lambda i, r: (0, i)),
                pl.BlockSpec(block, lambda i, r: (0, i)),
                pl.BlockSpec(block, lambda i, r: (0, i)),
                pl.BlockSpec((8, PAIR), lambda i, r: (0, i)),
            ],
            scratch_shapes=[
                pltpu.VMEM((ROWS, ROWS), jnp.float32),
                pltpu.VMEM(block, jnp.bfloat16),
                pltpu.VMEM(block, jnp.bfloat16),
                pltpu.VMEM((PAIR, ROWS), jnp.bfloat16),
                pltpu.VMEM(block, jnp.float32),
                pltpu.VMEM(block, jnp.float32),
            ],
        ),
        out_shape=[wide, wide, wide, jax.ShapeDtypeStruct((8, pairs * PAIR), jnp.float32)],
        compiler_params=pltpu.CompilerParams(vmem_limit_bytes=28 << 20),
        cost_estimate=light(),
        name="attend_back",
    )(rank, qkv, qkv, qkv, grads, key_info, query_info)


WIDE = 512
VMEM_BYTES = 56 << 20


def light(flops=1 << 20):
    return pl.CostEstimate(flops=flops, bytes_accessed=1 << 12, transcendentals=0)


def settings():
    return pltpu.CompilerParams(vmem_limit_bytes=VMEM_BYTES)


def whole(shape):
    return pl.BlockSpec(shape, lambda i: (0,) * len(shape))


def project_kernel(near_ref, far_ref, weight_ref, bias_ref, out_ref):
    rows = near_ref.shape[0]
    bias = bias_ref[...]
    out_ref[pl.ds(0, rows), :] = (nt_dot(near_ref[...], weight_ref[...]) + bias).astype(out_ref.dtype)
    out_ref[pl.ds(rows, rows), :] = (nt_dot(far_ref[...], weight_ref[...]) + bias).astype(out_ref.dtype)


def project(near, far, weight, bias):
    rows, depth = near.shape
    cols = weight.shape[0]
    return pl.pallas_call(
        project_kernel,
        grid=(cols // WIDE,),
        in_specs=[
            whole((rows, depth)),
            whole((rows, depth)),
            pl.BlockSpec((WIDE, depth), lambda i: (i, 0)),
            pl.BlockSpec((1, WIDE), lambda i: (0, i)),
        ],
        out_specs=pl.BlockSpec((2 * rows, WIDE), lambda i: (0, i)),
        out_shape=jax.ShapeDtypeStruct((2 * rows, cols), jnp.bfloat16),
        compiler_params=settings(),
        cost_estimate=light(),
        name="project",
    )(near, far, weight, bias)


def expand_kernel(near_ref, far_ref, weight_ref, bias_ref, hidden_ref, slope_ref):
    rows = near_ref.shape[0]
    bias = bias_ref[...]
    for part, ref in enumerate((near_ref, far_ref)):
        at = pl.ds(part * rows, rows)
        pre = nt_dot(ref[...], weight_ref[...]) + bias
        cube = 0.044715 * pre * pre
        bend = jnp.tanh((0.7978845608028654 * pre) * (1.0 + cube))
        half = 0.5 + 0.5 * bend
        inner = 0.7978845608028654 + (3.0 * 0.7978845608028654) * cube
        hidden_ref[at, :] = (pre * half).astype(jnp.bfloat16)
        slope_ref[at, :] = (half + (pre * half) * ((1.0 - bend) * inner)).astype(jnp.bfloat16)


def expand(near, far, weight, bias):
    rows, depth = near.shape
    cols = weight.shape[0]
    out = jax.ShapeDtypeStruct((2 * rows, cols), jnp.bfloat16)
    return pl.pallas_call(
        expand_kernel,
        grid=(cols // WIDE,),
        in_specs=[
            whole((rows, depth)),
            whole((rows, depth)),
            pl.BlockSpec((WIDE, depth), lambda i: (i, 0)),
            pl.BlockSpec((1, WIDE), lambda i: (0, i)),
        ],
        out_specs=[pl.BlockSpec((2 * rows, WIDE), lambda i: (0, i))] * 2,
        out_shape=[out, out],
        compiler_params=settings(),
        cost_estimate=light(),
        name="expand",
    )(near, far, weight, bias)


def expand_back_kernel(near_ref, far_ref, weight_ref, slope_ref, low_ref, sums_ref):
    rows = near_ref.shape[0]
    total = jnp.zeros((1, low_ref.shape[1]), jnp.float32)
    for part, ref in enumerate((near_ref, far_ref)):
        at = pl.ds(part * rows, rows)
        grad = nt_dot(ref[...], weight_ref[...]) * slope_ref[at, :].astype(jnp.float32)
        total = total + jnp.sum(grad, axis=0, keepdims=True)
        low_ref[at, :] = grad.astype(jnp.bfloat16)
    sums_ref[...] = jnp.broadcast_to(total, sums_ref.shape)


def expand_back(near, far, weight, slope):
    rows, depth = near.shape
    cols = weight.shape[0]
    return pl.pallas_call(
        expand_back_kernel,
        grid=(cols // WIDE,),
        in_specs=[
            whole((rows, depth)),
            whole((rows, depth)),
            pl.BlockSpec((WIDE, depth), lambda i: (i, 0)),
            pl.BlockSpec((2 * rows, WIDE), lambda i: (0, i)),
        ],
        out_specs=[pl.BlockSpec((2 * rows, WIDE), lambda i: (0, i)), pl.BlockSpec((8, WIDE), lambda i: (0, i))],
        out_shape=[
            jax.ShapeDtypeStruct((2 * rows, cols), jnp.bfloat16),
            jax.ShapeDtypeStruct((8, cols), jnp.float32),
        ],
        compiler_params=settings(),
        cost_estimate=light(),
        name="expand_back",
    )(near, far, weight, slope)


def partial_kernel(left_ref, weight_ref, near_ref, far_ref):
    rows = near_ref.shape[0]
    far_ref[...] = nn_dot(left_ref[pl.ds(rows, rows), :], weight_ref[...]).astype(far_ref.dtype)
    near_ref[...] = nn_dot(left_ref[pl.ds(0, rows), :], weight_ref[...])


def partial_sums(left, weight):
    rows, depth = left.shape
    cols = weight.shape[1]
    half = rows // 2
    return pl.pallas_call(
        partial_kernel,
        grid=(cols // WIDE,),
        in_specs=[whole((rows, depth)), pl.BlockSpec((depth, WIDE), lambda i: (0, i))],
        out_specs=[pl.BlockSpec((half, WIDE), lambda i: (0, i))] * 2,
        out_shape=[
            jax.ShapeDtypeStruct((half, cols), jnp.float32),
            jax.ShapeDtypeStruct((half, cols), jnp.bfloat16),
        ],
        compiler_params=settings(),
        cost_estimate=light(),
        name="partial_sums",
    )(left, weight)


def tn_dot(left, right):
    return lax.dot_general(left, right, (((0,), (0,)), ((), ())), preferred_element_type=jnp.float32)


def cross_kernel(left_a, near_a, far_a, left_b, near_b, far_b, out_ref):
    rows = near_a.shape[0]
    top, low = pl.ds(0, rows), pl.ds(rows, rows)
    total = tn_dot(left_a[top, :], near_a[...]) + tn_dot(left_a[low, :], far_a[...])
    total = total + tn_dot(left_b[top, :], near_b[...]) + tn_dot(left_b[low, :], far_b[...])
    out_ref[...] = total.astype(out_ref.dtype)


def cross_sums(left_a, right_a, left_b, right_b, start, size):
    rows = left_a.shape[0]
    cols = right_a[0].shape[1]
    tall = 256
    first = start // tall
    left_spec = pl.BlockSpec((rows, tall), lambda i: (0, first + i))
    right_spec = whole((rows // 2, cols))
    return pl.pallas_call(
        cross_kernel,
        grid=(size // tall,),
        in_specs=[left_spec, right_spec, right_spec] * 2,
        out_specs=pl.BlockSpec((tall, cols), lambda i: (i, 0)),
        out_shape=jax.ShapeDtypeStruct((size, cols), jnp.bfloat16),
        compiler_params=settings(),
        cost_estimate=light(),
        name="cross_sums",
    )(left_a, *right_a, left_b, *right_b)


def flip_kernel(first_ref, weight_ref, out_ref):
    out_ref[...] = weight_ref[...].T


def flipped(weight, first, count):
    depth = weight.shape[0]
    return pl.pallas_call(
        flip_kernel,
        grid_spec=pltpu.PrefetchScalarGridSpec(
            num_scalar_prefetch=1,
            grid=(count,),
            in_specs=[pl.BlockSpec((depth, 128), lambda i, first: (0, first[0] + i))],
            out_specs=pl.BlockSpec((128, depth), lambda i, first: (i, 0)),
        ),
        out_shape=jax.ShapeDtypeStruct((count * 128, depth), weight.dtype),
        compiler_params=settings(),
        cost_estimate=light(),
        name="flipped",
    )(first.reshape(1).astype(jnp.int32), weight)


def attn_pack_kernel(
    place_ref, query_ref, key_ref, value_ref, out_w_ref, bias_mine, bias_other, mine_ref, other_ref
):
    half = place_ref[1]
    mine_ref[pl.ds(4 * HEAD_DIM, 8), :] = bias_mine[...]
    other_ref[pl.ds(4 * HEAD_DIM, 8), :] = bias_other[...]
    for which, ref in enumerate((mine_ref, other_ref)):
        rows = pl.ds(pl.multiple_of(jnp.where(which == 0, half, 1 - half) * HEAD_DIM, HEAD_DIM), HEAD_DIM)
        ref[pl.ds(3 * HEAD_DIM, HEAD_DIM), :] = out_w_ref[rows, :]
    for index, source in enumerate((query_ref, key_ref, value_ref)):
        flat = source[...].T
        low, high = flat[:HEAD_DIM, :], flat[HEAD_DIM:, :]
        at = pl.ds(index * HEAD_DIM, HEAD_DIM)
        mine_ref[at, :] = jnp.where(half == 0, low, high)
        other_ref[at, :] = jnp.where(half == 0, high, low)


def attn_pack(query_weight, key_weight, value_weight, out_weight, bias_mine, bias_other, team, half):
    depth = query_weight.shape[0]
    out = jax.ShapeDtypeStruct((4 * HEAD_DIM + 8, depth), query_weight.dtype)
    column = pl.BlockSpec((depth, 128), lambda i, place: (0, place[0]))
    full = pl.BlockSpec((4 * HEAD_DIM + 8, depth), lambda i, place: (0, 0))
    bias = pl.BlockSpec((8, depth), lambda i, place: (0, 0))
    return pl.pallas_call(
        attn_pack_kernel,
        grid_spec=pltpu.PrefetchScalarGridSpec(
            num_scalar_prefetch=1,
            grid=(1,),
            in_specs=[column, column, column, pl.BlockSpec((128, depth), lambda i, place: (place[0], 0)), bias, bias],
            out_specs=[full, full],
        ),
        out_shape=[out, out],
        compiler_params=settings(),
        cost_estimate=light(),
        name="attn_pack",
    )(jnp.stack([team, half]).astype(jnp.int32), query_weight, key_weight, value_weight, out_weight, bias_mine, bias_other)


def pick_kernel(index_ref, rows_ref, out_ref):
    wanted = index_ref[...]
    place = lax.broadcasted_iota(jnp.int32, (wanted.shape[0], rows_ref.shape[0]), 1)
    hot = jnp.where(place == wanted, 1.0, 0.0).astype(jnp.bfloat16)
    out_ref[...] = nn_dot(hot, rows_ref[...]).astype(out_ref.dtype)


def pick_rows(index, rows, tall):
    count = index.shape[0]
    cols = rows.shape[1]
    return pl.pallas_call(
        pick_kernel,
        grid=(count // tall,),
        in_specs=[pl.BlockSpec((tall, 1), lambda i: (i, 0)), whole(rows.shape)],
        out_specs=pl.BlockSpec((tall, cols), lambda i: (i, 0)),
        out_shape=jax.ShapeDtypeStruct((count, cols), rows.dtype),
        compiler_params=settings(),
        cost_estimate=light(),
        name="pick_rows",
    )(index[:, None], rows)


def drop_kernel(index_ref, rows_ref, out_ref):
    wanted = index_ref[...]
    tall = out_ref.shape[0]
    place = lax.broadcasted_iota(jnp.int32, (tall, rows_ref.shape[0]), 0) + pl.program_id(0) * tall
    hot = jnp.where(place == wanted, 1.0, 0.0).astype(jnp.bfloat16)
    out_ref[...] = nn_dot(hot, rows_ref[...]).astype(out_ref.dtype)


def drop_rows(index, rows, count, tall):
    cols = rows.shape[1]
    return pl.pallas_call(
        drop_kernel,
        grid=(count // tall,),
        in_specs=[whole((1, index.shape[0])), whole(rows.shape)],
        out_specs=pl.BlockSpec((tall, cols), lambda i: (i, 0)),
        out_shape=jax.ShapeDtypeStruct((count, cols), rows.dtype),
        compiler_params=settings(),
        cost_estimate=light(),
        name="drop_rows",
    )(index[None, :], rows)


def settle_kernel(index_ref, boxes_ref, out_ref):
    wanted = index_ref[...]
    place = lax.broadcasted_iota(jnp.int32, (out_ref.shape[0], boxes_ref.shape[1]), 0)
    hot = jnp.where(place == wanted, 1.0, 0.0).astype(jnp.bfloat16)
    out_ref[...] = nn_dot(hot, boxes_ref[0]).astype(out_ref.dtype)


def settle_rows(index, boxes, count):
    depth, slots, cols = boxes.shape
    return pl.pallas_call(
        settle_kernel,
        grid=(depth,),
        in_specs=[whole((1, slots)), pl.BlockSpec((1, slots, cols), lambda i: (i, 0, 0))],
        out_specs=pl.BlockSpec((count, cols), lambda i: (0, i)),
        out_shape=jax.ShapeDtypeStruct((count, depth * cols), boxes.dtype),
        compiler_params=settings(),
        cost_estimate=light(),
        name="settle_rows",
    )(index[None, :], boxes)


def unsettle_kernel(index_ref, rows_ref, out_ref):
    wanted = index_ref[...]
    place = lax.broadcasted_iota(jnp.int32, (wanted.shape[0], rows_ref.shape[0]), 1)
    hot = jnp.where(place == wanted, 1.0, 0.0).astype(jnp.bfloat16)
    out_ref[0] = nn_dot(hot, rows_ref[...]).astype(out_ref.dtype)


def unsettle_rows(index, rows, depth):
    slots = index.shape[0]
    count = rows.shape[0]
    cols = rows.shape[1] // depth
    return pl.pallas_call(
        unsettle_kernel,
        grid=(depth,),
        in_specs=[whole((slots, 1)), pl.BlockSpec((count, cols), lambda i: (0, i))],
        out_specs=pl.BlockSpec((1, slots, cols), lambda i: (i, 0, 0)),
        out_shape=jax.ShapeDtypeStruct((depth, slots, cols), rows.dtype),
        compiler_params=settings(),
        cost_estimate=light(),
        name="unsettle_rows",
    )(index[:, None], rows)


def code_of(place, own):
    return jnp.bitwise_xor(place, own)


def piece_of(code):
    return ((code >> 2) & 1) + 2 * (code & 1)


def stack_kernel(own_ref, near_ref, far_ref, out_ref):
    code = code_of(pl.program_id(0), own_ref[0])
    block = jnp.where((code & 2) == 0, near_ref[...], far_ref[...])
    out_ref[...] = block.astype(out_ref.dtype)


def stack_kernel_t(own_ref, near_ref, far_ref, out_ref):
    code = code_of(pl.program_id(0), own_ref[0])
    block = jnp.where((code & 2) == 0, near_ref[...], far_ref[...])
    out_ref[...] = block.T.astype(out_ref.dtype)


def stack_pieces(near, far, own, transposed):
    tall = near.shape[0] // 4
    cols = near.shape[1]
    spec = pl.BlockSpec((tall, cols), lambda i, own: (piece_of(code_of(i, own[0])), 0))
    return pl.pallas_call(
        stack_kernel_t if transposed else stack_kernel,
        grid_spec=pltpu.PrefetchScalarGridSpec(
            num_scalar_prefetch=1,
            grid=(8,),
            in_specs=[spec, spec],
            out_specs=pl.BlockSpec((cols, tall), lambda i, own: (0, i))
            if transposed
            else pl.BlockSpec((tall, cols), lambda i, own: (i, 0)),
        ),
        out_shape=jax.ShapeDtypeStruct((cols, 8 * tall) if transposed else (8 * tall, cols), jnp.float32),
        compiler_params=settings(),
        cost_estimate=light(),
        name="stack_pieces",
    )(own, near, far)


def stack_heads_kernel(flips, own_ref, near_low, far_low, near_high, far_high, *outs):
    code = code_of(2 * pl.program_id(0), own_ref[0])
    take_near = (code & 2) == 0
    low = jnp.where(take_near, near_low[...], far_low[...])
    high = jnp.where(take_near, near_high[...], far_high[...])
    for index, ref in enumerate(outs):
        at = slice(index * HEAD_DIM, (index + 1) * HEAD_DIM)
        both = jnp.concatenate([low[at], high[at]], axis=0)
        ref[...] = (both.T if flips[index] else both).astype(ref.dtype)


def stack_heads(near, far, own, flips):
    tall = near.shape[0] // 4
    cols = near.shape[1]
    low = pl.BlockSpec((tall, cols), lambda i, own: (piece_of(code_of(2 * i, own[0])), 0))
    high = pl.BlockSpec((tall, cols), lambda i, own: (piece_of(code_of(2 * i + 1, own[0])), 0))
    column = pl.BlockSpec((cols, 128), lambda i, own: (0, i))
    row = pl.BlockSpec((128, cols), lambda i, own: (i, 0))
    tall_out = jax.ShapeDtypeStruct((cols, 512), jnp.float32)
    flat_out = jax.ShapeDtypeStruct((512, cols), jnp.float32)
    return pl.pallas_call(
        functools.partial(stack_heads_kernel, flips),
        grid_spec=pltpu.PrefetchScalarGridSpec(
            num_scalar_prefetch=1,
            grid=(4,),
            in_specs=[low, low, high, high],
            out_specs=[column if flip else row for flip in flips],
        ),
        out_shape=[tall_out if flip else flat_out for flip in flips],
        compiler_params=settings(),
        cost_estimate=light(),
        name="stack_heads",
    )(own, near, far, near, far)


def add_rows_kernel(*refs):
    total = refs[0][...].astype(jnp.float32)
    for ref in refs[1:-1]:
        total = total + ref[...].astype(jnp.float32)
    refs[-1][...] = total.astype(refs[-1].dtype)


def add_pieces(near, got, moved, index):
    tall = near.shape[0] // 4
    cols = near.shape[1]
    at = pl.BlockSpec((tall, cols), lambda i: (index, 0))
    return pl.pallas_call(
        add_rows_kernel,
        grid=(1,),
        in_specs=[at, at] + [whole((tall, cols))] * len(moved),
        out_specs=whole((tall, cols)),
        out_shape=jax.ShapeDtypeStruct((tall, cols), near.dtype),
        compiler_params=settings(),
        cost_estimate=light(),
        name="add_pieces",
    )(near, got, *moved)


def add_rows(near, got, index):
    return add_pieces(near, got, (), index)


def add_three(near, got, moved, index):
    return add_pieces(near, got, (moved,), index)


def add_four(near, got, first, second, index):
    return add_pieces(near, got, (first, second), index)


def partial_three_kernel(query_ref, key_ref, value_ref, weight_ref, near_ref, far_ref):
    rows = near_ref.shape[0]
    depth = query_ref.shape[1]
    for at, out in ((pl.ds(rows, rows), far_ref), (pl.ds(0, rows), near_ref)):
        total = nn_dot(query_ref[at, :], weight_ref[pl.ds(0, depth), :])
        total = total + nn_dot(key_ref[at, :], weight_ref[pl.ds(depth, depth), :])
        total = total + nn_dot(value_ref[at, :], weight_ref[pl.ds(2 * depth, depth), :])
        out[...] = total.astype(out.dtype)


def partial_three(query, key, value, weight):
    rows, depth = query.shape
    cols = weight.shape[1]
    half = rows // 2
    return pl.pallas_call(
        partial_three_kernel,
        grid=(cols // WIDE,),
        in_specs=[whole((rows, depth))] * 3 + [pl.BlockSpec((3 * depth, WIDE), lambda i: (0, i))],
        out_specs=[pl.BlockSpec((half, WIDE), lambda i: (0, i))] * 2,
        out_shape=[
            jax.ShapeDtypeStruct((half, cols), jnp.float32),
            jax.ShapeDtypeStruct((half, cols), jnp.bfloat16),
        ],
        compiler_params=settings(),
        cost_estimate=light(),
        name="partial_three",
    )(query, key, value, weight)


def rows_call(kernel, name, grid_rows, ins, outs, sums=0):
    tall = 128
    cols = 2048
    steps = grid_rows // tall

    def spec(array, first):
        if first is None:
            return pl.BlockSpec(array.shape, lambda i: (0, 0))
        return pl.BlockSpec((tall, cols), lambda i: (first * steps + i, 0))

    out_specs = [pl.BlockSpec((tall, cols), lambda i: (i, 0)) for _ in outs]
    out_shape = [jax.ShapeDtypeStruct((grid_rows, cols), kind) for kind in outs]
    if sums:
        out_specs.append(pl.BlockSpec((8, cols), lambda i: (0, 0)))
        out_shape.append(jax.ShapeDtypeStruct((8, cols), jnp.float32))
    return pl.pallas_call(
        kernel,
        grid=(steps,),
        in_specs=[spec(array, first) for array, first in ins],
        out_specs=out_specs,
        out_shape=out_shape,
        compiler_params=settings(),
        cost_estimate=light(),
        name=name,
    )(*[array for array, _ in ins])


def wide(ref):
    return ref[...].astype(jnp.float32)


def norm_in_kernel(rows_ref, gain_ref, shift_ref, out_ref):
    normed, _ = normalize(wide(rows_ref))
    out_ref[...] = (normed * gain_ref[...] + shift_ref[...]).astype(out_ref.dtype)


def norm_in(tok, m, gain, shift_by):
    return rows_call(
        norm_in_kernel, "norm_in", tok.shape[0] // 2, [(tok, m), (gain, None), (shift_by, None)], [jnp.bfloat16]
    )[0]


def resid_kernel(rows_ref, kept_ref, got_ref, bias_ref, gain_ref, shift_ref, resid_ref, out_ref):
    resid = wide(rows_ref) + kept_ref[...] + wide(got_ref) + bias_ref[...]
    resid_ref[...] = resid
    normed, _ = normalize(resid.astype(jnp.bfloat16).astype(jnp.float32))
    out_ref[...] = (normed * gain_ref[...] + shift_ref[...]).astype(out_ref.dtype)


def resid_norm(tok, m, kept, got, bias, gain, shift_by):
    ins = [(tok, m), (kept, 0), (got, 0), (bias, None), (gain, None), (shift_by, None)]
    return rows_call(resid_kernel, "resid_norm", kept.shape[0], ins, [jnp.float32, jnp.bfloat16])


def layer_kernel(resid_ref, kept_ref, got_ref, bias_ref, out_ref):
    out_ref[...] = (resid_ref[...] + kept_ref[...] + wide(got_ref) + bias_ref[...]).astype(out_ref.dtype)


def layer_rows_of(resid, kept, got, bias):
    ins = [(resid, 0), (kept, 0), (got, 0), (bias, None)]
    return rows_call(layer_kernel, "layer_rows", kept.shape[0], ins, [jnp.bfloat16])[0]


def add_sums(sums_ref, parts):
    @pl.when(pl.program_id(0) == 0)
    def _():
        sums_ref[...] = jnp.zeros_like(sums_ref)

    for index, part in enumerate(parts):
        sums_ref[index : index + 1, :] += jnp.sum(part, axis=0, keepdims=True)


def norm_back_rows(grad, normed, inverse, gain):
    scaled = grad * gain
    first_mean = jnp.mean(scaled, axis=1, keepdims=True)
    second_mean = jnp.mean(scaled * normed, axis=1, keepdims=True)
    return inverse * (scaled - first_mean - normed * second_mean)


def second_back_kernel(kept_ref, got_ref, resid_ref, cot_ref, gain_ref, grad_ref, low_ref, sums_ref):
    grad = (kept_ref[...] + wide(got_ref)).astype(jnp.bfloat16).astype(jnp.float32)
    normed, inverse = normalize(resid_ref[...].astype(jnp.bfloat16).astype(jnp.float32))
    cot = wide(cot_ref)
    total = cot + norm_back_rows(grad, normed, inverse, gain_ref[...])
    grad_ref[...] = total
    low_ref[...] = total.astype(low_ref.dtype)
    add_sums(sums_ref, (total, cot, grad * normed, grad))


def second_back_rows(kept, got, resid, cot, m, gain):
    ins = [(kept, 0), (got, 0), (resid, 0), (cot, m), (gain, None)]
    return rows_call(second_back_kernel, "second_back", kept.shape[0], ins, [jnp.float32, jnp.bfloat16], sums=4)


def first_back_kernel(kept_ref, got_ref, rows_ref, resid_grad_ref, gain_ref, out_ref, sums_ref):
    grad = (kept_ref[...] + wide(got_ref)).astype(jnp.bfloat16).astype(jnp.float32)
    normed, inverse = normalize(wide(rows_ref))
    back = norm_back_rows(grad, normed, inverse, gain_ref[...])
    out_ref[...] = (resid_grad_ref[...] + back).astype(out_ref.dtype)
    add_sums(sums_ref, (grad * normed, grad))


def first_back_rows(kept, got, tok, m, resid_grad, gain):
    ins = [(kept, 0), (got, 0), (tok, m), (resid_grad, 0), (gain, None)]
    return rows_call(first_back_kernel, "first_back", kept.shape[0], ins, [jnp.bfloat16], sums=2)


def middle_kernel(near_top, near_low, got_top, got_low, kept_ref, moving_ref):
    kept_ref[...] = near_top[...] + wide(got_top)
    moving_ref[...] = (near_low[...] + wide(got_low)).astype(moving_ref.dtype)


def middle_rows(near, got):
    ins = [(near, 0), (near, 1), (got, 0), (got, 1)]
    return rows_call(middle_kernel, "middle_rows", near.shape[0] // 2, ins, [jnp.float32, jnp.bfloat16])


def join_kernel(count, *refs):
    sources, out_ref = refs[:count], refs[count]
    offset = 0
    for source in sources:
        rows = source.shape[0]
        out_ref[pl.ds(offset, rows), :] = source[...]
        offset += rows


def join_rows(arrays):
    count = len(arrays)
    rows = sum(array.shape[0] for array in arrays)
    cols = arrays[0].shape[1]
    chunk = cols // 4
    return pl.pallas_call(
        functools.partial(join_kernel, count),
        grid=(4,),
        in_specs=[pl.BlockSpec((array.shape[0], chunk), lambda i: (0, i)) for array in arrays],
        out_specs=pl.BlockSpec((rows, chunk), lambda i: (0, i)),
        out_shape=jax.ShapeDtypeStruct((rows, cols), arrays[0].dtype),
        compiler_params=settings(),
        cost_estimate=light(),
        name="join_rows",
    )(*arrays)


def attn_join_kernel(count, *refs):
    sources, qkv_ref, out_w_ref, bias_ref = refs[:count], *refs[count:]
    rows = HEAD_DIM
    for index, source in enumerate(sources):
        for k in range(3):
            qkv_ref[pl.ds((k * count + index) * rows, rows), :] = source[pl.ds(k * rows, rows), :]
        out_w_ref[pl.ds(index * rows, rows), :] = source[pl.ds(3 * rows, rows), :]
        bias_ref[pl.ds(index * 8, 8), :] = source[pl.ds(4 * rows, 8), :]


def attn_join(arrays):
    count = len(arrays)
    cols = arrays[0].shape[1]
    kind = arrays[0].dtype
    chunk = cols // 4
    sizes = (3 * count * HEAD_DIM, count * HEAD_DIM, count * 8)
    return pl.pallas_call(
        functools.partial(attn_join_kernel, count),
        grid=(4,),
        in_specs=[pl.BlockSpec((array.shape[0], chunk), lambda i: (0, i)) for array in arrays],
        out_specs=[pl.BlockSpec((size, chunk), lambda i: (0, i)) for size in sizes],
        out_shape=[jax.ShapeDtypeStruct((size, cols), kind) for size in sizes],
        compiler_params=settings(),
        cost_estimate=light(),
        name="attn_join",
    )(*arrays)


def cross_pair_kernel(rights, *refs):
    out_ref = refs[-1]
    lefts, right_refs = refs[:4], refs[4:-1]
    for which in range(2):
        right = right_refs[:4] if rights == 1 or which == 0 else right_refs[4:]
        near_a, far_a, near_b, far_b = right
        left_a, left_b = lefts[2 * which], lefts[2 * which + 1]
        rows = near_a.shape[0]
        top, low = pl.ds(0, rows), pl.ds(rows, rows)
        total = tn_dot(left_a[top, :], near_a[...]) + tn_dot(left_a[low, :], far_a[...])
        total = total + tn_dot(left_b[top, :], near_b[...]) + tn_dot(left_b[low, :], far_b[...])
        total = total.astype(out_ref.dtype)
        for piece in range(total.shape[0] // HEAD_DIM):
            at = pl.ds((2 * piece + which) * HEAD_DIM, HEAD_DIM)
            out_ref[at, :] = total[piece * HEAD_DIM : (piece + 1) * HEAD_DIM, :]


def cross_pair(first, second, rights, half):
    rows = first[0].shape[0]
    cols = rights[0][0].shape[1]
    tall = first[0].shape[1] // 2
    wide_cols = 1024
    left_spec = pl.BlockSpec((rows, tall), lambda i: (0, half))
    right_spec = pl.BlockSpec((rows // 2, wide_cols), lambda i: (0, i))
    flat = [array for right in rights for array in right]
    return pl.pallas_call(
        functools.partial(cross_pair_kernel, len(rights)),
        grid=(cols // wide_cols,),
        in_specs=[left_spec] * 4 + [right_spec] * len(flat),
        out_specs=pl.BlockSpec((2 * tall, wide_cols), lambda i: (0, i)),
        out_shape=jax.ShapeDtypeStruct((2 * tall, cols), jnp.bfloat16),
        compiler_params=settings(),
        cost_estimate=light(),
        name="cross_pair",
    )(*first, *second, *flat)


SWAP = [(0, 1), (1, 0)]
PLANE = ("y", "x", "core")
EVERY = ("z", "y", "x", "core")
MICRO = 2
SLOTS = 72


def after(value, *others):
    return lax.optimization_barrier((value, *others))[0]


class Order:

    def __init__(self):
        self.last = ()

    def take(self, value):
        return lax.optimization_barrier((value, self.last))[0]

    def mark(self, value):
        self.last = value
        return value

    def step(self, value):
        return self.mark(self.take(value))


def swap_along(array, axis):
    return lax.ppermute(array, axis, SWAP)


def shift(array, step):
    size = lax.axis_size("z")
    return lax.ppermute(array, "z", [(i, (i + step) % size) for i in range(size)])


def joined(arrays):
    return jnp.concatenate(arrays, axis=0)


def plane_start(piece):
    return (piece, swap_along(piece, "x"), swap_along(piece, "y"))


def plane_middle(started, order):
    piece, by_x, by_y = started
    half = piece.shape[0] // 2
    by_x, by_y = order.step((by_x, by_y))
    return (piece, by_x, by_y, swap_along(by_y[:half], "x"), swap_along(by_x[half:], "y"))


def plane_end(started, order):
    piece, by_x, by_y, corner_top, corner_low = started
    near = order.mark(join_rows([piece, by_x, by_y, *order.take((corner_top, corner_low))]))
    return (near, swap_along(near, "core"))


def held_before(bound, residue, parts):
    return (bound + (parts - 1) - residue) // parts


def piece_tables(lengths, starts, quarter_low, quarter_rows, residue, parts):
    ends = running_sum(lengths)
    firsts = ends - lengths
    shift = starts - firsts
    low = jnp.maximum(firsts, quarter_low)
    high = jnp.minimum(ends, quarter_low + quarter_rows)
    begin = held_before(low + shift, residue, parts)
    count = jnp.where(high > low, held_before(high + shift, residue, parts) - begin, 0)
    return (begin, count, shift)


def slot_lookup(begin, count, value_of):
    base = running_sum(count) - count
    slot = jnp.arange(SLOTS, dtype=jnp.int32)
    inside = (slot >= base[..., None]) & (slot < (base + count)[..., None])
    held = begin[..., None] + slot - base[..., None]
    return jnp.sum(jnp.where(inside, value_of(held) + 1, 0), axis=-2, dtype=jnp.int32) - 1


def layer(
    tokens,
    cotangent,
    lengths,
    dealing,
    query_weight,
    key_weight,
    value_weight,
    out_weight,
    query_bias,
    value_bias,
    out_bias,
    up_weight,
    up_bias,
    down_weight,
    down_bias,
    attn_gain,
    attn_shift,
    mlp_gain,
    mlp_shift,
):
    tok_rows = tokens.shape[1]
    col_width = tokens.shape[2]
    width = out_weight.shape[1]
    seq_dev = lengths.shape[2]
    depth = lax.axis_size("z")
    parts = lax.axis_size("y") * 4
    own_rows = tok_rows // 4
    y, x, core, z = (lax.axis_index(name) for name in ("y", "x", "core", "z"))
    team = 2 * x + core
    eighth = 2 * team + y
    residue = 4 * y + team
    group = 2 * z + y

    given_off = []
    for micro_step in range(MICRO):
        given_off.append(given_layout(lengths[micro_step], dealing[micro_step])[2])
    starts = jnp.stack(given_off).reshape(lengths.shape)
    quarter_low = (jnp.arange(4, dtype=jnp.int32) * own_rows)[None, None, :, None]
    begin, count, _ = piece_tables(
        lengths[:, :, None, :], starts[:, :, None, :], quarter_low, own_rows, residue, parts
    )
    micro_ids = jnp.arange(MICRO, dtype=jnp.int32)[:, None, None, None]
    begin = jnp.transpose(begin + micro_ids * tok_rows, (1, 2, 0, 3)).reshape(-1, MICRO * seq_dev)
    count = jnp.transpose(count, (1, 2, 0, 3)).reshape(-1, MICRO * seq_dev)
    send_row = slot_lookup(begin, count, lambda held: held).reshape(-1)

    my_lengths = lax.dynamic_index_in_dim(lengths, group, 1, keepdims=False)
    my_starts = lax.dynamic_index_in_dim(starts, group, 1, keepdims=False)
    residues = jnp.arange(parts, dtype=jnp.int32)[:, None, None]
    my_begin, my_count, my_shift = piece_tables(
        my_lengths[None], my_starts[None], team * own_rows, own_rows, residues, parts
    )
    flat = (parts, MICRO * seq_dev)
    row_shift = (
        my_shift + team * own_rows - jnp.arange(MICRO, dtype=jnp.int32)[None, :, None] * own_rows
    )
    row_shift = jnp.broadcast_to(row_shift, my_count.shape).reshape(flat)
    own_row = slot_lookup(
        my_begin.reshape(flat),
        my_count.reshape(flat),
        lambda held: held * parts + residues - row_shift[..., None],
    ).reshape(-1)
    head_rows = HEAD_DIM
    half_units = up_weight.shape[1] // 8

    shard_heads = query_weight.shape[1]

    def bias_rows(half):
        row = jnp.concatenate(
            [
                lax.dynamic_slice_in_dim(bias, (2 * team + half) * size, size)
                for bias, size in ((query_bias, HEAD_DIM), (value_bias, HEAD_DIM), (up_bias, half_units))
            ]
        )
        return jnp.pad(row[None, :], ((0, 7), (0, width - row.shape[0])))

    attn_mine, attn_other = attn_pack(
        query_weight, key_weight, value_weight, out_weight, bias_rows(y), bias_rows(1 - y), team, y
    )
    blocks = half_units // 128
    up_mine = flipped(up_weight, (2 * team + y) * blocks, blocks)
    up_other = flipped(up_weight, (2 * team + 1 - y) * blocks, blocks)
    down_mine = lax.dynamic_slice_in_dim(down_weight, (2 * team + y) * half_units, half_units, 0)
    down_other = lax.dynamic_slice_in_dim(down_weight, (2 * team + 1 - y) * half_units, half_units, 0)

    order = Order()

    def spread_out(array):
        spread = array.reshape(MICRO, tok_rows // parts, parts, col_width)
        spread = lax.all_to_all(spread, PLANE, split_axis=2, concat_axis=1, tiled=True)
        return spread.reshape(MICRO * tok_rows, col_width)

    def box_exchange(sent):
        return lax.all_to_all(sent, EVERY, split_axis=0, concat_axis=0, tiled=True)

    def boxes(spread):
        return pick_rows(send_row, spread, 384)

    def settle(got):
        return settle_rows(own_row, got.reshape(depth, parts * SLOTS, col_width), MICRO * own_rows)

    gain_one, shift_one, gain_two, shift_two, out_b, down_b = (
        array.astype(jnp.float32)[None, :]
        for array in (attn_gain, attn_shift, mlp_gain, mlp_shift, out_bias, down_bias)
    )

    rank = jnp.full((1,), team, jnp.int32)
    infos = []
    for micro_step in range(MICRO):
        holder, position, _ = buffer_layout(my_lengths[micro_step], my_starts[micro_step], tok_rows)
        segment = holder * tok_rows + position // (SEG + SUMM)
        summary = jnp.where(position % (SEG + SUMM) >= SEG, holder, -1)
        infos.append((jnp.stack([segment, summary], axis=1), jnp.stack([segment, holder], axis=0)))

    def up_down(piece):
        piece = order.take(piece)
        return (shift(piece, 1), shift(piece, -1))

    def onward(piece):
        piece = order.step(piece)
        return (piece, shift(piece, 1), swap_along(piece, "y"))

    def swapped(piece):
        piece = order.step(piece)
        return (piece, swap_along(piece, "y"))

    def team_start(rows):
        return (rows, swap_along(rows, "x"))

    def team_middle(started):
        own, by_x = started
        near = order.mark(join_rows([own, order.take(by_x)]))
        return (near, swap_along(near, "core"))

    def team_end(started):
        near, far = started
        return (near, order.step(far))

    def sum_start(left, weight):
        near, far = order.mark(partial_sums(order.take(left), weight))
        return (near, swap_along(far, "core"))

    def sum_middle(started):
        near, got = started
        kept, moving = order.mark(middle_rows(near, order.take(got)))
        return (kept, swap_along(moving, "x"))

    def sum_end(started):
        kept, got = started
        return (kept, order.take(got))

    def unsettle(array):
        return unsettle_rows(own_row, array, depth).reshape(-1, col_width)

    def unbox(got):
        return drop_rows(send_row, got, MICRO * tok_rows, 256)

    def spread_back(held):
        held = held.reshape(MICRO, tok_rows, 1, col_width)
        back = lax.all_to_all(held, PLANE, split_axis=1, concat_axis=2, tiled=True)
        return back.reshape(MICRO, tok_rows, col_width)

    order.mark(attn_mine)
    attn_1 = shift(attn_mine, 1)
    tok_spread = spread_out(tokens)
    attn_1 = order.step(attn_1)
    attn_2 = shift(attn_1, 1)
    attn_y1 = swap_along(attn_1, "y")
    tok_spread = order.step(tok_spread)
    attn_2 = order.step(attn_2)
    attn_3 = shift(order.take(attn_mine), -1)
    attn_y2 = swap_along(attn_2, "y")
    tok_sent = order.mark(boxes(order.take(tok_spread)))
    tok_got = box_exchange(tok_sent)
    attn_3, attn_y3 = swapped(attn_3)
    tok = order.mark(settle(order.take(tok_got)))
    up_1, up_3 = up_down(up_mine)
    cot_spread = spread_out(after(cotangent, tok))

    first_a = team_start(order.mark(norm_in(tok, 0, gain_one, shift_one)))
    first_b = team_start(order.mark(norm_in(order.take(tok), 1, gain_one, shift_one)))
    attn_all = [attn_mine, attn_1, attn_2, attn_3, attn_other, *order.take((attn_y1, attn_y2, attn_y3))]
    qkv_w, out_w, bias_w = order.mark(attn_join(attn_all))
    bias_w = bias_w.reshape(2 * depth, 8, width)[:, 0, :].astype(jnp.float32)
    query_b = bias_w[:, :head_rows].reshape(1, -1)
    value_b = bias_w[:, head_rows : 2 * head_rows].reshape(1, -1)
    up_b = bias_w[:, 2 * head_rows : 2 * head_rows + half_units].reshape(1, -1)
    qkv_b = jnp.concatenate([query_b, jnp.zeros_like(query_b), value_b], axis=1)
    no_b = jnp.zeros((1, out_w.shape[0]), jnp.float32)

    first_a = team_middle(first_a)
    cot_sent = order.mark(boxes(order.take(cot_spread)))
    first_a = team_end(first_a)
    up_1, up_2, up_y1 = onward(up_1)
    up_3, up_y3 = swapped(up_3)
    qkv_a = order.mark(project(*order.take(first_a), qkv_w, qkv_b))
    mixed_a = order.mark(attend(order.take(qkv_a), rank, *infos[0]))
    up_y1 = order.step(up_y1)
    up_2, up_y2 = swapped(up_2)
    down_1, down_3 = up_down(down_mine)
    first_b = team_middle(first_b)
    sum_a1 = sum_start(mixed_a, out_w)
    first_b = team_end(first_b)
    qkv_b_ = order.mark(project(*order.take(first_b), qkv_w, qkv_b))
    up_y3 = order.step(up_y3)
    sum_a1 = sum_middle(sum_a1)
    mixed_b = order.mark(attend(order.take(qkv_b_), rank, *infos[1]))
    up_y2 = order.step(up_y2)
    down_1, down_2, down_y1 = onward(down_1)
    resid_a, second_a = order.mark(resid_norm(tok, 0, *sum_end(sum_a1), out_b, gain_two, shift_two))
    second_a = team_start(second_a)
    down_3, down_y3 = swapped(down_3)
    cot_got = box_exchange(order.take(cot_sent))
    sum_b1 = sum_start(mixed_b, out_w)
    up_w = order.mark(join_rows([up_mine, up_1, up_2, up_3, up_other, *order.take((up_y1, up_y2, up_y3))]))
    sum_b1 = sum_middle(sum_b1)
    down_y1 = order.step(down_y1)
    second_a = team_end(team_middle(second_a))

    hidden_a, slope_a = order.mark(expand(*order.take(second_a), up_w, up_b))
    down_2, down_y2 = swapped(down_2)
    down_y3 = order.step(down_y3)
    resid_b, second_b = order.mark(resid_norm(tok, 1, *sum_end(sum_b1), out_b, gain_two, shift_two))
    second_b = team_start(second_b)
    cot = order.mark(settle(order.take(cot_got)))
    cot_own = cot.reshape(MICRO, own_rows, width)
    second_b = team_middle(second_b)
    cot_parts = [team_start(cot_own[m]) for m in range(MICRO)]
    second_b = team_end(second_b)
    hidden_b, slope_b = order.mark(expand(*order.take(second_b), up_w, up_b))
    down_w = order.mark(
        join_rows([down_mine, down_1, down_2, down_3, down_other, *order.take((down_y1, down_y2, down_y3))])
    )
    sum_a4 = sum_start(hidden_a, down_w)
    cot_parts[0] = team_middle(cot_parts[0])
    sum_b4 = sum_start(hidden_b, down_w)
    cot_a = team_end(cot_parts[0])

    low_a, up_sum_a = order.mark(expand_back(*order.take(cot_a), down_w, slope_a))
    cot_parts[1] = team_middle(cot_parts[1])
    sum_a2 = sum_start(low_a, up_w)
    cot_b = team_end(cot_parts[1])
    low_b, up_sum_b = order.mark(expand_back(*order.take(cot_b), down_w, slope_b))
    up_sum_a, up_sum_b = up_sum_a[0], up_sum_b[0]
    sum_a2 = sum_middle(sum_a2)
    sum_b2 = sum_start(low_b, up_w)

    def cross_half(left_a, right_a, left_b, right_b, half):
        size = left_a.shape[1] // 2
        return order.mark(cross_sums(order.take(left_a), right_a, left_b, right_b, half * size, size))

    down_far = cross_half(hidden_a, cot_a, hidden_b, cot_b, 1)
    down_swap = swap_along(down_far, "y")
    sum_b2 = sum_middle(sum_b2)

    def second_back(started, resid, m):
        return order.mark(second_back_rows(*sum_end(started), resid, cot, m, gain_two))

    resid_grad_a, attn_low_a, norm_sums_a = second_back(sum_a2, resid_a, 0)
    attn_low_a = team_start(attn_low_a)
    down_near = cross_half(hidden_a, cot_a, hidden_b, cot_b, 0)
    resid_grad_b, attn_low_b, norm_sums_b = second_back(sum_b2, resid_b, 1)
    attn_low_b = team_start(attn_low_b)
    sum_a4 = sum_middle(sum_a4)
    up_far = cross_half(low_a, second_a, low_b, second_b, 1)
    attn_low_a = team_middle(attn_low_a)
    sum_b4 = sum_middle(sum_b4)
    attn_low_a = team_end(attn_low_a)

    def ring_start(near, got):
        got = order.take(got)
        far_2 = order.mark(add_rows(near, got, 2))
        move = shift(far_2, 1)
        far_1 = order.mark(add_rows(near, order.take(got), 1))
        back = shift(far_1, -1)
        return (near, got, move, back)

    def ring_middle(started):
        near, got, move, back = started
        far_3 = order.mark(add_three(near, got, order.take(move), 3))
        return (near, got, shift(far_3, 1), back)

    def ring_end(started):
        near, got, move, back = started
        move, back = order.take((move, back))
        return order.mark(add_four(near, got, move, back, 0))

    def attn_back(attn_low, qkv, m):
        mixed_grad = order.mark(project(*order.take(attn_low), out_w, no_b))
        return order.mark(attend_back(qkv, order.take(mixed_grad), rank, *infos[m]))

    def sum_start_three(lefts, weight):
        near, far = order.mark(partial_three(*order.take(lefts), weight))
        return (near, swap_along(far, "core"))

    *lows_a, sums_a = attn_back(attn_low_a, qkv_a, 0)
    attn_low_b = team_middle(attn_low_b)
    down_ring = ring_start(down_near, down_swap)
    up_swap = swap_along(order.take(up_far), "y")
    sum_a3 = sum_start_three(lows_a, qkv_w)
    attn_low_b = team_end(attn_low_b)
    up_near = cross_half(low_a, second_a, low_b, second_b, 0)
    sum_a3 = sum_middle(sum_a3)
    layer_a = order.mark(layer_rows_of(resid_a, *sum_end(sum_a4), down_b))
    layer_b = order.mark(layer_rows_of(resid_b, *sum_end(sum_b4), down_b))
    layer_sent = order.mark(unsettle(join_rows([layer_a, layer_b])))
    down_ring = ring_middle(down_ring)
    layer_got = box_exchange(order.take(layer_sent))

    def pack_small():
        slots = jnp.arange(8 * depth, dtype=jnp.int32)
        index = jnp.arange(2 * depth, dtype=jnp.int32)
        owner = lax.rem(z - index % depth + depth, depth)
        flip = jnp.where(index < depth, y, 1 - y)
        hot = (slots[:, None] == (owner * 8 + 2 * team + flip)[None, :]).astype(jnp.float32)

        def place(vector):
            local = vector.reshape(2 * depth, -1)
            return jnp.dot(hot, local, precision=lax.Precision.HIGHEST).reshape(-1)

        head_sums = sums_a + sums_b
        norm_sums = norm_sums_a + norm_sums_b
        back_sums = back_sums_a + back_sums_b
        return jnp.concatenate(
            [
                place(head_sums[0]),
                place(head_sums[1]),
                place(up_sum_a + up_sum_b),
                norm_sums[:4].reshape(-1),
                back_sums[:2].reshape(-1),
            ]
        ).reshape(-1, 128)

    def ring_start(near, got):
        piece = near.shape[0] // depth
        got = order.take(got)
        far_2 = order.mark(add_rows(near, got, 2))
        move = shift(far_2, 1)
        far_1 = order.mark(add_rows(near, order.take(got), 1))
        back = shift(far_1, -1)
        return (near, got, move, back)

    def ring_middle(started):
        near, got, move, back = started
        far_3 = order.mark(add_three(near, got, order.take(move), 3))
        return (near, got, shift(far_3, 1), back)

    def ring_end(started):
        near, got, move, back = started
        move, back = order.take((move, back))
        return order.mark(add_four(near, got, move, back, 0))

    *lows_b, sums_b = attn_back(attn_low_b, qkv_b_, 1)
    def first_back(started, resid_grad, m):
        return order.mark(first_back_rows(*sum_end(started), tok, m, resid_grad, gain_one))

    firsts = (*first_a, *first_b)

    def one_half(half):
        lefts = order.take((lows_a[0], lows_b[0]))
        return order.mark(cross_pair(lefts, (lows_a[1], lows_b[1]), (firsts,), half))

    def two_half(half):
        lefts = order.take((lows_a[2], lows_b[2]))
        rights = (firsts, (*attn_low_a, *attn_low_b))
        return order.mark(cross_pair(lefts, (mixed_a, mixed_b), rights, half))

    input_a, back_sums_a = first_back(sum_a3, resid_grad_a, 0)
    up_ring = ring_start(up_near, up_swap)
    sum_b3 = sum_start_three(lows_b, qkv_w)
    one_far = one_half(1)
    one_swap = swap_along(one_far, "y")
    sum_b3 = sum_middle(sum_b3)
    two_far = two_half(1)
    two_swap = swap_along(two_far, "y")
    down_total = ring_end(down_ring)
    down_plane = plane_start(down_total)
    layer_held = order.mark(unbox(order.take(layer_got)))
    layer_out = spread_back(layer_held)
    one_near = one_half(0)
    up_ring = ring_middle(up_ring)
    input_b, back_sums_b = first_back(sum_b3, resid_grad_b, 1)
    input_sent = order.mark(unsettle(join_rows([input_a, input_b])))
    one_ring = ring_start(one_near, one_swap)
    layer_out = order.step(layer_out)
    input_got = box_exchange(order.take(input_sent))
    two_near = two_half(0)
    up_total = ring_end(up_ring)
    up_plane = plane_start(up_total)
    one_ring = ring_middle(one_ring)
    two_ring = ring_start(two_near, two_swap)
    down_plane = plane_middle(down_plane, order)
    small = order.mark(order.take(pack_small()))
    small_got = swap_along(small, "core")
    one_total = ring_end(one_ring)
    one_plane = plane_start(one_total)
    two_ring = ring_middle(two_ring)
    small = order.mark(small + order.take(small_got))
    small_got = swap_along(small, "x")
    down_plane = plane_end(down_plane, order)
    own = jnp.full((1,), eighth, jnp.int32)
    up_plane = plane_middle(up_plane, order)
    input_held = order.mark(unbox(order.take(input_got)))
    input_grad = spread_back(input_held)
    down_grad = order.mark(stack_pieces(*order.take(down_plane), own, False))
    two_total = ring_end(two_ring)
    two_plane = plane_start(two_total)
    small = order.mark(small + order.take(small_got))
    small_got = swap_along(small, "y")
    up_plane = plane_end(up_plane, order)
    one_plane = plane_middle(one_plane, order)
    up_grad = order.mark(stack_pieces(*order.take(up_plane), own, True))
    one_plane = plane_end(one_plane, order)
    small = order.mark(small + order.take(small_got))
    small_got = lax.ppermute(small, "z", [(i, i ^ 1) for i in range(depth)])
    two_plane = plane_middle(two_plane, order)
    input_grad = order.step(input_grad)
    query_grad, key_grad = order.mark(stack_heads(*order.take(one_plane), own, (True, True)))
    two_plane = plane_end(two_plane, order)
    small = order.mark(small + order.take(small_got))
    small_got = lax.ppermute(small, "z", [(i, i ^ 2) for i in range(depth)])
    value_grad, out_w_grad = order.mark(stack_heads(*order.take(two_plane), own, (True, False)))
    packed = small + order.take(small_got)
    packed = packed.reshape(-1)
    pieces = []
    offset = 0
    heads_all = depth * shard_heads
    for size in (heads_all, heads_all, depth * up_weight.shape[1]) + (width,) * 6:
        pieces.append(packed[offset : offset + size])
        offset += size
    query_b_grad, value_b_grad, up_b_grad, out_b_grad, down_b_grad, gain_two_g, shift_two_g, *norm_grads = pieces
    norm_grads = norm_grads + [gain_two_g, shift_two_g]

    def own_shard(vector):
        size = vector.shape[0] // depth
        return lax.dynamic_slice_in_dim(vector, z * size, size)

    return (
        layer_out,
        input_grad,
        query_grad,
        key_grad,
        value_grad,
        out_w_grad,
        own_shard(query_b_grad),
        own_shard(value_b_grad),
        out_b_grad,
        up_grad,
        own_shard(up_b_grad),
        down_grad,
        down_b_grad,
        *norm_grads,
    )


def team_layer(mesh):
    axes = ("y", "x", "core", "z")
    inner = Mesh(mesh.devices.reshape(2, 2, 2, 4), axes)
    rows = P(None, PLANE, "z")
    in_specs = (
        rows, rows, P(), P(), P(None, "z"), P(None, "z"), P(None, "z"), P("z", None), P("z"), P("z"),
        P(), P(None, "z"), P("z"), P("z", None), P(), P(), P(), P(), P(),
    )
    out_specs = (
        rows, rows, P(None, "z"), P(None, "z"), P(None, "z"), P("z", None), P("z"), P("z"),
        P(), P(None, "z"), P("z"), P("z", None), P(), P(), P(), P(), P(),
    )
    return jax.shard_map(layer, mesh=inner, in_specs=in_specs, out_specs=out_specs, check_vma=False)


def solution(mesh):
    if dict(mesh.shape) == {"dp": 8, "tensor": 4}:
        return team_layer(mesh)
    return general_layer(mesh)
```

```python
import functools

import jax
import jax.numpy as jnp
from jax import lax
from jax.experimental import pallas as pl
from jax.experimental.pallas import tpu as pltpu
from jax.sharding import Mesh
from jax.sharding import PartitionSpec as P


HEAD_DIM = 64
SEG = 512
SUMM = 50
NBLK = 2


NORM_EPS = 1e-05
MASKED = -1e30


def gelu_tanh(values):
    return jax.nn.gelu(values, approximate=True)


def matmul(left_array, right_array):
    return jnp.dot(left_array, right_array, preferred_element_type=jnp.float32)


def cross_rows(left_array, right_array):
    return lax.dot_general(
        left_array, right_array, (((0,), (0,)), ((), ())), preferred_element_type=jnp.float32
    )


def times_transpose(left_array, right_array):
    return lax.dot_general(
        left_array, right_array, (((1,), (1,)), ((), ())), preferred_element_type=jnp.float32
    )


def normalize(values):
    center = jnp.mean(values, axis=1, keepdims=True)
    shifted = values - center
    spread = jnp.mean(shifted * shifted, axis=1, keepdims=True)
    inverse = lax.rsqrt(spread + NORM_EPS)
    return (shifted * inverse, inverse)


def norm_backward(grad_in, normed, inverse, gain_row):
    gain_grad = jnp.sum(grad_in * normed, axis=0)
    shift_grad = jnp.sum(grad_in, axis=0)
    scaled = grad_in * gain_row
    first_mean = jnp.mean(scaled, axis=1, keepdims=True)
    second_mean = jnp.mean(scaled * normed, axis=1, keepdims=True)
    return (inverse * (scaled - first_mean - normed * second_mean), gain_grad, shift_grad)


def running_sum(counts):
    size = counts.shape[-1]
    places = jnp.arange(size, dtype=jnp.int32)
    upto = (places[:, None] <= places[None, :]).astype(jnp.int32)
    return jnp.sum(counts[..., :, None] * upto, axis=-2, dtype=jnp.int32)


def given_layout(lengths_mb, dealing_mb):
    seq_count = dealing_mb.shape[0]
    labels = jnp.arange(seq_count, dtype=jnp.int32)
    flat_lengths = lengths_mb.reshape(seq_count)
    one_hot = (dealing_mb[:, None] == labels[None, :]).astype(jnp.int32)
    given_len = jnp.sum(one_hot * flat_lengths[None, :], axis=1, dtype=jnp.int32)
    given_off = running_sum(given_len) - given_len
    start_by_seq = jnp.sum(one_hot * given_off[:, None], axis=0, dtype=jnp.int32)
    return (given_len, given_off, start_by_seq)


def buffer_layout(lengths_dev, start_dev, rows_total):
    seq_count = lengths_dev.shape[0]
    end_rows = running_sum(lengths_dev)
    offsets = end_rows - lengths_dev
    row_ids = jnp.arange(rows_total, dtype=jnp.int32)
    holder = jnp.sum(
        (row_ids[:, None] >= end_rows[None, :]).astype(jnp.int32), axis=1, dtype=jnp.int32
    )
    one_hot = (holder[:, None] == jnp.arange(seq_count, dtype=jnp.int32)[None, :]).astype(jnp.int32)
    position = row_ids - jnp.sum(one_hot * offsets[None, :], axis=1, dtype=jnp.int32)
    source = jnp.sum(one_hot * start_dev[None, :], axis=1, dtype=jnp.int32) + position
    return (holder, position, source)


def visible(holder, position, first_row, last_row, key_reach):
    period = SEG + SUMM
    query_seq = holder[first_row:last_row, None]
    key_seq = holder[None, :key_reach]
    query_part = position[first_row:last_row, None] // period
    key_part = position[None, :key_reach] // period
    summary = position[None, :key_reach] % period >= SEG
    query_row = jnp.arange(first_row, last_row, dtype=jnp.int32)[:, None]
    key_row = jnp.arange(key_reach, dtype=jnp.int32)[None, :]
    same_part = (query_part == key_part) & (key_row <= query_row)
    earlier = (key_part < query_part) & summary
    return (query_seq == key_seq) & (same_part | earlier)


def block_scores(queries, keys_all, allowed, score_scale):
    scores = (
        jnp.einsum("qhd,khd->hqk", queries, keys_all, preferred_element_type=jnp.float32)
        * score_scale
    )
    return jnp.where(allowed[None], scores, MASKED)


def shards(
    tokens,
    cotangent,
    lengths,
    dealing,
    query_weight,
    key_weight,
    value_weight,
    out_weight,
    query_bias,
    value_bias,
    out_bias,
    up_weight,
    up_bias,
    down_weight,
    down_bias,
    attn_gain,
    attn_shift,
    mlp_gain,
    mlp_shift,
):
    micro_count = tokens.shape[0]
    tok_rows = tokens.shape[1]
    col_width = tokens.shape[2]
    seq_dev = lengths.shape[2]
    heads_here = query_weight.shape[1] // HEAD_DIM
    head_cols = heads_here * HEAD_DIM
    block_rows = tok_rows // NBLK
    score_scale = HEAD_DIM ** (-0.5)
    device = lax.axis_index("dp")
    column = lax.axis_index("tensor")
    gain_one = attn_gain.astype(jnp.float32)
    shift_one = attn_shift.astype(jnp.float32)
    gain_two = mlp_gain.astype(jnp.float32)
    shift_two = mlp_shift.astype(jnp.float32)
    query_bias_f = query_bias.astype(jnp.float32)
    value_bias_f = value_bias.astype(jnp.float32)
    up_bias_f = up_bias.astype(jnp.float32)
    out_bias_cols = lax.dynamic_slice_in_dim(
        out_bias.astype(jnp.float32), column * col_width, col_width
    )
    down_bias_cols = lax.dynamic_slice_in_dim(
        down_bias.astype(jnp.float32), column * col_width, col_width
    )
    query_w_grad = jnp.zeros(query_weight.shape, jnp.float32)
    key_w_grad = jnp.zeros(key_weight.shape, jnp.float32)
    value_w_grad = jnp.zeros(value_weight.shape, jnp.float32)
    out_w_grad = jnp.zeros(out_weight.shape, jnp.float32)
    query_b_grad = jnp.zeros(query_bias.shape, jnp.float32)
    value_b_grad = jnp.zeros(value_bias.shape, jnp.float32)
    out_b_grad = jnp.zeros(out_bias.shape, jnp.float32)
    up_w_grad = jnp.zeros(up_weight.shape, jnp.float32)
    up_b_grad = jnp.zeros(up_bias.shape, jnp.float32)
    down_w_grad = jnp.zeros(down_weight.shape, jnp.float32)
    down_b_grad = jnp.zeros(down_bias.shape, jnp.float32)
    gain_one_grad = jnp.zeros(attn_gain.shape, jnp.float32)
    shift_one_grad = jnp.zeros(attn_shift.shape, jnp.float32)
    gain_two_grad = jnp.zeros(mlp_gain.shape, jnp.float32)
    shift_two_grad = jnp.zeros(mlp_shift.shape, jnp.float32)
    layer_parts = []
    grad_parts = []
    for micro_step in range(micro_count):
        lengths_mb = lengths[micro_step]
        dealing_mb = dealing[micro_step]
        given_len, given_off, start_by_seq = given_layout(lengths_mb, dealing_mb)
        lengths_dev = lax.dynamic_index_in_dim(lengths_mb, device, 0, keepdims=False)
        start_dev = lax.dynamic_slice_in_dim(start_by_seq, device * seq_dev, seq_dev)
        holder, position, source = buffer_layout(lengths_dev, start_dev, tok_rows)
        blank_rows = jnp.zeros((tok_rows, col_width), jnp.bfloat16)
        pieces = (
            lax.all_gather(tokens[micro_step], "dp", axis=0, tiled=True),
            lax.all_gather(cotangent[micro_step], "dp", axis=0, tiled=True),
        )
        span_rows = pieces[0].shape[0]
        inside = ((source >= 0) & (source < span_rows))[:, None]
        fetch_at = jnp.clip(source, 0, span_rows - 1)
        tok_buf = jnp.where(inside, jnp.take(pieces[0], fetch_at, axis=0), blank_rows)
        cot_buf = jnp.where(inside, jnp.take(pieces[1], fetch_at, axis=0), blank_rows)
        tok_full, cot_full = (
            lax.all_gather(tok_buf, "tensor", axis=1, tiled=True),
            lax.all_gather(cot_buf, "tensor", axis=1, tiled=True),
        )
        normed_one, inverse_one = normalize(tok_full.astype(jnp.float32))
        first_in = (normed_one * gain_one + shift_one).astype(jnp.bfloat16)
        queries = (
            (matmul(first_in, query_weight) + query_bias_f)
            .astype(jnp.bfloat16)
            .reshape(tok_rows, heads_here, HEAD_DIM)
        )
        keys_here = (
            matmul(first_in, key_weight)
            .astype(jnp.bfloat16)
            .reshape(tok_rows, heads_here, HEAD_DIM)
        )
        values_here = (
            (matmul(first_in, value_weight) + value_bias_f)
            .astype(jnp.bfloat16)
            .reshape(tok_rows, heads_here, HEAD_DIM)
        )
        outputs = []
        row_tops = []
        row_totals = []
        for block_index in range(NBLK):
            row_lower = block_index * block_rows
            row_upper = row_lower + block_rows
            allowed = visible(holder, position, row_lower, row_upper, row_upper)
            scores = block_scores(
                queries[row_lower:row_upper], keys_here[:row_upper], allowed, score_scale
            )
            row_top = jnp.max(scores, axis=2, keepdims=True)
            exp_terms = jnp.exp(scores - row_top)
            row_total = jnp.sum(exp_terms, axis=2, keepdims=True)
            attn_prob = exp_terms / row_total
            outputs.append(
                jnp.einsum(
                    "hqk,khd->qhd",
                    attn_prob.astype(jnp.bfloat16),
                    values_here[:row_upper],
                    preferred_element_type=jnp.float32,
                )
            )
            row_tops.append(row_top)
            row_totals.append(row_total)
        mixed_heads = (
            jnp.concatenate(outputs, axis=0).reshape(tok_rows, head_cols).astype(jnp.bfloat16)
        )
        attn_cols = lax.psum_scatter(
            matmul(mixed_heads, out_weight), "tensor", scatter_dimension=1, tiled=True
        )
        resid_cols = tok_buf.astype(jnp.float32) + attn_cols + out_bias_cols
        resid_full = lax.all_gather(resid_cols.astype(jnp.bfloat16), "tensor", axis=1, tiled=True)
        normed_two, inverse_two = normalize(resid_full.astype(jnp.float32))
        second_in = (normed_two * gain_two + shift_two).astype(jnp.bfloat16)
        hidden_pre = matmul(second_in, up_weight) + up_bias_f
        hidden_act, gelu_pull = jax.vjp(gelu_tanh, hidden_pre)
        hidden = hidden_act.astype(jnp.bfloat16)
        mlp_cols = lax.psum_scatter(
            matmul(hidden, down_weight).astype(jnp.bfloat16),
            "tensor",
            scatter_dimension=1,
            tiled=True,
        ).astype(jnp.float32)
        layer_cols = (resid_cols + mlp_cols + down_bias_cols).astype(jnp.bfloat16)
        grad_out = cot_full.astype(jnp.float32)
        down_w_grad = down_w_grad + cross_rows(hidden, cot_full)
        down_b_grad = down_b_grad + jnp.sum(grad_out, axis=0)
        hidden_grad = gelu_pull(times_transpose(cot_full, down_weight))[0]
        up_b_grad = up_b_grad + jnp.sum(hidden_grad, axis=0)
        hidden_low = hidden_grad.astype(jnp.bfloat16)
        up_w_grad = up_w_grad + cross_rows(second_in, hidden_low)
        second_cols = lax.psum_scatter(
            times_transpose(hidden_low, up_weight), "tensor", scatter_dimension=1, tiled=True
        )
        second_grad = lax.all_gather(
            second_cols.astype(jnp.bfloat16), "tensor", axis=1, tiled=True
        ).astype(jnp.float32)
        resid_back, gain_part, shift_part = norm_backward(
            second_grad, normed_two, inverse_two, gain_two
        )
        gain_two_grad = gain_two_grad + gain_part
        shift_two_grad = shift_two_grad + shift_part
        resid_grad = grad_out + resid_back
        out_b_grad = out_b_grad + jnp.sum(resid_grad, axis=0)
        attn_low = resid_grad.astype(jnp.bfloat16)
        out_w_grad = out_w_grad + cross_rows(mixed_heads, attn_low)
        mixed_grad = (
            times_transpose(attn_low, out_weight)
            .astype(jnp.bfloat16)
            .reshape(tok_rows, heads_here, HEAD_DIM)
        )
        query_parts = []
        key_acc = jnp.zeros((tok_rows, heads_here, HEAD_DIM), jnp.float32)
        value_acc = jnp.zeros((tok_rows, heads_here, HEAD_DIM), jnp.float32)
        for block_index in range(NBLK):
            row_lower = block_index * block_rows
            row_upper = row_lower + block_rows
            allowed = visible(holder, position, row_lower, row_upper, row_upper)
            scores = block_scores(
                queries[row_lower:row_upper], keys_here[:row_upper], allowed, score_scale
            )
            attn_prob = jnp.exp(scores - row_tops[block_index]) / row_totals[block_index]
            grad_block = mixed_grad[row_lower:row_upper]
            prob_grad = jnp.einsum(
                "qhd,khd->hqk",
                grad_block,
                values_here[:row_upper],
                preferred_element_type=jnp.float32,
            )
            inner_sum = jnp.sum(attn_prob * prob_grad, axis=2, keepdims=True)
            score_grad = (attn_prob * (prob_grad - inner_sum)).astype(jnp.bfloat16)
            query_parts.append(
                jnp.einsum(
                    "hqk,khd->qhd",
                    score_grad,
                    keys_here[:row_upper],
                    preferred_element_type=jnp.float32,
                )
                * score_scale
            )
            pad_rows = ((0, tok_rows - row_upper), (0, 0), (0, 0))
            key_acc = key_acc + jnp.pad(
                jnp.einsum(
                    "hqk,qhd->khd",
                    score_grad,
                    queries[row_lower:row_upper],
                    preferred_element_type=jnp.float32,
                )
                * score_scale,
                pad_rows,
            )
            value_acc = value_acc + jnp.pad(
                jnp.einsum(
                    "hqk,qhd->khd",
                    attn_prob.astype(jnp.bfloat16),
                    grad_block,
                    preferred_element_type=jnp.float32,
                ),
                pad_rows,
            )
        query_grad = jnp.concatenate(query_parts, axis=0).reshape(tok_rows, head_cols)
        key_grad = key_acc.reshape(tok_rows, head_cols)
        value_grad = value_acc.reshape(tok_rows, head_cols)
        query_b_grad = query_b_grad + jnp.sum(query_grad, axis=0)
        value_b_grad = value_b_grad + jnp.sum(value_grad, axis=0)
        query_low = query_grad.astype(jnp.bfloat16)
        key_low = key_grad.astype(jnp.bfloat16)
        value_low = value_grad.astype(jnp.bfloat16)
        query_w_grad = query_w_grad + cross_rows(first_in, query_low)
        key_w_grad = key_w_grad + cross_rows(first_in, key_low)
        value_w_grad = value_w_grad + cross_rows(first_in, value_low)
        first_part = (
            times_transpose(query_low, query_weight)
            + times_transpose(key_low, key_weight)
            + times_transpose(value_low, value_weight)
        )
        first_cols = lax.psum_scatter(first_part, "tensor", scatter_dimension=1, tiled=True)
        first_grad = lax.all_gather(
            first_cols.astype(jnp.bfloat16), "tensor", axis=1, tiled=True
        ).astype(jnp.float32)
        input_back, gain_part, shift_part = norm_backward(
            first_grad, normed_one, inverse_one, gain_one
        )
        gain_one_grad = gain_one_grad + gain_part
        shift_one_grad = shift_one_grad + shift_part
        input_cols = lax.dynamic_slice_in_dim(
            resid_grad + input_back, column * col_width, col_width, axis=1
        ).astype(jnp.bfloat16)
        packed = jnp.concatenate([layer_cols, input_cols], axis=1)
        given_end = given_off + given_len
        dest_off = (running_sum(lengths_mb) - lengths_mb).reshape(-1)
        labels = jnp.arange(dealing_mb.shape[0], dtype=jnp.int32)
        give_row_ids = jnp.arange(tok_rows * lax.axis_size("dp"), dtype=jnp.int32)
        owner_seq = jnp.sum(
            (give_row_ids[:, None] >= given_end[None, :]).astype(jnp.int32), axis=1, dtype=jnp.int32
        )
        one_hot = (owner_seq[:, None] == labels[None, :]).astype(jnp.int32)
        within = give_row_ids - jnp.sum(one_hot * given_off[None, :], axis=1, dtype=jnp.int32)
        seq_label = jnp.sum(one_hot * dealing_mb[None, :], axis=1, dtype=jnp.int32)
        seq_hot = (seq_label[:, None] == labels[None, :]).astype(jnp.int32)
        buffer_row = jnp.sum(seq_hot * dest_off[None, :], axis=1, dtype=jnp.int32) + within
        owner_dev = seq_label // seq_dev
        is_mine = owner_dev == device
        fetched = jnp.take(packed, jnp.clip(buffer_row, 0, tok_rows - 1), axis=0).astype(
            jnp.float32
        )
        returned = lax.psum_scatter(
            jnp.where(is_mine[:, None], fetched, 0.0).astype(jnp.bfloat16),
            "dp",
            scatter_dimension=0,
            tiled=True,
        ).astype(jnp.float32)
        layer_parts.append(returned[:, :col_width].astype(jnp.bfloat16))
        grad_parts.append(returned[:, col_width:].astype(jnp.bfloat16))
    (
        query_w_grad,
        key_w_grad,
        value_w_grad,
        out_w_grad,
        query_b_grad,
        value_b_grad,
        out_b_grad,
        gain_one_grad,
        shift_one_grad,
        up_w_grad,
        up_b_grad,
        down_w_grad,
        down_b_grad,
        gain_two_grad,
        shift_two_grad,
    ) = lax.psum(
        (
            query_w_grad,
            key_w_grad,
            value_w_grad,
            out_w_grad,
            query_b_grad,
            value_b_grad,
            out_b_grad,
            gain_one_grad,
            shift_one_grad,
            up_w_grad,
            up_b_grad,
            down_w_grad,
            down_b_grad,
            gain_two_grad,
            shift_two_grad,
        ),
        "dp",
    )
    layer_out = jnp.stack(layer_parts, axis=0)
    input_grad = jnp.stack(grad_parts, axis=0)
    return (
        layer_out,
        input_grad,
        query_w_grad,
        key_w_grad,
        value_w_grad,
        out_w_grad,
        query_b_grad,
        value_b_grad,
        out_b_grad,
        up_w_grad,
        up_b_grad,
        down_w_grad,
        down_b_grad,
        gain_one_grad,
        shift_one_grad,
        gain_two_grad,
        shift_two_grad,
    )


def general_layer(mesh):
    in_specs = (
        P(None, "dp", "tensor"),
        P(None, "dp", "tensor"),
        P(),
        P(),
        P(None, "tensor"),
        P(None, "tensor"),
        P(None, "tensor"),
        P("tensor", None),
        P("tensor"),
        P("tensor"),
        P(),
        P(None, "tensor"),
        P("tensor"),
        P("tensor", None),
        P(),
        P(),
        P(),
        P(),
        P(),
    )
    out_specs = (
        P(None, "dp", "tensor"),
        P(None, "dp", "tensor"),
        P(None, "tensor"),
        P(None, "tensor"),
        P(None, "tensor"),
        P("tensor", None),
        P("tensor"),
        P("tensor"),
        P(),
        P(None, "tensor"),
        P("tensor"),
        P("tensor", None),
        P(),
        P(),
        P(),
        P(),
        P(),
    )
    return jax.shard_map(shards, mesh=mesh, in_specs=in_specs, out_specs=out_specs, check_vma=False)


ROWS = 1024
QBLK = 256
PAIR = 128


def slot_of(block, rank):
    piece = jnp.bitwise_xor(block, rank)
    return jnp.bitwise_or(piece >> 1, (piece & 1) << 1)


def rows_of(block, rank):
    return pl.ds(pl.multiple_of(slot_of(block, rank) * QBLK, QBLK), QBLK)


def fill_bias(bias_ref, key_info_ref, query_info_ref):
    for block in range(ROWS // QBLK):
        reach = (block + 1) * QBLK
        cols = pl.ds(block * QBLK, QBLK)
        key_part = key_info_ref[pl.ds(0, reach), 0:1]
        key_summary = key_info_ref[pl.ds(0, reach), 1:2]
        query_part = query_info_ref[0:1, cols]
        query_seq = query_info_ref[1:2, cols]
        key_row = lax.broadcasted_iota(jnp.int32, (reach, QBLK), 0)
        query_row = lax.broadcasted_iota(jnp.int32, (reach, QBLK), 1) + block * QBLK
        seen = (key_row <= query_row) & ((key_part == query_part) | (key_summary == query_seq))
        bias_ref[pl.ds(0, reach), cols] = jnp.where(seen, 0.0, MASKED)


def nt_dot(left, right):
    return lax.dot_general(left, right, (((1,), (1,)), ((), ())), preferred_element_type=jnp.float32)


def nn_dot(left, right):
    return jnp.dot(left, right, preferred_element_type=jnp.float32)


def head_lanes(block, head):
    lane = lax.broadcasted_iota(jnp.int32, block.shape, 1)
    inside = (lane >= head * HEAD_DIM) & (lane < (head + 1) * HEAD_DIM)
    return jnp.where(inside, block, jnp.zeros_like(block))


def attend_kernel(
    rank_ref, query_ref, key_ref, value_ref, key_info_ref, query_info_ref, out_ref, bias_ref, keys, value_t
):
    rank = rank_ref[0]

    @pl.when(pl.program_id(0) == 0)
    def _():
        fill_bias(bias_ref, key_info_ref, query_info_ref)

    for block in range(ROWS // QBLK):
        here = rows_of(block, rank)
        keys[pl.ds(block * QBLK, QBLK), :] = key_ref[here, :]
        value_t[:, pl.ds(block * QBLK, QBLK)] = value_ref[here, :].T
    for block in range(ROWS // QBLK):
        reach = (block + 1) * QBLK
        here = rows_of(block, rank)
        queries = query_ref[here, :] * jnp.bfloat16(HEAD_DIM**-0.5)
        bias = bias_ref[pl.ds(0, reach), pl.ds(block * QBLK, QBLK)]
        parts = []
        for head in range(2):
            scores = nt_dot(keys[pl.ds(0, reach), :], head_lanes(queries, head)) + bias
            top = jnp.max(scores, axis=0, keepdims=True)
            terms = jnp.exp(scores - top)
            total = jnp.sum(terms, axis=0, keepdims=True)
            heads_t = nn_dot(
                value_t[pl.ds(head * HEAD_DIM, HEAD_DIM), pl.ds(0, reach)], terms.astype(jnp.bfloat16)
            )
            parts.append(heads_t / total)
        out_ref[here, :] = jnp.concatenate(parts, axis=0).T.astype(out_ref.dtype)


def attend(qkv, rank, key_info, query_info):
    pairs = qkv.shape[1] // (3 * PAIR)
    cells = ROWS * ROWS * 5 // 8
    return pl.pallas_call(
        attend_kernel,
        grid_spec=pltpu.PrefetchScalarGridSpec(
            num_scalar_prefetch=1,
            grid=(pairs,),
            in_specs=[
                pl.BlockSpec((ROWS, PAIR), lambda i, r: (0, i)),
                pl.BlockSpec((ROWS, PAIR), lambda i, r: (0, pairs + i)),
                pl.BlockSpec((ROWS, PAIR), lambda i, r: (0, 2 * pairs + i)),
                pl.BlockSpec((ROWS, 2), lambda i, r: (0, 0)),
                pl.BlockSpec((2, ROWS), lambda i, r: (0, 0)),
            ],
            out_specs=pl.BlockSpec((ROWS, PAIR), lambda i, r: (0, i)),
            scratch_shapes=[
                pltpu.VMEM((ROWS, ROWS), jnp.float32),
                pltpu.VMEM((ROWS, PAIR), jnp.bfloat16),
                pltpu.VMEM((PAIR, ROWS), jnp.bfloat16),
            ],
        ),
        out_shape=jax.ShapeDtypeStruct((ROWS, pairs * PAIR), jnp.bfloat16),
        compiler_params=pltpu.CompilerParams(vmem_limit_bytes=24 << 20),
        cost_estimate=light(),
        name="attend",
    )(rank, qkv, qkv, qkv, key_info, query_info)


def attend_back_kernel(
    rank_ref,
    query_ref,
    key_ref,
    value_ref,
    grad_ref,
    key_info_ref,
    query_info_ref,
    query_out,
    key_out,
    value_out,
    sums_out,
    bias_ref,
    keys,
    values,
    key_t,
    key_acc,
    value_acc,
):
    rank = rank_ref[0]
    scale = HEAD_DIM**-0.5

    @pl.when(pl.program_id(0) == 0)
    def _():
        fill_bias(bias_ref, key_info_ref, query_info_ref)

    for block in range(ROWS // QBLK):
        here = rows_of(block, rank)
        there = pl.ds(block * QBLK, QBLK)
        keys[there, :] = key_ref[here, :]
        values[there, :] = value_ref[here, :]
        key_t[:, there] = key_ref[here, :].T
    query_sum = jnp.zeros((1, PAIR), jnp.float32)
    for block in reversed(range(ROWS // QBLK)):
        reach = (block + 1) * QBLK
        here = rows_of(block, rank)
        upto = pl.ds(0, reach)
        queries = query_ref[here, :] * jnp.bfloat16(scale)
        grads = grad_ref[here, :]
        bias = bias_ref[upto, pl.ds(block * QBLK, QBLK)]
        parts = []
        key_add = None
        value_add = None
        for head in range(2):
            query_h = head_lanes(queries, head)
            grad_h = head_lanes(grads, head)
            scores = nt_dot(keys[upto, :], query_h) + bias
            top = jnp.max(scores, axis=0, keepdims=True)
            terms = jnp.exp(scores - top)
            prob = terms * (1.0 / jnp.sum(terms, axis=0, keepdims=True))
            prob_grad = nt_dot(values[upto, :], grad_h)
            inner = jnp.sum(prob * prob_grad, axis=0, keepdims=True)
            score_grad = (prob * (prob_grad - inner)).astype(jnp.bfloat16)
            value_part = nn_dot(prob.astype(jnp.bfloat16), grad_h)
            key_part = nn_dot(score_grad, query_h)
            value_add = value_part if value_add is None else value_add + value_part
            key_add = key_part if key_add is None else key_add + key_part
            parts.append(nn_dot(key_t[pl.ds(head * HEAD_DIM, HEAD_DIM), upto], score_grad))
        if block == ROWS // QBLK - 1:
            key_acc[...] = key_add
            value_acc[...] = value_add
        else:
            key_acc[upto, :] += key_add
            value_acc[upto, :] += value_add
        query_grad = jnp.concatenate(parts, axis=0).T * scale
        query_sum = query_sum + jnp.sum(query_grad, axis=0, keepdims=True)
        query_out[here, :] = query_grad.astype(query_out.dtype)
    for block in range(ROWS // QBLK):
        here = rows_of(block, rank)
        there = pl.ds(block * QBLK, QBLK)
        key_out[here, :] = key_acc[there, :].astype(key_out.dtype)
        value_out[here, :] = value_acc[there, :].astype(value_out.dtype)
    value_sum = jnp.sum(value_acc[...], axis=0, keepdims=True)
    row = lax.broadcasted_iota(jnp.int32, (8, PAIR), 0)
    sums_out[...] = jnp.where(row == 0, query_sum, jnp.where(row == 1, value_sum, 0.0))


def attend_back(qkv, grads, rank, key_info, query_info):
    pairs = qkv.shape[1] // (3 * PAIR)
    cells = ROWS * ROWS * 5 // 8
    block = (ROWS, PAIR)
    wide = jax.ShapeDtypeStruct((ROWS, pairs * PAIR), jnp.bfloat16)
    return pl.pallas_call(
        attend_back_kernel,
        grid_spec=pltpu.PrefetchScalarGridSpec(
            num_scalar_prefetch=1,
            grid=(pairs,),
            in_specs=[
                pl.BlockSpec(block, lambda i, r: (0, i)),
                pl.BlockSpec(block, lambda i, r: (0, pairs + i)),
                pl.BlockSpec(block, lambda i, r: (0, 2 * pairs + i)),
                pl.BlockSpec(block, lambda i, r: (0, i)),
                pl.BlockSpec((ROWS, 2), lambda i, r: (0, 0)),
                pl.BlockSpec((2, ROWS), lambda i, r: (0, 0)),
            ],
            out_specs=[
                pl.BlockSpec(block, lambda i, r: (0, i)),
                pl.BlockSpec(block, lambda i, r: (0, i)),
                pl.BlockSpec(block, lambda i, r: (0, i)),
                pl.BlockSpec((8, PAIR), lambda i, r: (0, i)),
            ],
            scratch_shapes=[
                pltpu.VMEM((ROWS, ROWS), jnp.float32),
                pltpu.VMEM(block, jnp.bfloat16),
                pltpu.VMEM(block, jnp.bfloat16),
                pltpu.VMEM((PAIR, ROWS), jnp.bfloat16),
                pltpu.VMEM(block, jnp.float32),
                pltpu.VMEM(block, jnp.float32),
            ],
        ),
        out_shape=[wide, wide, wide, jax.ShapeDtypeStruct((8, pairs * PAIR), jnp.float32)],
        compiler_params=pltpu.CompilerParams(vmem_limit_bytes=28 << 20),
        cost_estimate=light(),
        name="attend_back",
    )(rank, qkv, qkv, qkv, grads, key_info, query_info)


WIDE = 512
VMEM_BYTES = 56 << 20


def light(flops=1 << 20):
    return pl.CostEstimate(flops=flops, bytes_accessed=1 << 12, transcendentals=0)


def settings():
    return pltpu.CompilerParams(vmem_limit_bytes=VMEM_BYTES)


def whole(shape):
    return pl.BlockSpec(shape, lambda i: (0,) * len(shape))


def project_kernel(near_ref, far_ref, weight_ref, bias_ref, out_ref):
    rows = near_ref.shape[0]
    bias = bias_ref[...]
    out_ref[pl.ds(0, rows), :] = (nt_dot(near_ref[...], weight_ref[...]) + bias).astype(out_ref.dtype)
    out_ref[pl.ds(rows, rows), :] = (nt_dot(far_ref[...], weight_ref[...]) + bias).astype(out_ref.dtype)


def project(near, far, weight, bias):
    rows, depth = near.shape
    cols = weight.shape[0]
    return pl.pallas_call(
        project_kernel,
        grid=(cols // WIDE,),
        in_specs=[
            whole((rows, depth)),
            whole((rows, depth)),
            pl.BlockSpec((WIDE, depth), lambda i: (i, 0)),
            pl.BlockSpec((1, WIDE), lambda i: (0, i)),
        ],
        out_specs=pl.BlockSpec((2 * rows, WIDE), lambda i: (0, i)),
        out_shape=jax.ShapeDtypeStruct((2 * rows, cols), jnp.bfloat16),
        compiler_params=settings(),
        cost_estimate=light(),
        name="project",
    )(near, far, weight, bias)


def expand_kernel(near_ref, far_ref, weight_ref, bias_ref, hidden_ref, slope_ref):
    rows = near_ref.shape[0]
    bias = bias_ref[...]
    for part, ref in enumerate((near_ref, far_ref)):
        at = pl.ds(part * rows, rows)
        pre = nt_dot(ref[...], weight_ref[...]) + bias
        cube = 0.044715 * pre * pre
        bend = jnp.tanh((0.7978845608028654 * pre) * (1.0 + cube))
        half = 0.5 + 0.5 * bend
        inner = 0.7978845608028654 + (3.0 * 0.7978845608028654) * cube
        hidden_ref[at, :] = (pre * half).astype(jnp.bfloat16)
        slope_ref[at, :] = (half + (pre * half) * ((1.0 - bend) * inner)).astype(jnp.bfloat16)


def expand(near, far, weight, bias):
    rows, depth = near.shape
    cols = weight.shape[0]
    out = jax.ShapeDtypeStruct((2 * rows, cols), jnp.bfloat16)
    return pl.pallas_call(
        expand_kernel,
        grid=(cols // WIDE,),
        in_specs=[
            whole((rows, depth)),
            whole((rows, depth)),
            pl.BlockSpec((WIDE, depth), lambda i: (i, 0)),
            pl.BlockSpec((1, WIDE), lambda i: (0, i)),
        ],
        out_specs=[pl.BlockSpec((2 * rows, WIDE), lambda i: (0, i))] * 2,
        out_shape=[out, out],
        compiler_params=settings(),
        cost_estimate=light(),
        name="expand",
    )(near, far, weight, bias)


def expand_back_kernel(near_ref, far_ref, weight_ref, slope_ref, low_ref, sums_ref):
    rows = near_ref.shape[0]
    total = jnp.zeros((1, low_ref.shape[1]), jnp.float32)
    for part, ref in enumerate((near_ref, far_ref)):
        at = pl.ds(part * rows, rows)
        grad = nt_dot(ref[...], weight_ref[...]) * slope_ref[at, :].astype(jnp.float32)
        total = total + jnp.sum(grad, axis=0, keepdims=True)
        low_ref[at, :] = grad.astype(jnp.bfloat16)
    sums_ref[...] = jnp.broadcast_to(total, sums_ref.shape)


def expand_back(near, far, weight, slope):
    rows, depth = near.shape
    cols = weight.shape[0]
    return pl.pallas_call(
        expand_back_kernel,
        grid=(cols // WIDE,),
        in_specs=[
            whole((rows, depth)),
            whole((rows, depth)),
            pl.BlockSpec((WIDE, depth), lambda i: (i, 0)),
            pl.BlockSpec((2 * rows, WIDE), lambda i: (0, i)),
        ],
        out_specs=[pl.BlockSpec((2 * rows, WIDE), lambda i: (0, i)), pl.BlockSpec((8, WIDE), lambda i: (0, i))],
        out_shape=[
            jax.ShapeDtypeStruct((2 * rows, cols), jnp.bfloat16),
            jax.ShapeDtypeStruct((8, cols), jnp.float32),
        ],
        compiler_params=settings(),
        cost_estimate=light(),
        name="expand_back",
    )(near, far, weight, slope)


def partial_kernel(left_ref, weight_ref, near_ref, far_ref):
    rows = near_ref.shape[0]
    far_ref[...] = nn_dot(left_ref[pl.ds(rows, rows), :], weight_ref[...]).astype(far_ref.dtype)
    near_ref[...] = nn_dot(left_ref[pl.ds(0, rows), :], weight_ref[...])


def partial_sums(left, weight):
    rows, depth = left.shape
    cols = weight.shape[1]
    half = rows // 2
    return pl.pallas_call(
        partial_kernel,
        grid=(cols // WIDE,),
        in_specs=[whole((rows, depth)), pl.BlockSpec((depth, WIDE), lambda i: (0, i))],
        out_specs=[pl.BlockSpec((half, WIDE), lambda i: (0, i))] * 2,
        out_shape=[
            jax.ShapeDtypeStruct((half, cols), jnp.float32),
            jax.ShapeDtypeStruct((half, cols), jnp.bfloat16),
        ],
        compiler_params=settings(),
        cost_estimate=light(),
        name="partial_sums",
    )(left, weight)


def tn_dot(left, right):
    return lax.dot_general(left, right, (((0,), (0,)), ((), ())), preferred_element_type=jnp.float32)


def cross_kernel(left_a, near_a, far_a, left_b, near_b, far_b, out_ref):
    rows = near_a.shape[0]
    top, low = pl.ds(0, rows), pl.ds(rows, rows)
    total = tn_dot(left_a[top, :], near_a[...]) + tn_dot(left_a[low, :], far_a[...])
    total = total + tn_dot(left_b[top, :], near_b[...]) + tn_dot(left_b[low, :], far_b[...])
    out_ref[...] = total.astype(out_ref.dtype)


def cross_sums(left_a, right_a, left_b, right_b, start, size):
    rows = left_a.shape[0]
    cols = right_a[0].shape[1]
    tall = 256
    first = start // tall
    left_spec = pl.BlockSpec((rows, tall), lambda i: (0, first + i))
    right_spec = whole((rows // 2, cols))
    return pl.pallas_call(
        cross_kernel,
        grid=(size // tall,),
        in_specs=[left_spec, right_spec, right_spec] * 2,
        out_specs=pl.BlockSpec((tall, cols), lambda i: (i, 0)),
        out_shape=jax.ShapeDtypeStruct((size, cols), jnp.bfloat16),
        compiler_params=settings(),
        cost_estimate=light(),
        name="cross_sums",
    )(left_a, *right_a, left_b, *right_b)


def flip_kernel(first_ref, weight_ref, out_ref):
    out_ref[...] = weight_ref[...].T


def flipped(weight, first, count):
    depth = weight.shape[0]
    return pl.pallas_call(
        flip_kernel,
        grid_spec=pltpu.PrefetchScalarGridSpec(
            num_scalar_prefetch=1,
            grid=(count,),
            in_specs=[pl.BlockSpec((depth, 128), lambda i, first: (0, first[0] + i))],
            out_specs=pl.BlockSpec((128, depth), lambda i, first: (i, 0)),
        ),
        out_shape=jax.ShapeDtypeStruct((count * 128, depth), weight.dtype),
        compiler_params=settings(),
        cost_estimate=light(),
        name="flipped",
    )(first.reshape(1).astype(jnp.int32), weight)


def attn_pack_kernel(
    place_ref, query_ref, key_ref, value_ref, out_w_ref, bias_mine, bias_other, mine_ref, other_ref
):
    half = place_ref[1]
    mine_ref[pl.ds(4 * HEAD_DIM, 8), :] = bias_mine[...]
    other_ref[pl.ds(4 * HEAD_DIM, 8), :] = bias_other[...]
    for which, ref in enumerate((mine_ref, other_ref)):
        rows = pl.ds(pl.multiple_of(jnp.where(which == 0, half, 1 - half) * HEAD_DIM, HEAD_DIM), HEAD_DIM)
        ref[pl.ds(3 * HEAD_DIM, HEAD_DIM), :] = out_w_ref[rows, :]
    for index, source in enumerate((query_ref, key_ref, value_ref)):
        flat = source[...].T
        low, high = flat[:HEAD_DIM, :], flat[HEAD_DIM:, :]
        at = pl.ds(index * HEAD_DIM, HEAD_DIM)
        mine_ref[at, :] = jnp.where(half == 0, low, high)
        other_ref[at, :] = jnp.where(half == 0, high, low)


def attn_pack(query_weight, key_weight, value_weight, out_weight, bias_mine, bias_other, team, half):
    depth = query_weight.shape[0]
    out = jax.ShapeDtypeStruct((4 * HEAD_DIM + 8, depth), query_weight.dtype)
    column = pl.BlockSpec((depth, 128), lambda i, place: (0, place[0]))
    full = pl.BlockSpec((4 * HEAD_DIM + 8, depth), lambda i, place: (0, 0))
    bias = pl.BlockSpec((8, depth), lambda i, place: (0, 0))
    return pl.pallas_call(
        attn_pack_kernel,
        grid_spec=pltpu.PrefetchScalarGridSpec(
            num_scalar_prefetch=1,
            grid=(1,),
            in_specs=[column, column, column, pl.BlockSpec((128, depth), lambda i, place: (place[0], 0)), bias, bias],
            out_specs=[full, full],
        ),
        out_shape=[out, out],
        compiler_params=settings(),
        cost_estimate=light(),
        name="attn_pack",
    )(jnp.stack([team, half]).astype(jnp.int32), query_weight, key_weight, value_weight, out_weight, bias_mine, bias_other)


def pick_kernel(index_ref, rows_ref, out_ref):
    wanted = index_ref[...]
    place = lax.broadcasted_iota(jnp.int32, (wanted.shape[0], rows_ref.shape[0]), 1)
    hot = jnp.where(place == wanted, 1.0, 0.0).astype(jnp.bfloat16)
    out_ref[...] = nn_dot(hot, rows_ref[...]).astype(out_ref.dtype)


def pick_rows(index, rows, tall):
    count = index.shape[0]
    cols = rows.shape[1]
    return pl.pallas_call(
        pick_kernel,
        grid=(count // tall,),
        in_specs=[pl.BlockSpec((tall, 1), lambda i: (i, 0)), whole(rows.shape)],
        out_specs=pl.BlockSpec((tall, cols), lambda i: (i, 0)),
        out_shape=jax.ShapeDtypeStruct((count, cols), rows.dtype),
        compiler_params=settings(),
        cost_estimate=light(),
        name="pick_rows",
    )(index[:, None], rows)


def drop_kernel(index_ref, rows_ref, out_ref):
    wanted = index_ref[...]
    tall = out_ref.shape[0]
    place = lax.broadcasted_iota(jnp.int32, (tall, rows_ref.shape[0]), 0) + pl.program_id(0) * tall
    hot = jnp.where(place == wanted, 1.0, 0.0).astype(jnp.bfloat16)
    out_ref[...] = nn_dot(hot, rows_ref[...]).astype(out_ref.dtype)


def drop_rows(index, rows, count, tall):
    cols = rows.shape[1]
    return pl.pallas_call(
        drop_kernel,
        grid=(count // tall,),
        in_specs=[whole((1, index.shape[0])), whole(rows.shape)],
        out_specs=pl.BlockSpec((tall, cols), lambda i: (i, 0)),
        out_shape=jax.ShapeDtypeStruct((count, cols), rows.dtype),
        compiler_params=settings(),
        cost_estimate=light(),
        name="drop_rows",
    )(index[None, :], rows)


def settle_kernel(index_ref, boxes_ref, out_ref):
    wanted = index_ref[...]
    place = lax.broadcasted_iota(jnp.int32, (out_ref.shape[0], boxes_ref.shape[1]), 0)
    hot = jnp.where(place == wanted, 1.0, 0.0).astype(jnp.bfloat16)
    out_ref[...] = nn_dot(hot, boxes_ref[0]).astype(out_ref.dtype)


def settle_rows(index, boxes, count):
    depth, slots, cols = boxes.shape
    return pl.pallas_call(
        settle_kernel,
        grid=(depth,),
        in_specs=[whole((1, slots)), pl.BlockSpec((1, slots, cols), lambda i: (i, 0, 0))],
        out_specs=pl.BlockSpec((count, cols), lambda i: (0, i)),
        out_shape=jax.ShapeDtypeStruct((count, depth * cols), boxes.dtype),
        compiler_params=settings(),
        cost_estimate=light(),
        name="settle_rows",
    )(index[None, :], boxes)


def unsettle_kernel(index_ref, rows_ref, out_ref):
    wanted = index_ref[...]
    place = lax.broadcasted_iota(jnp.int32, (wanted.shape[0], rows_ref.shape[0]), 1)
    hot = jnp.where(place == wanted, 1.0, 0.0).astype(jnp.bfloat16)
    out_ref[0] = nn_dot(hot, rows_ref[...]).astype(out_ref.dtype)


def unsettle_rows(index, rows, depth):
    slots = index.shape[0]
    count = rows.shape[0]
    cols = rows.shape[1] // depth
    return pl.pallas_call(
        unsettle_kernel,
        grid=(depth,),
        in_specs=[whole((slots, 1)), pl.BlockSpec((count, cols), lambda i: (0, i))],
        out_specs=pl.BlockSpec((1, slots, cols), lambda i: (i, 0, 0)),
        out_shape=jax.ShapeDtypeStruct((depth, slots, cols), rows.dtype),
        compiler_params=settings(),
        cost_estimate=light(),
        name="unsettle_rows",
    )(index[:, None], rows)


def code_of(place, own):
    return jnp.bitwise_xor(place, own)


def piece_of(code):
    return ((code >> 2) & 1) + 2 * (code & 1)


def stack_kernel(own_ref, near_ref, far_ref, out_ref):
    code = code_of(pl.program_id(0), own_ref[0])
    block = jnp.where((code & 2) == 0, near_ref[...], far_ref[...])
    out_ref[...] = block.astype(out_ref.dtype)


def stack_kernel_t(own_ref, near_ref, far_ref, out_ref):
    code = code_of(pl.program_id(0), own_ref[0])
    block = jnp.where((code & 2) == 0, near_ref[...], far_ref[...])
    out_ref[...] = block.T.astype(out_ref.dtype)


def stack_pieces(near, far, own, transposed):
    tall = near.shape[0] // 4
    cols = near.shape[1]
    spec = pl.BlockSpec((tall, cols), lambda i, own: (piece_of(code_of(i, own[0])), 0))
    return pl.pallas_call(
        stack_kernel_t if transposed else stack_kernel,
        grid_spec=pltpu.PrefetchScalarGridSpec(
            num_scalar_prefetch=1,
            grid=(8,),
            in_specs=[spec, spec],
            out_specs=pl.BlockSpec((cols, tall), lambda i, own: (0, i))
            if transposed
            else pl.BlockSpec((tall, cols), lambda i, own: (i, 0)),
        ),
        out_shape=jax.ShapeDtypeStruct((cols, 8 * tall) if transposed else (8 * tall, cols), jnp.float32),
        compiler_params=settings(),
        cost_estimate=light(),
        name="stack_pieces",
    )(own, near, far)


def stack_heads_kernel(flips, own_ref, near_low, far_low, near_high, far_high, *outs):
    code = code_of(2 * pl.program_id(0), own_ref[0])
    take_near = (code & 2) == 0
    low = jnp.where(take_near, near_low[...], far_low[...])
    high = jnp.where(take_near, near_high[...], far_high[...])
    for index, ref in enumerate(outs):
        at = slice(index * HEAD_DIM, (index + 1) * HEAD_DIM)
        both = jnp.concatenate([low[at], high[at]], axis=0)
        ref[...] = (both.T if flips[index] else both).astype(ref.dtype)


def stack_heads(near, far, own, flips):
    tall = near.shape[0] // 4
    cols = near.shape[1]
    low = pl.BlockSpec((tall, cols), lambda i, own: (piece_of(code_of(2 * i, own[0])), 0))
    high = pl.BlockSpec((tall, cols), lambda i, own: (piece_of(code_of(2 * i + 1, own[0])), 0))
    column = pl.BlockSpec((cols, 128), lambda i, own: (0, i))
    row = pl.BlockSpec((128, cols), lambda i, own: (i, 0))
    tall_out = jax.ShapeDtypeStruct((cols, 512), jnp.float32)
    flat_out = jax.ShapeDtypeStruct((512, cols), jnp.float32)
    return pl.pallas_call(
        functools.partial(stack_heads_kernel, flips),
        grid_spec=pltpu.PrefetchScalarGridSpec(
            num_scalar_prefetch=1,
            grid=(4,),
            in_specs=[low, low, high, high],
            out_specs=[column if flip else row for flip in flips],
        ),
        out_shape=[tall_out if flip else flat_out for flip in flips],
        compiler_params=settings(),
        cost_estimate=light(),
        name="stack_heads",
    )(own, near, far, near, far)


def add_rows_kernel(*refs):
    total = refs[0][...].astype(jnp.float32)
    for ref in refs[1:-1]:
        total = total + ref[...].astype(jnp.float32)
    refs[-1][...] = total.astype(refs[-1].dtype)


def add_pieces(near, got, moved, index):
    tall = near.shape[0] // 4
    cols = near.shape[1]
    at = pl.BlockSpec((tall, cols), lambda i: (index, 0))
    return pl.pallas_call(
        add_rows_kernel,
        grid=(1,),
        in_specs=[at, at] + [whole((tall, cols))] * len(moved),
        out_specs=whole((tall, cols)),
        out_shape=jax.ShapeDtypeStruct((tall, cols), near.dtype),
        compiler_params=settings(),
        cost_estimate=light(),
        name="add_pieces",
    )(near, got, *moved)


def add_rows(near, got, index):
    return add_pieces(near, got, (), index)


def add_three(near, got, moved, index):
    return add_pieces(near, got, (moved,), index)


def add_four(near, got, first, second, index):
    return add_pieces(near, got, (first, second), index)


def partial_three_kernel(query_ref, key_ref, value_ref, weight_ref, near_ref, far_ref):
    rows = near_ref.shape[0]
    depth = query_ref.shape[1]
    for at, out in ((pl.ds(rows, rows), far_ref), (pl.ds(0, rows), near_ref)):
        total = nn_dot(query_ref[at, :], weight_ref[pl.ds(0, depth), :])
        total = total + nn_dot(key_ref[at, :], weight_ref[pl.ds(depth, depth), :])
        total = total + nn_dot(value_ref[at, :], weight_ref[pl.ds(2 * depth, depth), :])
        out[...] = total.astype(out.dtype)


def partial_three(query, key, value, weight):
    rows, depth = query.shape
    cols = weight.shape[1]
    half = rows // 2
    return pl.pallas_call(
        partial_three_kernel,
        grid=(cols // WIDE,),
        in_specs=[whole((rows, depth))] * 3 + [pl.BlockSpec((3 * depth, WIDE), lambda i: (0, i))],
        out_specs=[pl.BlockSpec((half, WIDE), lambda i: (0, i))] * 2,
        out_shape=[
            jax.ShapeDtypeStruct((half, cols), jnp.float32),
            jax.ShapeDtypeStruct((half, cols), jnp.bfloat16),
        ],
        compiler_params=settings(),
        cost_estimate=light(),
        name="partial_three",
    )(query, key, value, weight)


def rows_call(kernel, name, grid_rows, ins, outs, sums=0):
    tall = 128
    cols = 2048
    steps = grid_rows // tall

    def spec(array, first):
        if first is None:
            return pl.BlockSpec(array.shape, lambda i: (0, 0))
        return pl.BlockSpec((tall, cols), lambda i: (first * steps + i, 0))

    out_specs = [pl.BlockSpec((tall, cols), lambda i: (i, 0)) for _ in outs]
    out_shape = [jax.ShapeDtypeStruct((grid_rows, cols), kind) for kind in outs]
    if sums:
        out_specs.append(pl.BlockSpec((8, cols), lambda i: (0, 0)))
        out_shape.append(jax.ShapeDtypeStruct((8, cols), jnp.float32))
    return pl.pallas_call(
        kernel,
        grid=(steps,),
        in_specs=[spec(array, first) for array, first in ins],
        out_specs=out_specs,
        out_shape=out_shape,
        compiler_params=settings(),
        cost_estimate=light(),
        name=name,
    )(*[array for array, _ in ins])


def wide(ref):
    return ref[...].astype(jnp.float32)


def norm_in_kernel(rows_ref, gain_ref, shift_ref, out_ref):
    normed, _ = normalize(wide(rows_ref))
    out_ref[...] = (normed * gain_ref[...] + shift_ref[...]).astype(out_ref.dtype)


def norm_in(tok, m, gain, shift_by):
    return rows_call(
        norm_in_kernel, "norm_in", tok.shape[0] // 2, [(tok, m), (gain, None), (shift_by, None)], [jnp.bfloat16]
    )[0]


def resid_kernel(rows_ref, kept_ref, got_ref, bias_ref, gain_ref, shift_ref, resid_ref, out_ref):
    resid = wide(rows_ref) + kept_ref[...] + wide(got_ref) + bias_ref[...]
    resid_ref[...] = resid
    normed, _ = normalize(resid.astype(jnp.bfloat16).astype(jnp.float32))
    out_ref[...] = (normed * gain_ref[...] + shift_ref[...]).astype(out_ref.dtype)


def resid_norm(tok, m, kept, got, bias, gain, shift_by):
    ins = [(tok, m), (kept, 0), (got, 0), (bias, None), (gain, None), (shift_by, None)]
    return rows_call(resid_kernel, "resid_norm", kept.shape[0], ins, [jnp.float32, jnp.bfloat16])


def layer_kernel(resid_ref, kept_ref, got_ref, bias_ref, out_ref):
    out_ref[...] = (resid_ref[...] + kept_ref[...] + wide(got_ref) + bias_ref[...]).astype(out_ref.dtype)


def layer_rows_of(resid, kept, got, bias):
    ins = [(resid, 0), (kept, 0), (got, 0), (bias, None)]
    return rows_call(layer_kernel, "layer_rows", kept.shape[0], ins, [jnp.bfloat16])[0]


def add_sums(sums_ref, parts):
    @pl.when(pl.program_id(0) == 0)
    def _():
        sums_ref[...] = jnp.zeros_like(sums_ref)

    for index, part in enumerate(parts):
        sums_ref[index : index + 1, :] += jnp.sum(part, axis=0, keepdims=True)


def norm_back_rows(grad, normed, inverse, gain):
    scaled = grad * gain
    first_mean = jnp.mean(scaled, axis=1, keepdims=True)
    second_mean = jnp.mean(scaled * normed, axis=1, keepdims=True)
    return inverse * (scaled - first_mean - normed * second_mean)


def second_back_kernel(kept_ref, got_ref, resid_ref, cot_ref, gain_ref, grad_ref, low_ref, sums_ref):
    grad = (kept_ref[...] + wide(got_ref)).astype(jnp.bfloat16).astype(jnp.float32)
    normed, inverse = normalize(resid_ref[...].astype(jnp.bfloat16).astype(jnp.float32))
    cot = wide(cot_ref)
    total = cot + norm_back_rows(grad, normed, inverse, gain_ref[...])
    grad_ref[...] = total
    low_ref[...] = total.astype(low_ref.dtype)
    add_sums(sums_ref, (total, cot, grad * normed, grad))


def second_back_rows(kept, got, resid, cot, m, gain):
    ins = [(kept, 0), (got, 0), (resid, 0), (cot, m), (gain, None)]
    return rows_call(second_back_kernel, "second_back", kept.shape[0], ins, [jnp.float32, jnp.bfloat16], sums=4)


def first_back_kernel(kept_ref, got_ref, rows_ref, resid_grad_ref, gain_ref, out_ref, sums_ref):
    grad = (kept_ref[...] + wide(got_ref)).astype(jnp.bfloat16).astype(jnp.float32)
    normed, inverse = normalize(wide(rows_ref))
    back = norm_back_rows(grad, normed, inverse, gain_ref[...])
    out_ref[...] = (resid_grad_ref[...] + back).astype(out_ref.dtype)
    add_sums(sums_ref, (grad * normed, grad))


def first_back_rows(kept, got, tok, m, resid_grad, gain):
    ins = [(kept, 0), (got, 0), (tok, m), (resid_grad, 0), (gain, None)]
    return rows_call(first_back_kernel, "first_back", kept.shape[0], ins, [jnp.bfloat16], sums=2)


def middle_kernel(near_top, near_low, got_top, got_low, kept_ref, moving_ref):
    kept_ref[...] = near_top[...] + wide(got_top)
    moving_ref[...] = (near_low[...] + wide(got_low)).astype(moving_ref.dtype)


def middle_rows(near, got):
    ins = [(near, 0), (near, 1), (got, 0), (got, 1)]
    return rows_call(middle_kernel, "middle_rows", near.shape[0] // 2, ins, [jnp.float32, jnp.bfloat16])


def join_kernel(count, *refs):
    sources, out_ref = refs[:count], refs[count]
    offset = 0
    for source in sources:
        rows = source.shape[0]
        out_ref[pl.ds(offset, rows), :] = source[...]
        offset += rows


def join_rows(arrays):
    count = len(arrays)
    rows = sum(array.shape[0] for array in arrays)
    cols = arrays[0].shape[1]
    chunk = cols // 4
    return pl.pallas_call(
        functools.partial(join_kernel, count),
        grid=(4,),
        in_specs=[pl.BlockSpec((array.shape[0], chunk), lambda i: (0, i)) for array in arrays],
        out_specs=pl.BlockSpec((rows, chunk), lambda i: (0, i)),
        out_shape=jax.ShapeDtypeStruct((rows, cols), arrays[0].dtype),
        compiler_params=settings(),
        cost_estimate=light(),
        name="join_rows",
    )(*arrays)


def attn_join_kernel(count, *refs):
    sources, qkv_ref, out_w_ref, bias_ref = refs[:count], *refs[count:]
    rows = HEAD_DIM
    for index, source in enumerate(sources):
        for k in range(3):
            qkv_ref[pl.ds((k * count + index) * rows, rows), :] = source[pl.ds(k * rows, rows), :]
        out_w_ref[pl.ds(index * rows, rows), :] = source[pl.ds(3 * rows, rows), :]
        bias_ref[pl.ds(index * 8, 8), :] = source[pl.ds(4 * rows, 8), :]


def attn_join(arrays):
    count = len(arrays)
    cols = arrays[0].shape[1]
    kind = arrays[0].dtype
    chunk = cols // 4
    sizes = (3 * count * HEAD_DIM, count * HEAD_DIM, count * 8)
    return pl.pallas_call(
        functools.partial(attn_join_kernel, count),
        grid=(4,),
        in_specs=[pl.BlockSpec((array.shape[0], chunk), lambda i: (0, i)) for array in arrays],
        out_specs=[pl.BlockSpec((size, chunk), lambda i: (0, i)) for size in sizes],
        out_shape=[jax.ShapeDtypeStruct((size, cols), kind) for size in sizes],
        compiler_params=settings(),
        cost_estimate=light(),
        name="attn_join",
    )(*arrays)


def cross_pair_kernel(rights, *refs):
    out_ref = refs[-1]
    lefts, right_refs = refs[:4], refs[4:-1]
    for which in range(2):
        right = right_refs[:4] if rights == 1 or which == 0 else right_refs[4:]
        near_a, far_a, near_b, far_b = right
        left_a, left_b = lefts[2 * which], lefts[2 * which + 1]
        rows = near_a.shape[0]
        top, low = pl.ds(0, rows), pl.ds(rows, rows)
        total = tn_dot(left_a[top, :], near_a[...]) + tn_dot(left_a[low, :], far_a[...])
        total = total + tn_dot(left_b[top, :], near_b[...]) + tn_dot(left_b[low, :], far_b[...])
        total = total.astype(out_ref.dtype)
        for piece in range(total.shape[0] // HEAD_DIM):
            at = pl.ds((2 * piece + which) * HEAD_DIM, HEAD_DIM)
            out_ref[at, :] = total[piece * HEAD_DIM : (piece + 1) * HEAD_DIM, :]


def cross_pair(first, second, rights, half):
    rows = first[0].shape[0]
    cols = rights[0][0].shape[1]
    tall = first[0].shape[1] // 2
    wide_cols = 1024
    left_spec = pl.BlockSpec((rows, tall), lambda i: (0, half))
    right_spec = pl.BlockSpec((rows // 2, wide_cols), lambda i: (0, i))
    flat = [array for right in rights for array in right]
    return pl.pallas_call(
        functools.partial(cross_pair_kernel, len(rights)),
        grid=(cols // wide_cols,),
        in_specs=[left_spec] * 4 + [right_spec] * len(flat),
        out_specs=pl.BlockSpec((2 * tall, wide_cols), lambda i: (0, i)),
        out_shape=jax.ShapeDtypeStruct((2 * tall, cols), jnp.bfloat16),
        compiler_params=settings(),
        cost_estimate=light(),
        name="cross_pair",
    )(*first, *second, *flat)


SWAP = [(0, 1), (1, 0)]
PLANE = ("y", "x", "core")
EVERY = ("z", "y", "x", "core")
MICRO = 2
SLOTS = 72


def after(value, *others):
    return lax.optimization_barrier((value, *others))[0]


class Order:

    def __init__(self):
        self.last = ()

    def take(self, value):
        return lax.optimization_barrier((value, self.last))[0]

    def mark(self, value):
        self.last = value
        return value

    def step(self, value):
        return self.mark(self.take(value))


def swap_along(array, axis):
    return lax.ppermute(array, axis, SWAP)


def shift(array, step):
    size = lax.axis_size("z")
    return lax.ppermute(array, "z", [(i, (i + step) % size) for i in range(size)])


def joined(arrays):
    return jnp.concatenate(arrays, axis=0)


def plane_start(piece):
    return (piece, swap_along(piece, "x"), swap_along(piece, "y"))


def plane_middle(started, order):
    piece, by_x, by_y = started
    half = piece.shape[0] // 2
    by_x, by_y = order.step((by_x, by_y))
    return (piece, by_x, by_y, swap_along(by_y[:half], "x"), swap_along(by_x[half:], "y"))


def plane_end(started, order):
    piece, by_x, by_y, corner_top, corner_low = started
    near = order.mark(join_rows([piece, by_x, by_y, *order.take((corner_top, corner_low))]))
    return (near, swap_along(near, "core"))


def held_before(bound, residue, parts):
    return (bound + (parts - 1) - residue) // parts


def piece_tables(lengths, starts, quarter_low, quarter_rows, residue, parts):
    ends = running_sum(lengths)
    firsts = ends - lengths
    shift = starts - firsts
    low = jnp.maximum(firsts, quarter_low)
    high = jnp.minimum(ends, quarter_low + quarter_rows)
    begin = held_before(low + shift, residue, parts)
    count = jnp.where(high > low, held_before(high + shift, residue, parts) - begin, 0)
    return (begin, count, shift)


def slot_lookup(begin, count, value_of):
    base = running_sum(count) - count
    slot = jnp.arange(SLOTS, dtype=jnp.int32)
    inside = (slot >= base[..., None]) & (slot < (base + count)[..., None])
    held = begin[..., None] + slot - base[..., None]
    return jnp.sum(jnp.where(inside, value_of(held) + 1, 0), axis=-2, dtype=jnp.int32) - 1


def layer(
    tokens,
    cotangent,
    lengths,
    dealing,
    query_weight,
    key_weight,
    value_weight,
    out_weight,
    query_bias,
    value_bias,
    out_bias,
    up_weight,
    up_bias,
    down_weight,
    down_bias,
    attn_gain,
    attn_shift,
    mlp_gain,
    mlp_shift,
):
    tok_rows = tokens.shape[1]
    col_width = tokens.shape[2]
    width = out_weight.shape[1]
    seq_dev = lengths.shape[2]
    depth = lax.axis_size("z")
    parts = lax.axis_size("y") * 4
    own_rows = tok_rows // 4
    y, x, core, z = (lax.axis_index(name) for name in ("y", "x", "core", "z"))
    team = 2 * x + core
    eighth = 2 * team + y
    residue = 4 * y + team
    group = 2 * z + y

    given_off = []
    for micro_step in range(MICRO):
        given_off.append(given_layout(lengths[micro_step], dealing[micro_step])[2])
    starts = jnp.stack(given_off).reshape(lengths.shape)
    quarter_low = (jnp.arange(4, dtype=jnp.int32) * own_rows)[None, None, :, None]
    begin, count, _ = piece_tables(
        lengths[:, :, None, :], starts[:, :, None, :], quarter_low, own_rows, residue, parts
    )
    micro_ids = jnp.arange(MICRO, dtype=jnp.int32)[:, None, None, None]
    begin = jnp.transpose(begin + micro_ids * tok_rows, (1, 2, 0, 3)).reshape(-1, MICRO * seq_dev)
    count = jnp.transpose(count, (1, 2, 0, 3)).reshape(-1, MICRO * seq_dev)
    send_row = slot_lookup(begin, count, lambda held: held).reshape(-1)

    my_lengths = lax.dynamic_index_in_dim(lengths, group, 1, keepdims=False)
    my_starts = lax.dynamic_index_in_dim(starts, group, 1, keepdims=False)
    residues = jnp.arange(parts, dtype=jnp.int32)[:, None, None]
    my_begin, my_count, my_shift = piece_tables(
        my_lengths[None], my_starts[None], team * own_rows, own_rows, residues, parts
    )
    flat = (parts, MICRO * seq_dev)
    row_shift = (
        my_shift + team * own_rows - jnp.arange(MICRO, dtype=jnp.int32)[None, :, None] * own_rows
    )
    row_shift = jnp.broadcast_to(row_shift, my_count.shape).reshape(flat)
    own_row = slot_lookup(
        my_begin.reshape(flat),
        my_count.reshape(flat),
        lambda held: held * parts + residues - row_shift[..., None],
    ).reshape(-1)
    head_rows = HEAD_DIM
    half_units = up_weight.shape[1] // 8

    shard_heads = query_weight.shape[1]

    def bias_rows(half):
        row = jnp.concatenate(
            [
                lax.dynamic_slice_in_dim(bias, (2 * team + half) * size, size)
                for bias, size in ((query_bias, HEAD_DIM), (value_bias, HEAD_DIM), (up_bias, half_units))
            ]
        )
        return jnp.pad(row[None, :], ((0, 7), (0, width - row.shape[0])))

    attn_mine, attn_other = attn_pack(
        query_weight, key_weight, value_weight, out_weight, bias_rows(y), bias_rows(1 - y), team, y
    )
    blocks = half_units // 128
    up_mine = flipped(up_weight, (2 * team + y) * blocks, blocks)
    up_other = flipped(up_weight, (2 * team + 1 - y) * blocks, blocks)
    down_mine = lax.dynamic_slice_in_dim(down_weight, (2 * team + y) * half_units, half_units, 0)
    down_other = lax.dynamic_slice_in_dim(down_weight, (2 * team + 1 - y) * half_units, half_units, 0)

    order = Order()

    def spread_out(array):
        spread = array.reshape(MICRO, tok_rows // parts, parts, col_width)
        spread = lax.all_to_all(spread, PLANE, split_axis=2, concat_axis=1, tiled=True)
        return spread.reshape(MICRO * tok_rows, col_width)

    def box_exchange(sent):
        return lax.all_to_all(sent, EVERY, split_axis=0, concat_axis=0, tiled=True)

    def boxes(spread):
        return pick_rows(send_row, spread, 384)

    def settle(got):
        return settle_rows(own_row, got.reshape(depth, parts * SLOTS, col_width), MICRO * own_rows)

    gain_one, shift_one, gain_two, shift_two, out_b, down_b = (
        array.astype(jnp.float32)[None, :]
        for array in (attn_gain, attn_shift, mlp_gain, mlp_shift, out_bias, down_bias)
    )

    rank = jnp.full((1,), team, jnp.int32)
    infos = []
    for micro_step in range(MICRO):
        holder, position, _ = buffer_layout(my_lengths[micro_step], my_starts[micro_step], tok_rows)
        segment = holder * tok_rows + position // (SEG + SUMM)
        summary = jnp.where(position % (SEG + SUMM) >= SEG, holder, -1)
        infos.append((jnp.stack([segment, summary], axis=1), jnp.stack([segment, holder], axis=0)))

    def up_down(piece):
        piece = order.take(piece)
        return (shift(piece, 1), shift(piece, -1))

    def onward(piece):
        piece = order.step(piece)
        return (piece, shift(piece, 1), swap_along(piece, "y"))

    def swapped(piece):
        piece = order.step(piece)
        return (piece, swap_along(piece, "y"))

    def team_start(rows):
        return (rows, swap_along(rows, "x"))

    def team_middle(started):
        own, by_x = started
        near = order.mark(join_rows([own, order.take(by_x)]))
        return (near, swap_along(near, "core"))

    def team_end(started):
        near, far = started
        return (near, order.step(far))

    def sum_start(left, weight):
        near, far = order.mark(partial_sums(order.take(left), weight))
        return (near, swap_along(far, "core"))

    def sum_middle(started):
        near, got = started
        kept, moving = order.mark(middle_rows(near, order.take(got)))
        return (kept, swap_along(moving, "x"))

    def sum_end(started):
        kept, got = started
        return (kept, order.take(got))

    def unsettle(array):
        return unsettle_rows(own_row, array, depth).reshape(-1, col_width)

    def unbox(got):
        return drop_rows(send_row, got, MICRO * tok_rows, 256)

    def spread_back(held):
        held = held.reshape(MICRO, tok_rows, 1, col_width)
        back = lax.all_to_all(held, PLANE, split_axis=1, concat_axis=2, tiled=True)
        return back.reshape(MICRO, tok_rows, col_width)

    order.mark(attn_mine)
    attn_1 = shift(attn_mine, 1)
    tok_spread = spread_out(tokens)
    attn_1 = order.step(attn_1)
    attn_2 = shift(attn_1, 1)
    attn_y1 = swap_along(attn_1, "y")
    tok_spread = order.step(tok_spread)
    attn_2 = order.step(attn_2)
    attn_3 = shift(order.take(attn_mine), -1)
    attn_y2 = swap_along(attn_2, "y")
    tok_sent = order.mark(boxes(order.take(tok_spread)))
    tok_got = box_exchange(tok_sent)
    attn_3, attn_y3 = swapped(attn_3)
    tok = order.mark(settle(order.take(tok_got)))
    up_1, up_3 = up_down(up_mine)
    cot_spread = spread_out(after(cotangent, tok))

    first_a = team_start(order.mark(norm_in(tok, 0, gain_one, shift_one)))
    first_b = team_start(order.mark(norm_in(order.take(tok), 1, gain_one, shift_one)))
    attn_all = [attn_mine, attn_1, attn_2, attn_3, attn_other, *order.take((attn_y1, attn_y2, attn_y3))]
    qkv_w, out_w, bias_w = order.mark(attn_join(attn_all))
    bias_w = bias_w.reshape(2 * depth, 8, width)[:, 0, :].astype(jnp.float32)
    query_b = bias_w[:, :head_rows].reshape(1, -1)
    value_b = bias_w[:, head_rows : 2 * head_rows].reshape(1, -1)
    up_b = bias_w[:, 2 * head_rows : 2 * head_rows + half_units].reshape(1, -1)
    qkv_b = jnp.concatenate([query_b, jnp.zeros_like(query_b), value_b], axis=1)
    no_b = jnp.zeros((1, out_w.shape[0]), jnp.float32)

    first_a = team_middle(first_a)
    cot_sent = order.mark(boxes(order.take(cot_spread)))
    first_a = team_end(first_a)
    up_1, up_2, up_y1 = onward(up_1)
    up_3, up_y3 = swapped(up_3)
    qkv_a = order.mark(project(*order.take(first_a), qkv_w, qkv_b))
    mixed_a = order.mark(attend(order.take(qkv_a), rank, *infos[0]))
    up_y1 = order.step(up_y1)
    up_2, up_y2 = swapped(up_2)
    down_1, down_3 = up_down(down_mine)
    first_b = team_middle(first_b)
    sum_a1 = sum_start(mixed_a, out_w)
    first_b = team_end(first_b)
    qkv_b_ = order.mark(project(*order.take(first_b), qkv_w, qkv_b))
    up_y3 = order.step(up_y3)
    sum_a1 = sum_middle(sum_a1)
    mixed_b = order.mark(attend(order.take(qkv_b_), rank, *infos[1]))
    up_y2 = order.step(up_y2)
    down_1, down_2, down_y1 = onward(down_1)
    resid_a, second_a = order.mark(resid_norm(tok, 0, *sum_end(sum_a1), out_b, gain_two, shift_two))
    second_a = team_start(second_a)
    down_3, down_y3 = swapped(down_3)
    sum_b1 = sum_start(mixed_b, out_w)
    up_w = order.mark(join_rows([up_mine, up_1, up_2, up_3, up_other, *order.take((up_y1, up_y2, up_y3))]))
    sum_b1 = sum_middle(sum_b1)
    down_y1 = order.step(down_y1)
    second_a = team_middle(second_a)
    cot_got = box_exchange(order.take(cot_sent))
    second_a = team_end(second_a)

    hidden_a, slope_a = order.mark(expand(*order.take(second_a), up_w, up_b))
    down_2, down_y2 = swapped(down_2)
    down_y3 = order.step(down_y3)
    resid_b, second_b = order.mark(resid_norm(tok, 1, *sum_end(sum_b1), out_b, gain_two, shift_two))
    second_b = team_start(second_b)
    cot = order.mark(settle(order.take(cot_got)))
    cot_own = cot.reshape(MICRO, own_rows, width)
    second_b = team_middle(second_b)
    cot_parts = [team_start(cot_own[m]) for m in range(MICRO)]
    second_b = team_end(second_b)
    hidden_b, slope_b = order.mark(expand(*order.take(second_b), up_w, up_b))
    down_w = order.mark(
        join_rows([down_mine, down_1, down_2, down_3, down_other, *order.take((down_y1, down_y2, down_y3))])
    )
    sum_a4 = sum_start(hidden_a, down_w)
    cot_parts[0] = team_middle(cot_parts[0])
    sum_b4 = sum_start(hidden_b, down_w)
    cot_a = team_end(cot_parts[0])

    low_a, up_sum_a = order.mark(expand_back(*order.take(cot_a), down_w, slope_a))
    cot_parts[1] = team_middle(cot_parts[1])
    sum_a2 = sum_start(low_a, up_w)
    cot_b = team_end(cot_parts[1])
    low_b, up_sum_b = order.mark(expand_back(*order.take(cot_b), down_w, slope_b))
    up_sum_a, up_sum_b = up_sum_a[0], up_sum_b[0]
    sum_a2 = sum_middle(sum_a2)
    sum_b2 = sum_start(low_b, up_w)

    def cross_half(left_a, right_a, left_b, right_b, half):
        size = left_a.shape[1] // 2
        return order.mark(cross_sums(order.take(left_a), right_a, left_b, right_b, half * size, size))

    down_far = cross_half(hidden_a, cot_a, hidden_b, cot_b, 1)
    down_swap = swap_along(down_far, "y")
    sum_b2 = sum_middle(sum_b2)

    def second_back(started, resid, m):
        return order.mark(second_back_rows(*sum_end(started), resid, cot, m, gain_two))

    resid_grad_a, attn_low_a, norm_sums_a = second_back(sum_a2, resid_a, 0)
    attn_low_a = team_start(attn_low_a)
    down_near = cross_half(hidden_a, cot_a, hidden_b, cot_b, 0)
    resid_grad_b, attn_low_b, norm_sums_b = second_back(sum_b2, resid_b, 1)
    attn_low_b = team_start(attn_low_b)
    sum_a4 = sum_middle(sum_a4)
    up_far = cross_half(low_a, second_a, low_b, second_b, 1)
    attn_low_a = team_middle(attn_low_a)
    sum_b4 = sum_middle(sum_b4)
    attn_low_a = team_end(attn_low_a)

    def ring_start(near, got):
        got = order.take(got)
        far_2 = order.mark(add_rows(near, got, 2))
        move = shift(far_2, 1)
        far_1 = order.mark(add_rows(near, order.take(got), 1))
        back = shift(far_1, -1)
        return (near, got, move, back)

    def ring_middle(started):
        near, got, move, back = started
        far_3 = order.mark(add_three(near, got, order.take(move), 3))
        return (near, got, shift(far_3, 1), back)

    def ring_end(started):
        near, got, move, back = started
        move, back = order.take((move, back))
        return order.mark(add_four(near, got, move, back, 0))

    def attn_back(attn_low, qkv, m):
        mixed_grad = order.mark(project(*order.take(attn_low), out_w, no_b))
        return order.mark(attend_back(qkv, order.take(mixed_grad), rank, *infos[m]))

    def sum_start_three(lefts, weight):
        near, far = order.mark(partial_three(*order.take(lefts), weight))
        return (near, swap_along(far, "core"))

    *lows_a, sums_a = attn_back(attn_low_a, qkv_a, 0)
    attn_low_b = team_middle(attn_low_b)
    down_ring = ring_start(down_near, down_swap)
    up_swap = swap_along(order.take(up_far), "y")
    sum_a3 = sum_start_three(lows_a, qkv_w)
    attn_low_b = team_end(attn_low_b)
    up_near = cross_half(low_a, second_a, low_b, second_b, 0)
    sum_a3 = sum_middle(sum_a3)
    layer_a = order.mark(layer_rows_of(resid_a, *sum_end(sum_a4), down_b))
    layer_b = order.mark(layer_rows_of(resid_b, *sum_end(sum_b4), down_b))
    layer_sent = order.mark(unsettle(join_rows([layer_a, layer_b])))
    down_ring = ring_middle(down_ring)
    layer_got = box_exchange(order.take(layer_sent))

    def pack_small():
        slots = jnp.arange(8 * depth, dtype=jnp.int32)
        index = jnp.arange(2 * depth, dtype=jnp.int32)
        owner = lax.rem(z - index % depth + depth, depth)
        flip = jnp.where(index < depth, y, 1 - y)
        hot = (slots[:, None] == (owner * 8 + 2 * team + flip)[None, :]).astype(jnp.float32)

        def place(vector):
            local = vector.reshape(2 * depth, -1)
            return jnp.dot(hot, local, precision=lax.Precision.HIGHEST).reshape(-1)

        head_sums = sums_a + sums_b
        norm_sums = norm_sums_a + norm_sums_b
        back_sums = back_sums_a + back_sums_b
        return jnp.concatenate(
            [
                place(head_sums[0]),
                place(head_sums[1]),
                place(up_sum_a + up_sum_b),
                norm_sums[:4].reshape(-1),
                back_sums[:2].reshape(-1),
            ]
        ).reshape(-1, 128)

    def ring_start(near, got):
        piece = near.shape[0] // depth
        got = order.take(got)
        far_2 = order.mark(add_rows(near, got, 2))
        move = shift(far_2, 1)
        far_1 = order.mark(add_rows(near, order.take(got), 1))
        back = shift(far_1, -1)
        return (near, got, move, back)

    def ring_middle(started):
        near, got, move, back = started
        far_3 = order.mark(add_three(near, got, order.take(move), 3))
        return (near, got, shift(far_3, 1), back)

    def ring_end(started):
        near, got, move, back = started
        move, back = order.take((move, back))
        return order.mark(add_four(near, got, move, back, 0))

    *lows_b, sums_b = attn_back(attn_low_b, qkv_b_, 1)
    def first_back(started, resid_grad, m):
        return order.mark(first_back_rows(*sum_end(started), tok, m, resid_grad, gain_one))

    firsts = (*first_a, *first_b)

    def one_half(half):
        lefts = order.take((lows_a[0], lows_b[0]))
        return order.mark(cross_pair(lefts, (lows_a[1], lows_b[1]), (firsts,), half))

    def two_half(half):
        lefts = order.take((lows_a[2], lows_b[2]))
        rights = (firsts, (*attn_low_a, *attn_low_b))
        return order.mark(cross_pair(lefts, (mixed_a, mixed_b), rights, half))

    input_a, back_sums_a = first_back(sum_a3, resid_grad_a, 0)
    up_ring = ring_start(up_near, up_swap)
    sum_b3 = sum_start_three(lows_b, qkv_w)
    one_far = one_half(1)
    one_swap = swap_along(one_far, "y")
    sum_b3 = sum_middle(sum_b3)
    two_far = two_half(1)
    two_swap = swap_along(two_far, "y")
    layer_held = order.mark(unbox(order.take(layer_got)))
    layer_out = spread_back(layer_held)
    one_near = one_half(0)
    down_total = ring_end(down_ring)
    down_plane = plane_start(down_total)
    up_ring = ring_middle(up_ring)
    input_b, back_sums_b = first_back(sum_b3, resid_grad_b, 1)
    input_sent = order.mark(unsettle(join_rows([input_a, input_b])))
    one_ring = ring_start(one_near, one_swap)
    layer_out = order.step(layer_out)
    input_got = box_exchange(order.take(input_sent))
    two_near = two_half(0)
    up_total = ring_end(up_ring)
    up_plane = plane_start(up_total)
    one_ring = ring_middle(one_ring)
    two_ring = ring_start(two_near, two_swap)
    down_plane = plane_middle(down_plane, order)
    small = order.mark(order.take(pack_small()))
    small_got = swap_along(small, "core")
    one_total = ring_end(one_ring)
    one_plane = plane_start(one_total)
    two_ring = ring_middle(two_ring)
    small = order.mark(small + order.take(small_got))
    small_got = swap_along(small, "x")
    down_plane = plane_end(down_plane, order)
    own = jnp.full((1,), eighth, jnp.int32)
    down_grad = order.mark(stack_pieces(*order.take(down_plane), own, False))
    input_held = order.mark(unbox(order.take(input_got)))
    input_grad = spread_back(input_held)
    up_plane = plane_middle(up_plane, order)
    two_total = ring_end(two_ring)
    two_plane = plane_start(two_total)
    small = order.mark(small + order.take(small_got))
    small_got = swap_along(small, "y")
    up_plane = plane_end(up_plane, order)
    one_plane = plane_middle(one_plane, order)
    up_grad = order.mark(stack_pieces(*order.take(up_plane), own, True))
    two_plane = plane_middle(two_plane, order)
    small = order.mark(small + order.take(small_got))
    small_got = lax.ppermute(small, "z", [(i, i ^ 1) for i in range(depth)])
    one_plane = plane_end(one_plane, order)
    input_grad = order.step(input_grad)
    query_grad, key_grad = order.mark(stack_heads(*order.take(one_plane), own, (True, True)))
    small = order.mark(small + order.take(small_got))
    small_got = lax.ppermute(small, "z", [(i, i ^ 2) for i in range(depth)])
    two_plane = plane_end(two_plane, order)
    value_grad, out_w_grad = order.mark(stack_heads(*order.take(two_plane), own, (True, False)))
    packed = small + order.take(small_got)
    packed = packed.reshape(-1)
    pieces = []
    offset = 0
    heads_all = depth * shard_heads
    for size in (heads_all, heads_all, depth * up_weight.shape[1]) + (width,) * 6:
        pieces.append(packed[offset : offset + size])
        offset += size
    query_b_grad, value_b_grad, up_b_grad, out_b_grad, down_b_grad, gain_two_g, shift_two_g, *norm_grads = pieces
    norm_grads = norm_grads + [gain_two_g, shift_two_g]

    def own_shard(vector):
        size = vector.shape[0] // depth
        return lax.dynamic_slice_in_dim(vector, z * size, size)

    return (
        layer_out,
        input_grad,
        query_grad,
        key_grad,
        value_grad,
        out_w_grad,
        own_shard(query_b_grad),
        own_shard(value_b_grad),
        out_b_grad,
        up_grad,
        own_shard(up_b_grad),
        down_grad,
        down_b_grad,
        *norm_grads,
    )


def team_layer(mesh):
    axes = ("y", "x", "core", "z")
    inner = Mesh(mesh.devices.reshape(2, 2, 2, 4), axes)
    rows = P(None, PLANE, "z")
    in_specs = (
        rows, rows, P(), P(), P(None, "z"), P(None, "z"), P(None, "z"), P("z", None), P("z"), P("z"),
        P(), P(None, "z"), P("z"), P("z", None), P(), P(), P(), P(), P(),
    )
    out_specs = (
        rows, rows, P(None, "z"), P(None, "z"), P(None, "z"), P("z", None), P("z"), P("z"),
        P(), P(None, "z"), P("z"), P("z", None), P(), P(), P(), P(), P(),
    )
    return jax.shard_map(layer, mesh=inner, in_specs=in_specs, out_specs=out_specs, check_vma=False)


def solution(mesh):
    if dict(mesh.shape) == {"dp": 8, "tensor": 4}:
        return team_layer(mesh)
    return general_layer(mesh)
```

```python
import functools

import jax
import jax.numpy as jnp
from jax import lax
from jax.experimental import pallas as pl
from jax.experimental.pallas import tpu as pltpu
from jax.sharding import Mesh
from jax.sharding import PartitionSpec as P


HEAD_DIM = 64
SEG = 512
SUMM = 50
NBLK = 2


NORM_EPS = 1e-05
MASKED = -1e30


def gelu_tanh(values):
    return jax.nn.gelu(values, approximate=True)


def matmul(left_array, right_array):
    return jnp.dot(left_array, right_array, preferred_element_type=jnp.float32)


def cross_rows(left_array, right_array):
    return lax.dot_general(
        left_array, right_array, (((0,), (0,)), ((), ())), preferred_element_type=jnp.float32
    )


def times_transpose(left_array, right_array):
    return lax.dot_general(
        left_array, right_array, (((1,), (1,)), ((), ())), preferred_element_type=jnp.float32
    )


def normalize(values):
    center = jnp.mean(values, axis=1, keepdims=True)
    shifted = values - center
    spread = jnp.mean(shifted * shifted, axis=1, keepdims=True)
    inverse = lax.rsqrt(spread + NORM_EPS)
    return (shifted * inverse, inverse)


def norm_backward(grad_in, normed, inverse, gain_row):
    gain_grad = jnp.sum(grad_in * normed, axis=0)
    shift_grad = jnp.sum(grad_in, axis=0)
    scaled = grad_in * gain_row
    first_mean = jnp.mean(scaled, axis=1, keepdims=True)
    second_mean = jnp.mean(scaled * normed, axis=1, keepdims=True)
    return (inverse * (scaled - first_mean - normed * second_mean), gain_grad, shift_grad)


def running_sum(counts):
    size = counts.shape[-1]
    places = jnp.arange(size, dtype=jnp.int32)
    upto = (places[:, None] <= places[None, :]).astype(jnp.int32)
    return jnp.sum(counts[..., :, None] * upto, axis=-2, dtype=jnp.int32)


def given_layout(lengths_mb, dealing_mb):
    seq_count = dealing_mb.shape[0]
    labels = jnp.arange(seq_count, dtype=jnp.int32)
    flat_lengths = lengths_mb.reshape(seq_count)
    one_hot = (dealing_mb[:, None] == labels[None, :]).astype(jnp.int32)
    given_len = jnp.sum(one_hot * flat_lengths[None, :], axis=1, dtype=jnp.int32)
    given_off = running_sum(given_len) - given_len
    start_by_seq = jnp.sum(one_hot * given_off[:, None], axis=0, dtype=jnp.int32)
    return (given_len, given_off, start_by_seq)


def buffer_layout(lengths_dev, start_dev, rows_total):
    seq_count = lengths_dev.shape[0]
    end_rows = running_sum(lengths_dev)
    offsets = end_rows - lengths_dev
    row_ids = jnp.arange(rows_total, dtype=jnp.int32)
    holder = jnp.sum(
        (row_ids[:, None] >= end_rows[None, :]).astype(jnp.int32), axis=1, dtype=jnp.int32
    )
    one_hot = (holder[:, None] == jnp.arange(seq_count, dtype=jnp.int32)[None, :]).astype(jnp.int32)
    position = row_ids - jnp.sum(one_hot * offsets[None, :], axis=1, dtype=jnp.int32)
    source = jnp.sum(one_hot * start_dev[None, :], axis=1, dtype=jnp.int32) + position
    return (holder, position, source)


def visible(holder, position, first_row, last_row, key_reach):
    period = SEG + SUMM
    query_seq = holder[first_row:last_row, None]
    key_seq = holder[None, :key_reach]
    query_part = position[first_row:last_row, None] // period
    key_part = position[None, :key_reach] // period
    summary = position[None, :key_reach] % period >= SEG
    query_row = jnp.arange(first_row, last_row, dtype=jnp.int32)[:, None]
    key_row = jnp.arange(key_reach, dtype=jnp.int32)[None, :]
    same_part = (query_part == key_part) & (key_row <= query_row)
    earlier = (key_part < query_part) & summary
    return (query_seq == key_seq) & (same_part | earlier)


def block_scores(queries, keys_all, allowed, score_scale):
    scores = (
        jnp.einsum("qhd,khd->hqk", queries, keys_all, preferred_element_type=jnp.float32)
        * score_scale
    )
    return jnp.where(allowed[None], scores, MASKED)


def shards(
    tokens,
    cotangent,
    lengths,
    dealing,
    query_weight,
    key_weight,
    value_weight,
    out_weight,
    query_bias,
    value_bias,
    out_bias,
    up_weight,
    up_bias,
    down_weight,
    down_bias,
    attn_gain,
    attn_shift,
    mlp_gain,
    mlp_shift,
):
    micro_count = tokens.shape[0]
    tok_rows = tokens.shape[1]
    col_width = tokens.shape[2]
    seq_dev = lengths.shape[2]
    heads_here = query_weight.shape[1] // HEAD_DIM
    head_cols = heads_here * HEAD_DIM
    block_rows = tok_rows // NBLK
    score_scale = HEAD_DIM ** (-0.5)
    device = lax.axis_index("dp")
    column = lax.axis_index("tensor")
    gain_one = attn_gain.astype(jnp.float32)
    shift_one = attn_shift.astype(jnp.float32)
    gain_two = mlp_gain.astype(jnp.float32)
    shift_two = mlp_shift.astype(jnp.float32)
    query_bias_f = query_bias.astype(jnp.float32)
    value_bias_f = value_bias.astype(jnp.float32)
    up_bias_f = up_bias.astype(jnp.float32)
    out_bias_cols = lax.dynamic_slice_in_dim(
        out_bias.astype(jnp.float32), column * col_width, col_width
    )
    down_bias_cols = lax.dynamic_slice_in_dim(
        down_bias.astype(jnp.float32), column * col_width, col_width
    )
    query_w_grad = jnp.zeros(query_weight.shape, jnp.float32)
    key_w_grad = jnp.zeros(key_weight.shape, jnp.float32)
    value_w_grad = jnp.zeros(value_weight.shape, jnp.float32)
    out_w_grad = jnp.zeros(out_weight.shape, jnp.float32)
    query_b_grad = jnp.zeros(query_bias.shape, jnp.float32)
    value_b_grad = jnp.zeros(value_bias.shape, jnp.float32)
    out_b_grad = jnp.zeros(out_bias.shape, jnp.float32)
    up_w_grad = jnp.zeros(up_weight.shape, jnp.float32)
    up_b_grad = jnp.zeros(up_bias.shape, jnp.float32)
    down_w_grad = jnp.zeros(down_weight.shape, jnp.float32)
    down_b_grad = jnp.zeros(down_bias.shape, jnp.float32)
    gain_one_grad = jnp.zeros(attn_gain.shape, jnp.float32)
    shift_one_grad = jnp.zeros(attn_shift.shape, jnp.float32)
    gain_two_grad = jnp.zeros(mlp_gain.shape, jnp.float32)
    shift_two_grad = jnp.zeros(mlp_shift.shape, jnp.float32)
    layer_parts = []
    grad_parts = []
    for micro_step in range(micro_count):
        lengths_mb = lengths[micro_step]
        dealing_mb = dealing[micro_step]
        given_len, given_off, start_by_seq = given_layout(lengths_mb, dealing_mb)
        lengths_dev = lax.dynamic_index_in_dim(lengths_mb, device, 0, keepdims=False)
        start_dev = lax.dynamic_slice_in_dim(start_by_seq, device * seq_dev, seq_dev)
        holder, position, source = buffer_layout(lengths_dev, start_dev, tok_rows)
        blank_rows = jnp.zeros((tok_rows, col_width), jnp.bfloat16)
        pieces = (
            lax.all_gather(tokens[micro_step], "dp", axis=0, tiled=True),
            lax.all_gather(cotangent[micro_step], "dp", axis=0, tiled=True),
        )
        span_rows = pieces[0].shape[0]
        inside = ((source >= 0) & (source < span_rows))[:, None]
        fetch_at = jnp.clip(source, 0, span_rows - 1)
        tok_buf = jnp.where(inside, jnp.take(pieces[0], fetch_at, axis=0), blank_rows)
        cot_buf = jnp.where(inside, jnp.take(pieces[1], fetch_at, axis=0), blank_rows)
        tok_full, cot_full = (
            lax.all_gather(tok_buf, "tensor", axis=1, tiled=True),
            lax.all_gather(cot_buf, "tensor", axis=1, tiled=True),
        )
        normed_one, inverse_one = normalize(tok_full.astype(jnp.float32))
        first_in = (normed_one * gain_one + shift_one).astype(jnp.bfloat16)
        queries = (
            (matmul(first_in, query_weight) + query_bias_f)
            .astype(jnp.bfloat16)
            .reshape(tok_rows, heads_here, HEAD_DIM)
        )
        keys_here = (
            matmul(first_in, key_weight)
            .astype(jnp.bfloat16)
            .reshape(tok_rows, heads_here, HEAD_DIM)
        )
        values_here = (
            (matmul(first_in, value_weight) + value_bias_f)
            .astype(jnp.bfloat16)
            .reshape(tok_rows, heads_here, HEAD_DIM)
        )
        outputs = []
        row_tops = []
        row_totals = []
        for block_index in range(NBLK):
            row_lower = block_index * block_rows
            row_upper = row_lower + block_rows
            allowed = visible(holder, position, row_lower, row_upper, row_upper)
            scores = block_scores(
                queries[row_lower:row_upper], keys_here[:row_upper], allowed, score_scale
            )
            row_top = jnp.max(scores, axis=2, keepdims=True)
            exp_terms = jnp.exp(scores - row_top)
            row_total = jnp.sum(exp_terms, axis=2, keepdims=True)
            attn_prob = exp_terms / row_total
            outputs.append(
                jnp.einsum(
                    "hqk,khd->qhd",
                    attn_prob.astype(jnp.bfloat16),
                    values_here[:row_upper],
                    preferred_element_type=jnp.float32,
                )
            )
            row_tops.append(row_top)
            row_totals.append(row_total)
        mixed_heads = (
            jnp.concatenate(outputs, axis=0).reshape(tok_rows, head_cols).astype(jnp.bfloat16)
        )
        attn_cols = lax.psum_scatter(
            matmul(mixed_heads, out_weight), "tensor", scatter_dimension=1, tiled=True
        )
        resid_cols = tok_buf.astype(jnp.float32) + attn_cols + out_bias_cols
        resid_full = lax.all_gather(resid_cols.astype(jnp.bfloat16), "tensor", axis=1, tiled=True)
        normed_two, inverse_two = normalize(resid_full.astype(jnp.float32))
        second_in = (normed_two * gain_two + shift_two).astype(jnp.bfloat16)
        hidden_pre = matmul(second_in, up_weight) + up_bias_f
        hidden_act, gelu_pull = jax.vjp(gelu_tanh, hidden_pre)
        hidden = hidden_act.astype(jnp.bfloat16)
        mlp_cols = lax.psum_scatter(
            matmul(hidden, down_weight).astype(jnp.bfloat16),
            "tensor",
            scatter_dimension=1,
            tiled=True,
        ).astype(jnp.float32)
        layer_cols = (resid_cols + mlp_cols + down_bias_cols).astype(jnp.bfloat16)
        grad_out = cot_full.astype(jnp.float32)
        down_w_grad = down_w_grad + cross_rows(hidden, cot_full)
        down_b_grad = down_b_grad + jnp.sum(grad_out, axis=0)
        hidden_grad = gelu_pull(times_transpose(cot_full, down_weight))[0]
        up_b_grad = up_b_grad + jnp.sum(hidden_grad, axis=0)
        hidden_low = hidden_grad.astype(jnp.bfloat16)
        up_w_grad = up_w_grad + cross_rows(second_in, hidden_low)
        second_cols = lax.psum_scatter(
            times_transpose(hidden_low, up_weight), "tensor", scatter_dimension=1, tiled=True
        )
        second_grad = lax.all_gather(
            second_cols.astype(jnp.bfloat16), "tensor", axis=1, tiled=True
        ).astype(jnp.float32)
        resid_back, gain_part, shift_part = norm_backward(
            second_grad, normed_two, inverse_two, gain_two
        )
        gain_two_grad = gain_two_grad + gain_part
        shift_two_grad = shift_two_grad + shift_part
        resid_grad = grad_out + resid_back
        out_b_grad = out_b_grad + jnp.sum(resid_grad, axis=0)
        attn_low = resid_grad.astype(jnp.bfloat16)
        out_w_grad = out_w_grad + cross_rows(mixed_heads, attn_low)
        mixed_grad = (
            times_transpose(attn_low, out_weight)
            .astype(jnp.bfloat16)
            .reshape(tok_rows, heads_here, HEAD_DIM)
        )
        query_parts = []
        key_acc = jnp.zeros((tok_rows, heads_here, HEAD_DIM), jnp.float32)
        value_acc = jnp.zeros((tok_rows, heads_here, HEAD_DIM), jnp.float32)
        for block_index in range(NBLK):
            row_lower = block_index * block_rows
            row_upper = row_lower + block_rows
            allowed = visible(holder, position, row_lower, row_upper, row_upper)
            scores = block_scores(
                queries[row_lower:row_upper], keys_here[:row_upper], allowed, score_scale
            )
            attn_prob = jnp.exp(scores - row_tops[block_index]) / row_totals[block_index]
            grad_block = mixed_grad[row_lower:row_upper]
            prob_grad = jnp.einsum(
                "qhd,khd->hqk",
                grad_block,
                values_here[:row_upper],
                preferred_element_type=jnp.float32,
            )
            inner_sum = jnp.sum(attn_prob * prob_grad, axis=2, keepdims=True)
            score_grad = (attn_prob * (prob_grad - inner_sum)).astype(jnp.bfloat16)
            query_parts.append(
                jnp.einsum(
                    "hqk,khd->qhd",
                    score_grad,
                    keys_here[:row_upper],
                    preferred_element_type=jnp.float32,
                )
                * score_scale
            )
            pad_rows = ((0, tok_rows - row_upper), (0, 0), (0, 0))
            key_acc = key_acc + jnp.pad(
                jnp.einsum(
                    "hqk,qhd->khd",
                    score_grad,
                    queries[row_lower:row_upper],
                    preferred_element_type=jnp.float32,
                )
                * score_scale,
                pad_rows,
            )
            value_acc = value_acc + jnp.pad(
                jnp.einsum(
                    "hqk,qhd->khd",
                    attn_prob.astype(jnp.bfloat16),
                    grad_block,
                    preferred_element_type=jnp.float32,
                ),
                pad_rows,
            )
        query_grad = jnp.concatenate(query_parts, axis=0).reshape(tok_rows, head_cols)
        key_grad = key_acc.reshape(tok_rows, head_cols)
        value_grad = value_acc.reshape(tok_rows, head_cols)
        query_b_grad = query_b_grad + jnp.sum(query_grad, axis=0)
        value_b_grad = value_b_grad + jnp.sum(value_grad, axis=0)
        query_low = query_grad.astype(jnp.bfloat16)
        key_low = key_grad.astype(jnp.bfloat16)
        value_low = value_grad.astype(jnp.bfloat16)
        query_w_grad = query_w_grad + cross_rows(first_in, query_low)
        key_w_grad = key_w_grad + cross_rows(first_in, key_low)
        value_w_grad = value_w_grad + cross_rows(first_in, value_low)
        first_part = (
            times_transpose(query_low, query_weight)
            + times_transpose(key_low, key_weight)
            + times_transpose(value_low, value_weight)
        )
        first_cols = lax.psum_scatter(first_part, "tensor", scatter_dimension=1, tiled=True)
        first_grad = lax.all_gather(
            first_cols.astype(jnp.bfloat16), "tensor", axis=1, tiled=True
        ).astype(jnp.float32)
        input_back, gain_part, shift_part = norm_backward(
            first_grad, normed_one, inverse_one, gain_one
        )
        gain_one_grad = gain_one_grad + gain_part
        shift_one_grad = shift_one_grad + shift_part
        input_cols = lax.dynamic_slice_in_dim(
            resid_grad + input_back, column * col_width, col_width, axis=1
        ).astype(jnp.bfloat16)
        packed = jnp.concatenate([layer_cols, input_cols], axis=1)
        given_end = given_off + given_len
        dest_off = (running_sum(lengths_mb) - lengths_mb).reshape(-1)
        labels = jnp.arange(dealing_mb.shape[0], dtype=jnp.int32)
        give_row_ids = jnp.arange(tok_rows * lax.axis_size("dp"), dtype=jnp.int32)
        owner_seq = jnp.sum(
            (give_row_ids[:, None] >= given_end[None, :]).astype(jnp.int32), axis=1, dtype=jnp.int32
        )
        one_hot = (owner_seq[:, None] == labels[None, :]).astype(jnp.int32)
        within = give_row_ids - jnp.sum(one_hot * given_off[None, :], axis=1, dtype=jnp.int32)
        seq_label = jnp.sum(one_hot * dealing_mb[None, :], axis=1, dtype=jnp.int32)
        seq_hot = (seq_label[:, None] == labels[None, :]).astype(jnp.int32)
        buffer_row = jnp.sum(seq_hot * dest_off[None, :], axis=1, dtype=jnp.int32) + within
        owner_dev = seq_label // seq_dev
        is_mine = owner_dev == device
        fetched = jnp.take(packed, jnp.clip(buffer_row, 0, tok_rows - 1), axis=0).astype(
            jnp.float32
        )
        returned = lax.psum_scatter(
            jnp.where(is_mine[:, None], fetched, 0.0).astype(jnp.bfloat16),
            "dp",
            scatter_dimension=0,
            tiled=True,
        ).astype(jnp.float32)
        layer_parts.append(returned[:, :col_width].astype(jnp.bfloat16))
        grad_parts.append(returned[:, col_width:].astype(jnp.bfloat16))
    (
        query_w_grad,
        key_w_grad,
        value_w_grad,
        out_w_grad,
        query_b_grad,
        value_b_grad,
        out_b_grad,
        gain_one_grad,
        shift_one_grad,
        up_w_grad,
        up_b_grad,
        down_w_grad,
        down_b_grad,
        gain_two_grad,
        shift_two_grad,
    ) = lax.psum(
        (
            query_w_grad,
            key_w_grad,
            value_w_grad,
            out_w_grad,
            query_b_grad,
            value_b_grad,
            out_b_grad,
            gain_one_grad,
            shift_one_grad,
            up_w_grad,
            up_b_grad,
            down_w_grad,
            down_b_grad,
            gain_two_grad,
            shift_two_grad,
        ),
        "dp",
    )
    layer_out = jnp.stack(layer_parts, axis=0)
    input_grad = jnp.stack(grad_parts, axis=0)
    return (
        layer_out,
        input_grad,
        query_w_grad,
        key_w_grad,
        value_w_grad,
        out_w_grad,
        query_b_grad,
        value_b_grad,
        out_b_grad,
        up_w_grad,
        up_b_grad,
        down_w_grad,
        down_b_grad,
        gain_one_grad,
        shift_one_grad,
        gain_two_grad,
        shift_two_grad,
    )


def general_layer(mesh):
    in_specs = (
        P(None, "dp", "tensor"),
        P(None, "dp", "tensor"),
        P(),
        P(),
        P(None, "tensor"),
        P(None, "tensor"),
        P(None, "tensor"),
        P("tensor", None),
        P("tensor"),
        P("tensor"),
        P(),
        P(None, "tensor"),
        P("tensor"),
        P("tensor", None),
        P(),
        P(),
        P(),
        P(),
        P(),
    )
    out_specs = (
        P(None, "dp", "tensor"),
        P(None, "dp", "tensor"),
        P(None, "tensor"),
        P(None, "tensor"),
        P(None, "tensor"),
        P("tensor", None),
        P("tensor"),
        P("tensor"),
        P(),
        P(None, "tensor"),
        P("tensor"),
        P("tensor", None),
        P(),
        P(),
        P(),
        P(),
        P(),
    )
    return jax.shard_map(shards, mesh=mesh, in_specs=in_specs, out_specs=out_specs, check_vma=False)


ROWS = 1024
QBLK = 256
PAIR = 128


def slot_of(block, rank):
    piece = jnp.bitwise_xor(block, rank)
    return jnp.bitwise_or(piece >> 1, (piece & 1) << 1)


def rows_of(block, rank):
    return pl.ds(pl.multiple_of(slot_of(block, rank) * QBLK, QBLK), QBLK)


def fill_bias(bias_ref, key_info_ref, query_info_ref):
    for block in range(ROWS // QBLK):
        reach = (block + 1) * QBLK
        cols = pl.ds(block * QBLK, QBLK)
        key_part = key_info_ref[pl.ds(0, reach), 0:1]
        key_summary = key_info_ref[pl.ds(0, reach), 1:2]
        query_part = query_info_ref[0:1, cols]
        query_seq = query_info_ref[1:2, cols]
        key_row = lax.broadcasted_iota(jnp.int32, (reach, QBLK), 0)
        query_row = lax.broadcasted_iota(jnp.int32, (reach, QBLK), 1) + block * QBLK
        seen = (key_row <= query_row) & ((key_part == query_part) | (key_summary == query_seq))
        bias_ref[pl.ds(0, reach), cols] = jnp.where(seen, 0.0, MASKED)


def nt_dot(left, right):
    return lax.dot_general(left, right, (((1,), (1,)), ((), ())), preferred_element_type=jnp.float32)


def nn_dot(left, right):
    return jnp.dot(left, right, preferred_element_type=jnp.float32)


def head_lanes(block, head):
    lane = lax.broadcasted_iota(jnp.int32, block.shape, 1)
    inside = (lane >= head * HEAD_DIM) & (lane < (head + 1) * HEAD_DIM)
    return jnp.where(inside, block, jnp.zeros_like(block))


def attend_kernel(
    rank_ref, query_ref, key_ref, value_ref, key_info_ref, query_info_ref, out_ref, bias_ref, keys, value_t
):
    rank = rank_ref[0]

    @pl.when(pl.program_id(0) == 0)
    def _():
        fill_bias(bias_ref, key_info_ref, query_info_ref)

    for block in range(ROWS // QBLK):
        here = rows_of(block, rank)
        keys[pl.ds(block * QBLK, QBLK), :] = key_ref[here, :]
        value_t[:, pl.ds(block * QBLK, QBLK)] = value_ref[here, :].T
    for block in range(ROWS // QBLK):
        reach = (block + 1) * QBLK
        here = rows_of(block, rank)
        queries = query_ref[here, :] * jnp.bfloat16(HEAD_DIM**-0.5)
        bias = bias_ref[pl.ds(0, reach), pl.ds(block * QBLK, QBLK)]
        parts = []
        for head in range(2):
            scores = nt_dot(keys[pl.ds(0, reach), :], head_lanes(queries, head)) + bias
            top = jnp.max(scores, axis=0, keepdims=True)
            terms = jnp.exp(scores - top)
            total = jnp.sum(terms, axis=0, keepdims=True)
            heads_t = nn_dot(
                value_t[pl.ds(head * HEAD_DIM, HEAD_DIM), pl.ds(0, reach)], terms.astype(jnp.bfloat16)
            )
            parts.append(heads_t / total)
        out_ref[here, :] = jnp.concatenate(parts, axis=0).T.astype(out_ref.dtype)


def attend(qkv, rank, key_info, query_info):
    pairs = qkv.shape[1] // (3 * PAIR)
    cells = ROWS * ROWS * 5 // 8
    return pl.pallas_call(
        attend_kernel,
        grid_spec=pltpu.PrefetchScalarGridSpec(
            num_scalar_prefetch=1,
            grid=(pairs,),
            in_specs=[
                pl.BlockSpec((ROWS, PAIR), lambda i, r: (0, i)),
                pl.BlockSpec((ROWS, PAIR), lambda i, r: (0, pairs + i)),
                pl.BlockSpec((ROWS, PAIR), lambda i, r: (0, 2 * pairs + i)),
                pl.BlockSpec((ROWS, 2), lambda i, r: (0, 0)),
                pl.BlockSpec((2, ROWS), lambda i, r: (0, 0)),
            ],
            out_specs=pl.BlockSpec((ROWS, PAIR), lambda i, r: (0, i)),
            scratch_shapes=[
                pltpu.VMEM((ROWS, ROWS), jnp.float32),
                pltpu.VMEM((ROWS, PAIR), jnp.bfloat16),
                pltpu.VMEM((PAIR, ROWS), jnp.bfloat16),
            ],
        ),
        out_shape=jax.ShapeDtypeStruct((ROWS, pairs * PAIR), jnp.bfloat16),
        compiler_params=pltpu.CompilerParams(vmem_limit_bytes=24 << 20),
        cost_estimate=light(),
        name="attend",
    )(rank, qkv, qkv, qkv, key_info, query_info)


def attend_back_kernel(
    rank_ref,
    query_ref,
    key_ref,
    value_ref,
    grad_ref,
    key_info_ref,
    query_info_ref,
    query_out,
    key_out,
    value_out,
    sums_out,
    bias_ref,
    keys,
    values,
    key_t,
    key_acc,
    value_acc,
):
    rank = rank_ref[0]
    scale = HEAD_DIM**-0.5

    @pl.when(pl.program_id(0) == 0)
    def _():
        fill_bias(bias_ref, key_info_ref, query_info_ref)

    for block in range(ROWS // QBLK):
        here = rows_of(block, rank)
        there = pl.ds(block * QBLK, QBLK)
        keys[there, :] = key_ref[here, :]
        values[there, :] = value_ref[here, :]
        key_t[:, there] = key_ref[here, :].T
    query_sum = jnp.zeros((1, PAIR), jnp.float32)
    for block in reversed(range(ROWS // QBLK)):
        reach = (block + 1) * QBLK
        here = rows_of(block, rank)
        upto = pl.ds(0, reach)
        queries = query_ref[here, :] * jnp.bfloat16(scale)
        grads = grad_ref[here, :]
        bias = bias_ref[upto, pl.ds(block * QBLK, QBLK)]
        parts = []
        key_add = None
        value_add = None
        for head in range(2):
            query_h = head_lanes(queries, head)
            grad_h = head_lanes(grads, head)
            scores = nt_dot(keys[upto, :], query_h) + bias
            top = jnp.max(scores, axis=0, keepdims=True)
            terms = jnp.exp(scores - top)
            prob = terms * (1.0 / jnp.sum(terms, axis=0, keepdims=True))
            prob_grad = nt_dot(values[upto, :], grad_h)
            inner = jnp.sum(prob * prob_grad, axis=0, keepdims=True)
            score_grad = (prob * (prob_grad - inner)).astype(jnp.bfloat16)
            value_part = nn_dot(prob.astype(jnp.bfloat16), grad_h)
            key_part = nn_dot(score_grad, query_h)
            value_add = value_part if value_add is None else value_add + value_part
            key_add = key_part if key_add is None else key_add + key_part
            parts.append(nn_dot(key_t[pl.ds(head * HEAD_DIM, HEAD_DIM), upto], score_grad))
        if block == ROWS // QBLK - 1:
            key_acc[...] = key_add
            value_acc[...] = value_add
        else:
            key_acc[upto, :] += key_add
            value_acc[upto, :] += value_add
        query_grad = jnp.concatenate(parts, axis=0).T * scale
        query_sum = query_sum + jnp.sum(query_grad, axis=0, keepdims=True)
        query_out[here, :] = query_grad.astype(query_out.dtype)
    for block in range(ROWS // QBLK):
        here = rows_of(block, rank)
        there = pl.ds(block * QBLK, QBLK)
        key_out[here, :] = key_acc[there, :].astype(key_out.dtype)
        value_out[here, :] = value_acc[there, :].astype(value_out.dtype)
    value_sum = jnp.sum(value_acc[...], axis=0, keepdims=True)
    row = lax.broadcasted_iota(jnp.int32, (8, PAIR), 0)
    sums_out[...] = jnp.where(row == 0, query_sum, jnp.where(row == 1, value_sum, 0.0))


def attend_back(qkv, grads, rank, key_info, query_info):
    pairs = qkv.shape[1] // (3 * PAIR)
    cells = ROWS * ROWS * 5 // 8
    block = (ROWS, PAIR)
    wide = jax.ShapeDtypeStruct((ROWS, pairs * PAIR), jnp.bfloat16)
    return pl.pallas_call(
        attend_back_kernel,
        grid_spec=pltpu.PrefetchScalarGridSpec(
            num_scalar_prefetch=1,
            grid=(pairs,),
            in_specs=[
                pl.BlockSpec(block, lambda i, r: (0, i)),
                pl.BlockSpec(block, lambda i, r: (0, pairs + i)),
                pl.BlockSpec(block, lambda i, r: (0, 2 * pairs + i)),
                pl.BlockSpec(block, lambda i, r: (0, i)),
                pl.BlockSpec((ROWS, 2), lambda i, r: (0, 0)),
                pl.BlockSpec((2, ROWS), lambda i, r: (0, 0)),
            ],
            out_specs=[
                pl.BlockSpec(block, lambda i, r: (0, i)),
                pl.BlockSpec(block, lambda i, r: (0, i)),
                pl.BlockSpec(block, lambda i, r: (0, i)),
                pl.BlockSpec((8, PAIR), lambda i, r: (0, i)),
            ],
            scratch_shapes=[
                pltpu.VMEM((ROWS, ROWS), jnp.float32),
                pltpu.VMEM(block, jnp.bfloat16),
                pltpu.VMEM(block, jnp.bfloat16),
                pltpu.VMEM((PAIR, ROWS), jnp.bfloat16),
                pltpu.VMEM(block, jnp.float32),
                pltpu.VMEM(block, jnp.float32),
            ],
        ),
        out_shape=[wide, wide, wide, jax.ShapeDtypeStruct((8, pairs * PAIR), jnp.float32)],
        compiler_params=pltpu.CompilerParams(vmem_limit_bytes=28 << 20),
        cost_estimate=light(),
        name="attend_back",
    )(rank, qkv, qkv, qkv, grads, key_info, query_info)


WIDE = 512
VMEM_BYTES = 56 << 20


def light(flops=1 << 20):
    return pl.CostEstimate(flops=flops, bytes_accessed=1 << 12, transcendentals=0)


def settings():
    return pltpu.CompilerParams(vmem_limit_bytes=VMEM_BYTES)


def whole(shape):
    return pl.BlockSpec(shape, lambda i: (0,) * len(shape))


def project_kernel(near_ref, far_ref, weight_ref, bias_ref, out_ref):
    rows = near_ref.shape[0]
    bias = bias_ref[...]
    out_ref[pl.ds(0, rows), :] = (nt_dot(near_ref[...], weight_ref[...]) + bias).astype(out_ref.dtype)
    out_ref[pl.ds(rows, rows), :] = (nt_dot(far_ref[...], weight_ref[...]) + bias).astype(out_ref.dtype)


def project(near, far, weight, bias):
    rows, depth = near.shape
    cols = weight.shape[0]
    return pl.pallas_call(
        project_kernel,
        grid=(cols // WIDE,),
        in_specs=[
            whole((rows, depth)),
            whole((rows, depth)),
            pl.BlockSpec((WIDE, depth), lambda i: (i, 0)),
            pl.BlockSpec((1, WIDE), lambda i: (0, i)),
        ],
        out_specs=pl.BlockSpec((2 * rows, WIDE), lambda i: (0, i)),
        out_shape=jax.ShapeDtypeStruct((2 * rows, cols), jnp.bfloat16),
        compiler_params=settings(),
        cost_estimate=light(),
        name="project",
    )(near, far, weight, bias)


def expand_kernel(near_ref, far_ref, weight_ref, bias_ref, hidden_ref, slope_ref):
    rows = near_ref.shape[0]
    bias = bias_ref[...]
    for part, ref in enumerate((near_ref, far_ref)):
        at = pl.ds(part * rows, rows)
        pre = nt_dot(ref[...], weight_ref[...]) + bias
        cube = 0.044715 * pre * pre
        bend = jnp.tanh((0.7978845608028654 * pre) * (1.0 + cube))
        half = 0.5 + 0.5 * bend
        inner = 0.7978845608028654 + (3.0 * 0.7978845608028654) * cube
        hidden_ref[at, :] = (pre * half).astype(jnp.bfloat16)
        slope_ref[at, :] = (half + (pre * half) * ((1.0 - bend) * inner)).astype(jnp.bfloat16)


def expand(near, far, weight, bias):
    rows, depth = near.shape
    cols = weight.shape[0]
    out = jax.ShapeDtypeStruct((2 * rows, cols), jnp.bfloat16)
    return pl.pallas_call(
        expand_kernel,
        grid=(cols // WIDE,),
        in_specs=[
            whole((rows, depth)),
            whole((rows, depth)),
            pl.BlockSpec((WIDE, depth), lambda i: (i, 0)),
            pl.BlockSpec((1, WIDE), lambda i: (0, i)),
        ],
        out_specs=[pl.BlockSpec((2 * rows, WIDE), lambda i: (0, i))] * 2,
        out_shape=[out, out],
        compiler_params=settings(),
        cost_estimate=light(),
        name="expand",
    )(near, far, weight, bias)


def expand_back_kernel(near_ref, far_ref, weight_ref, slope_ref, low_ref, sums_ref):
    rows = near_ref.shape[0]
    total = jnp.zeros((1, low_ref.shape[1]), jnp.float32)
    for part, ref in enumerate((near_ref, far_ref)):
        at = pl.ds(part * rows, rows)
        grad = nt_dot(ref[...], weight_ref[...]) * slope_ref[at, :].astype(jnp.float32)
        total = total + jnp.sum(grad, axis=0, keepdims=True)
        low_ref[at, :] = grad.astype(jnp.bfloat16)
    sums_ref[...] = jnp.broadcast_to(total, sums_ref.shape)


def expand_back(near, far, weight, slope):
    rows, depth = near.shape
    cols = weight.shape[0]
    return pl.pallas_call(
        expand_back_kernel,
        grid=(cols // WIDE,),
        in_specs=[
            whole((rows, depth)),
            whole((rows, depth)),
            pl.BlockSpec((WIDE, depth), lambda i: (i, 0)),
            pl.BlockSpec((2 * rows, WIDE), lambda i: (0, i)),
        ],
        out_specs=[pl.BlockSpec((2 * rows, WIDE), lambda i: (0, i)), pl.BlockSpec((8, WIDE), lambda i: (0, i))],
        out_shape=[
            jax.ShapeDtypeStruct((2 * rows, cols), jnp.bfloat16),
            jax.ShapeDtypeStruct((8, cols), jnp.float32),
        ],
        compiler_params=settings(),
        cost_estimate=light(),
        name="expand_back",
    )(near, far, weight, slope)


def partial_kernel(left_ref, weight_ref, near_ref, far_ref):
    rows = near_ref.shape[0]
    far_ref[...] = nn_dot(left_ref[pl.ds(rows, rows), :], weight_ref[...]).astype(far_ref.dtype)
    near_ref[...] = nn_dot(left_ref[pl.ds(0, rows), :], weight_ref[...])


def partial_sums(left, weight):
    rows, depth = left.shape
    cols = weight.shape[1]
    half = rows // 2
    return pl.pallas_call(
        partial_kernel,
        grid=(cols // WIDE,),
        in_specs=[whole((rows, depth)), pl.BlockSpec((depth, WIDE), lambda i: (0, i))],
        out_specs=[pl.BlockSpec((half, WIDE), lambda i: (0, i))] * 2,
        out_shape=[
            jax.ShapeDtypeStruct((half, cols), jnp.float32),
            jax.ShapeDtypeStruct((half, cols), jnp.bfloat16),
        ],
        compiler_params=settings(),
        cost_estimate=light(),
        name="partial_sums",
    )(left, weight)


def tn_dot(left, right):
    return lax.dot_general(left, right, (((0,), (0,)), ((), ())), preferred_element_type=jnp.float32)


def cross_kernel(left_a, near_a, far_a, left_b, near_b, far_b, out_ref):
    rows = near_a.shape[0]
    top, low = pl.ds(0, rows), pl.ds(rows, rows)
    total = tn_dot(left_a[top, :], near_a[...]) + tn_dot(left_a[low, :], far_a[...])
    total = total + tn_dot(left_b[top, :], near_b[...]) + tn_dot(left_b[low, :], far_b[...])
    out_ref[...] = total.astype(out_ref.dtype)


def cross_sums(left_a, right_a, left_b, right_b, start, size):
    rows = left_a.shape[0]
    cols = right_a[0].shape[1]
    tall = 256
    first = start // tall
    left_spec = pl.BlockSpec((rows, tall), lambda i: (0, first + i))
    right_spec = whole((rows // 2, cols))
    return pl.pallas_call(
        cross_kernel,
        grid=(size // tall,),
        in_specs=[left_spec, right_spec, right_spec] * 2,
        out_specs=pl.BlockSpec((tall, cols), lambda i: (i, 0)),
        out_shape=jax.ShapeDtypeStruct((size, cols), jnp.bfloat16),
        compiler_params=settings(),
        cost_estimate=light(),
        name="cross_sums",
    )(left_a, *right_a, left_b, *right_b)


def flip_kernel(first_ref, weight_ref, out_ref):
    out_ref[...] = weight_ref[...].T


def flipped(weight, first, count):
    depth = weight.shape[0]
    return pl.pallas_call(
        flip_kernel,
        grid_spec=pltpu.PrefetchScalarGridSpec(
            num_scalar_prefetch=1,
            grid=(count,),
            in_specs=[pl.BlockSpec((depth, 128), lambda i, first: (0, first[0] + i))],
            out_specs=pl.BlockSpec((128, depth), lambda i, first: (i, 0)),
        ),
        out_shape=jax.ShapeDtypeStruct((count * 128, depth), weight.dtype),
        compiler_params=settings(),
        cost_estimate=light(),
        name="flipped",
    )(first.reshape(1).astype(jnp.int32), weight)


def attn_pack_kernel(
    place_ref, query_ref, key_ref, value_ref, out_w_ref, bias_mine, bias_other, mine_ref, other_ref
):
    half = place_ref[1]
    mine_ref[pl.ds(4 * HEAD_DIM, 8), :] = bias_mine[...]
    other_ref[pl.ds(4 * HEAD_DIM, 8), :] = bias_other[...]
    for which, ref in enumerate((mine_ref, other_ref)):
        rows = pl.ds(pl.multiple_of(jnp.where(which == 0, half, 1 - half) * HEAD_DIM, HEAD_DIM), HEAD_DIM)
        ref[pl.ds(3 * HEAD_DIM, HEAD_DIM), :] = out_w_ref[rows, :]
    for index, source in enumerate((query_ref, key_ref, value_ref)):
        flat = source[...].T
        low, high = flat[:HEAD_DIM, :], flat[HEAD_DIM:, :]
        at = pl.ds(index * HEAD_DIM, HEAD_DIM)
        mine_ref[at, :] = jnp.where(half == 0, low, high)
        other_ref[at, :] = jnp.where(half == 0, high, low)


def attn_pack(query_weight, key_weight, value_weight, out_weight, bias_mine, bias_other, team, half):
    depth = query_weight.shape[0]
    out = jax.ShapeDtypeStruct((4 * HEAD_DIM + 8, depth), query_weight.dtype)
    column = pl.BlockSpec((depth, 128), lambda i, place: (0, place[0]))
    full = pl.BlockSpec((4 * HEAD_DIM + 8, depth), lambda i, place: (0, 0))
    bias = pl.BlockSpec((8, depth), lambda i, place: (0, 0))
    return pl.pallas_call(
        attn_pack_kernel,
        grid_spec=pltpu.PrefetchScalarGridSpec(
            num_scalar_prefetch=1,
            grid=(1,),
            in_specs=[column, column, column, pl.BlockSpec((128, depth), lambda i, place: (place[0], 0)), bias, bias],
            out_specs=[full, full],
        ),
        out_shape=[out, out],
        compiler_params=settings(),
        cost_estimate=light(),
        name="attn_pack",
    )(jnp.stack([team, half]).astype(jnp.int32), query_weight, key_weight, value_weight, out_weight, bias_mine, bias_other)


def pick_kernel(index_ref, rows_ref, out_ref):
    wanted = index_ref[...]
    place = lax.broadcasted_iota(jnp.int32, (wanted.shape[0], rows_ref.shape[0]), 1)
    hot = jnp.where(place == wanted, 1.0, 0.0).astype(jnp.bfloat16)
    out_ref[...] = nn_dot(hot, rows_ref[...]).astype(out_ref.dtype)


def pick_rows(index, rows, tall):
    count = index.shape[0]
    cols = rows.shape[1]
    return pl.pallas_call(
        pick_kernel,
        grid=(count // tall,),
        in_specs=[pl.BlockSpec((tall, 1), lambda i: (i, 0)), whole(rows.shape)],
        out_specs=pl.BlockSpec((tall, cols), lambda i: (i, 0)),
        out_shape=jax.ShapeDtypeStruct((count, cols), rows.dtype),
        compiler_params=settings(),
        cost_estimate=light(),
        name="pick_rows",
    )(index[:, None], rows)


def drop_kernel(index_ref, rows_ref, out_ref):
    wanted = index_ref[...]
    tall = out_ref.shape[0]
    place = lax.broadcasted_iota(jnp.int32, (tall, rows_ref.shape[0]), 0) + pl.program_id(0) * tall
    hot = jnp.where(place == wanted, 1.0, 0.0).astype(jnp.bfloat16)
    out_ref[...] = nn_dot(hot, rows_ref[...]).astype(out_ref.dtype)


def drop_rows(index, rows, count, tall):
    cols = rows.shape[1]
    return pl.pallas_call(
        drop_kernel,
        grid=(count // tall,),
        in_specs=[whole((1, index.shape[0])), whole(rows.shape)],
        out_specs=pl.BlockSpec((tall, cols), lambda i: (i, 0)),
        out_shape=jax.ShapeDtypeStruct((count, cols), rows.dtype),
        compiler_params=settings(),
        cost_estimate=light(),
        name="drop_rows",
    )(index[None, :], rows)


def settle_kernel(index_ref, boxes_ref, out_ref):
    wanted = index_ref[...]
    place = lax.broadcasted_iota(jnp.int32, (out_ref.shape[0], boxes_ref.shape[1]), 0)
    hot = jnp.where(place == wanted, 1.0, 0.0).astype(jnp.bfloat16)
    out_ref[...] = nn_dot(hot, boxes_ref[0]).astype(out_ref.dtype)


def settle_rows(index, boxes, count):
    depth, slots, cols = boxes.shape
    return pl.pallas_call(
        settle_kernel,
        grid=(depth,),
        in_specs=[whole((1, slots)), pl.BlockSpec((1, slots, cols), lambda i: (i, 0, 0))],
        out_specs=pl.BlockSpec((count, cols), lambda i: (0, i)),
        out_shape=jax.ShapeDtypeStruct((count, depth * cols), boxes.dtype),
        compiler_params=settings(),
        cost_estimate=light(),
        name="settle_rows",
    )(index[None, :], boxes)


def unsettle_kernel(index_ref, rows_ref, out_ref):
    wanted = index_ref[...]
    place = lax.broadcasted_iota(jnp.int32, (wanted.shape[0], rows_ref.shape[0]), 1)
    hot = jnp.where(place == wanted, 1.0, 0.0).astype(jnp.bfloat16)
    out_ref[0] = nn_dot(hot, rows_ref[...]).astype(out_ref.dtype)


def unsettle_rows(index, rows, depth):
    slots = index.shape[0]
    count = rows.shape[0]
    cols = rows.shape[1] // depth
    return pl.pallas_call(
        unsettle_kernel,
        grid=(depth,),
        in_specs=[whole((slots, 1)), pl.BlockSpec((count, cols), lambda i: (0, i))],
        out_specs=pl.BlockSpec((1, slots, cols), lambda i: (i, 0, 0)),
        out_shape=jax.ShapeDtypeStruct((depth, slots, cols), rows.dtype),
        compiler_params=settings(),
        cost_estimate=light(),
        name="unsettle_rows",
    )(index[:, None], rows)


def code_of(place, own):
    return jnp.bitwise_xor(place, own)


def piece_of(code):
    return ((code >> 2) & 1) + 2 * (code & 1)


def stack_kernel(own_ref, near_ref, far_ref, out_ref):
    code = code_of(pl.program_id(0), own_ref[0])
    block = jnp.where((code & 2) == 0, near_ref[...], far_ref[...])
    out_ref[...] = block.astype(out_ref.dtype)


def stack_kernel_t(own_ref, near_ref, far_ref, out_ref):
    code = code_of(pl.program_id(0), own_ref[0])
    block = jnp.where((code & 2) == 0, near_ref[...], far_ref[...])
    out_ref[...] = block.T.astype(out_ref.dtype)


def stack_pieces(near, far, own, transposed):
    tall = near.shape[0] // 4
    cols = near.shape[1]
    spec = pl.BlockSpec((tall, cols), lambda i, own: (piece_of(code_of(i, own[0])), 0))
    return pl.pallas_call(
        stack_kernel_t if transposed else stack_kernel,
        grid_spec=pltpu.PrefetchScalarGridSpec(
            num_scalar_prefetch=1,
            grid=(8,),
            in_specs=[spec, spec],
            out_specs=pl.BlockSpec((cols, tall), lambda i, own: (0, i))
            if transposed
            else pl.BlockSpec((tall, cols), lambda i, own: (i, 0)),
        ),
        out_shape=jax.ShapeDtypeStruct((cols, 8 * tall) if transposed else (8 * tall, cols), jnp.float32),
        compiler_params=settings(),
        cost_estimate=light(),
        name="stack_pieces",
    )(own, near, far)


def stack_heads_kernel(flips, own_ref, near_low, far_low, near_high, far_high, *outs):
    code = code_of(2 * pl.program_id(0), own_ref[0])
    take_near = (code & 2) == 0
    low = jnp.where(take_near, near_low[...], far_low[...])
    high = jnp.where(take_near, near_high[...], far_high[...])
    for index, ref in enumerate(outs):
        at = slice(index * HEAD_DIM, (index + 1) * HEAD_DIM)
        both = jnp.concatenate([low[at], high[at]], axis=0)
        ref[...] = (both.T if flips[index] else both).astype(ref.dtype)


def stack_heads(near, far, own, flips):
    tall = near.shape[0] // 4
    cols = near.shape[1]
    low = pl.BlockSpec((tall, cols), lambda i, own: (piece_of(code_of(2 * i, own[0])), 0))
    high = pl.BlockSpec((tall, cols), lambda i, own: (piece_of(code_of(2 * i + 1, own[0])), 0))
    column = pl.BlockSpec((cols, 128), lambda i, own: (0, i))
    row = pl.BlockSpec((128, cols), lambda i, own: (i, 0))
    tall_out = jax.ShapeDtypeStruct((cols, 512), jnp.float32)
    flat_out = jax.ShapeDtypeStruct((512, cols), jnp.float32)
    return pl.pallas_call(
        functools.partial(stack_heads_kernel, flips),
        grid_spec=pltpu.PrefetchScalarGridSpec(
            num_scalar_prefetch=1,
            grid=(4,),
            in_specs=[low, low, high, high],
            out_specs=[column if flip else row for flip in flips],
        ),
        out_shape=[tall_out if flip else flat_out for flip in flips],
        compiler_params=settings(),
        cost_estimate=light(),
        name="stack_heads",
    )(own, near, far, near, far)


def add_rows_kernel(*refs):
    total = refs[0][...].astype(jnp.float32)
    for ref in refs[1:-1]:
        total = total + ref[...].astype(jnp.float32)
    refs[-1][...] = total.astype(refs[-1].dtype)


def add_pieces(near, got, moved, index):
    tall = near.shape[0] // 4
    cols = near.shape[1]
    at = pl.BlockSpec((tall, cols), lambda i: (index, 0))
    return pl.pallas_call(
        add_rows_kernel,
        grid=(1,),
        in_specs=[at, at] + [whole((tall, cols))] * len(moved),
        out_specs=whole((tall, cols)),
        out_shape=jax.ShapeDtypeStruct((tall, cols), near.dtype),
        compiler_params=settings(),
        cost_estimate=light(),
        name="add_pieces",
    )(near, got, *moved)


def add_rows(near, got, index):
    return add_pieces(near, got, (), index)


def add_three(near, got, moved, index):
    return add_pieces(near, got, (moved,), index)


def add_four(near, got, first, second, index):
    return add_pieces(near, got, (first, second), index)


def partial_three_kernel(query_ref, key_ref, value_ref, weight_ref, near_ref, far_ref):
    rows = near_ref.shape[0]
    depth = query_ref.shape[1]
    for at, out in ((pl.ds(rows, rows), far_ref), (pl.ds(0, rows), near_ref)):
        total = nn_dot(query_ref[at, :], weight_ref[pl.ds(0, depth), :])
        total = total + nn_dot(key_ref[at, :], weight_ref[pl.ds(depth, depth), :])
        total = total + nn_dot(value_ref[at, :], weight_ref[pl.ds(2 * depth, depth), :])
        out[...] = total.astype(out.dtype)


def partial_three(query, key, value, weight):
    rows, depth = query.shape
    cols = weight.shape[1]
    half = rows // 2
    return pl.pallas_call(
        partial_three_kernel,
        grid=(cols // WIDE,),
        in_specs=[whole((rows, depth))] * 3 + [pl.BlockSpec((3 * depth, WIDE), lambda i: (0, i))],
        out_specs=[pl.BlockSpec((half, WIDE), lambda i: (0, i))] * 2,
        out_shape=[
            jax.ShapeDtypeStruct((half, cols), jnp.float32),
            jax.ShapeDtypeStruct((half, cols), jnp.bfloat16),
        ],
        compiler_params=settings(),
        cost_estimate=light(),
        name="partial_three",
    )(query, key, value, weight)


def rows_call(kernel, name, grid_rows, ins, outs, sums=0):
    tall = 128
    cols = 2048
    steps = grid_rows // tall

    def spec(array, first):
        if first is None:
            return pl.BlockSpec(array.shape, lambda i: (0, 0))
        return pl.BlockSpec((tall, cols), lambda i: (first * steps + i, 0))

    out_specs = [pl.BlockSpec((tall, cols), lambda i: (i, 0)) for _ in outs]
    out_shape = [jax.ShapeDtypeStruct((grid_rows, cols), kind) for kind in outs]
    if sums:
        out_specs.append(pl.BlockSpec((8, cols), lambda i: (0, 0)))
        out_shape.append(jax.ShapeDtypeStruct((8, cols), jnp.float32))
    return pl.pallas_call(
        kernel,
        grid=(steps,),
        in_specs=[spec(array, first) for array, first in ins],
        out_specs=out_specs,
        out_shape=out_shape,
        compiler_params=settings(),
        cost_estimate=light(),
        name=name,
    )(*[array for array, _ in ins])


def wide(ref):
    return ref[...].astype(jnp.float32)


def norm_in_kernel(rows_ref, gain_ref, shift_ref, out_ref):
    normed, _ = normalize(wide(rows_ref))
    out_ref[...] = (normed * gain_ref[...] + shift_ref[...]).astype(out_ref.dtype)


def norm_in(tok, m, gain, shift_by):
    return rows_call(
        norm_in_kernel, "norm_in", tok.shape[0] // 2, [(tok, m), (gain, None), (shift_by, None)], [jnp.bfloat16]
    )[0]


def resid_kernel(rows_ref, kept_ref, got_ref, bias_ref, gain_ref, shift_ref, resid_ref, out_ref):
    resid = wide(rows_ref) + kept_ref[...] + wide(got_ref) + bias_ref[...]
    resid_ref[...] = resid
    normed, _ = normalize(resid.astype(jnp.bfloat16).astype(jnp.float32))
    out_ref[...] = (normed * gain_ref[...] + shift_ref[...]).astype(out_ref.dtype)


def resid_norm(tok, m, kept, got, bias, gain, shift_by):
    ins = [(tok, m), (kept, 0), (got, 0), (bias, None), (gain, None), (shift_by, None)]
    return rows_call(resid_kernel, "resid_norm", kept.shape[0], ins, [jnp.float32, jnp.bfloat16])


def layer_kernel(resid_ref, kept_ref, got_ref, bias_ref, out_ref):
    out_ref[...] = (resid_ref[...] + kept_ref[...] + wide(got_ref) + bias_ref[...]).astype(out_ref.dtype)


def layer_rows_of(resid, kept, got, bias):
    ins = [(resid, 0), (kept, 0), (got, 0), (bias, None)]
    return rows_call(layer_kernel, "layer_rows", kept.shape[0], ins, [jnp.bfloat16])[0]


def add_sums(sums_ref, parts):
    @pl.when(pl.program_id(0) == 0)
    def _():
        sums_ref[...] = jnp.zeros_like(sums_ref)

    for index, part in enumerate(parts):
        sums_ref[index : index + 1, :] += jnp.sum(part, axis=0, keepdims=True)


def norm_back_rows(grad, normed, inverse, gain):
    scaled = grad * gain
    first_mean = jnp.mean(scaled, axis=1, keepdims=True)
    second_mean = jnp.mean(scaled * normed, axis=1, keepdims=True)
    return inverse * (scaled - first_mean - normed * second_mean)


def second_back_kernel(kept_ref, got_ref, resid_ref, cot_ref, gain_ref, grad_ref, low_ref, sums_ref):
    grad = (kept_ref[...] + wide(got_ref)).astype(jnp.bfloat16).astype(jnp.float32)
    normed, inverse = normalize(resid_ref[...].astype(jnp.bfloat16).astype(jnp.float32))
    cot = wide(cot_ref)
    total = cot + norm_back_rows(grad, normed, inverse, gain_ref[...])
    grad_ref[...] = total
    low_ref[...] = total.astype(low_ref.dtype)
    add_sums(sums_ref, (total, cot, grad * normed, grad))


def second_back_rows(kept, got, resid, cot, m, gain):
    ins = [(kept, 0), (got, 0), (resid, 0), (cot, m), (gain, None)]
    return rows_call(second_back_kernel, "second_back", kept.shape[0], ins, [jnp.float32, jnp.bfloat16], sums=4)


def first_back_kernel(kept_ref, got_ref, rows_ref, resid_grad_ref, gain_ref, out_ref, sums_ref):
    grad = (kept_ref[...] + wide(got_ref)).astype(jnp.bfloat16).astype(jnp.float32)
    normed, inverse = normalize(wide(rows_ref))
    back = norm_back_rows(grad, normed, inverse, gain_ref[...])
    out_ref[...] = (resid_grad_ref[...] + back).astype(out_ref.dtype)
    add_sums(sums_ref, (grad * normed, grad))


def first_back_rows(kept, got, tok, m, resid_grad, gain):
    ins = [(kept, 0), (got, 0), (tok, m), (resid_grad, 0), (gain, None)]
    return rows_call(first_back_kernel, "first_back", kept.shape[0], ins, [jnp.bfloat16], sums=2)


def middle_kernel(near_top, near_low, got_top, got_low, kept_ref, moving_ref):
    kept_ref[...] = near_top[...] + wide(got_top)
    moving_ref[...] = (near_low[...] + wide(got_low)).astype(moving_ref.dtype)


def middle_rows(near, got):
    ins = [(near, 0), (near, 1), (got, 0), (got, 1)]
    return rows_call(middle_kernel, "middle_rows", near.shape[0] // 2, ins, [jnp.float32, jnp.bfloat16])


def join_kernel(count, *refs):
    sources, out_ref = refs[:count], refs[count]
    offset = 0
    for source in sources:
        rows = source.shape[0]
        out_ref[pl.ds(offset, rows), :] = source[...]
        offset += rows


def join_rows(arrays):
    count = len(arrays)
    rows = sum(array.shape[0] for array in arrays)
    cols = arrays[0].shape[1]
    chunk = cols // 4
    return pl.pallas_call(
        functools.partial(join_kernel, count),
        grid=(4,),
        in_specs=[pl.BlockSpec((array.shape[0], chunk), lambda i: (0, i)) for array in arrays],
        out_specs=pl.BlockSpec((rows, chunk), lambda i: (0, i)),
        out_shape=jax.ShapeDtypeStruct((rows, cols), arrays[0].dtype),
        compiler_params=settings(),
        cost_estimate=light(),
        name="join_rows",
    )(*arrays)


def attn_join_kernel(count, *refs):
    sources, qkv_ref, out_w_ref, bias_ref = refs[:count], *refs[count:]
    rows = HEAD_DIM
    for index, source in enumerate(sources):
        for k in range(3):
            qkv_ref[pl.ds((k * count + index) * rows, rows), :] = source[pl.ds(k * rows, rows), :]
        out_w_ref[pl.ds(index * rows, rows), :] = source[pl.ds(3 * rows, rows), :]
        bias_ref[pl.ds(index * 8, 8), :] = source[pl.ds(4 * rows, 8), :]


def attn_join(arrays):
    count = len(arrays)
    cols = arrays[0].shape[1]
    kind = arrays[0].dtype
    chunk = cols // 4
    sizes = (3 * count * HEAD_DIM, count * HEAD_DIM, count * 8)
    return pl.pallas_call(
        functools.partial(attn_join_kernel, count),
        grid=(4,),
        in_specs=[pl.BlockSpec((array.shape[0], chunk), lambda i: (0, i)) for array in arrays],
        out_specs=[pl.BlockSpec((size, chunk), lambda i: (0, i)) for size in sizes],
        out_shape=[jax.ShapeDtypeStruct((size, cols), kind) for size in sizes],
        compiler_params=settings(),
        cost_estimate=light(),
        name="attn_join",
    )(*arrays)


def cross_pair_kernel(rights, *refs):
    out_ref = refs[-1]
    lefts, right_refs = refs[:4], refs[4:-1]
    for which in range(2):
        right = right_refs[:4] if rights == 1 or which == 0 else right_refs[4:]
        near_a, far_a, near_b, far_b = right
        left_a, left_b = lefts[2 * which], lefts[2 * which + 1]
        rows = near_a.shape[0]
        top, low = pl.ds(0, rows), pl.ds(rows, rows)
        total = tn_dot(left_a[top, :], near_a[...]) + tn_dot(left_a[low, :], far_a[...])
        total = total + tn_dot(left_b[top, :], near_b[...]) + tn_dot(left_b[low, :], far_b[...])
        total = total.astype(out_ref.dtype)
        for piece in range(total.shape[0] // HEAD_DIM):
            at = pl.ds((2 * piece + which) * HEAD_DIM, HEAD_DIM)
            out_ref[at, :] = total[piece * HEAD_DIM : (piece + 1) * HEAD_DIM, :]


def cross_pair(first, second, rights, half):
    rows = first[0].shape[0]
    cols = rights[0][0].shape[1]
    tall = first[0].shape[1] // 2
    wide_cols = 1024
    left_spec = pl.BlockSpec((rows, tall), lambda i: (0, half))
    right_spec = pl.BlockSpec((rows // 2, wide_cols), lambda i: (0, i))
    flat = [array for right in rights for array in right]
    return pl.pallas_call(
        functools.partial(cross_pair_kernel, len(rights)),
        grid=(cols // wide_cols,),
        in_specs=[left_spec] * 4 + [right_spec] * len(flat),
        out_specs=pl.BlockSpec((2 * tall, wide_cols), lambda i: (0, i)),
        out_shape=jax.ShapeDtypeStruct((2 * tall, cols), jnp.bfloat16),
        compiler_params=settings(),
        cost_estimate=light(),
        name="cross_pair",
    )(*first, *second, *flat)


SWAP = [(0, 1), (1, 0)]
PLANE = ("y", "x", "core")
EVERY = ("z", "y", "x", "core")
MICRO = 2
SLOTS = 72


def after(value, *others):
    return lax.optimization_barrier((value, *others))[0]


class Order:

    def __init__(self):
        self.last = ()

    def take(self, value):
        return lax.optimization_barrier((value, self.last))[0]

    def mark(self, value):
        self.last = value
        return value

    def step(self, value):
        return self.mark(self.take(value))


def swap_along(array, axis):
    return lax.ppermute(array, axis, SWAP)


def shift(array, step):
    size = lax.axis_size("z")
    return lax.ppermute(array, "z", [(i, (i + step) % size) for i in range(size)])


def joined(arrays):
    return jnp.concatenate(arrays, axis=0)


def plane_start(piece):
    return (piece, swap_along(piece, "x"), swap_along(piece, "y"))


def plane_middle(started, order):
    piece, by_x, by_y = started
    half = piece.shape[0] // 2
    by_x, by_y = order.step((by_x, by_y))
    return (piece, by_x, by_y, swap_along(by_y[:half], "x"), swap_along(by_x[half:], "y"))


def plane_end(started, order):
    piece, by_x, by_y, corner_top, corner_low = started
    near = order.mark(join_rows([piece, by_x, by_y, *order.take((corner_top, corner_low))]))
    return (near, swap_along(near, "core"))


def held_before(bound, residue, parts):
    return (bound + (parts - 1) - residue) // parts


def piece_tables(lengths, starts, quarter_low, quarter_rows, residue, parts):
    ends = running_sum(lengths)
    firsts = ends - lengths
    shift = starts - firsts
    low = jnp.maximum(firsts, quarter_low)
    high = jnp.minimum(ends, quarter_low + quarter_rows)
    begin = held_before(low + shift, residue, parts)
    count = jnp.where(high > low, held_before(high + shift, residue, parts) - begin, 0)
    return (begin, count, shift)


def slot_lookup(begin, count, value_of):
    base = running_sum(count) - count
    slot = jnp.arange(SLOTS, dtype=jnp.int32)
    inside = (slot >= base[..., None]) & (slot < (base + count)[..., None])
    held = begin[..., None] + slot - base[..., None]
    return jnp.sum(jnp.where(inside, value_of(held) + 1, 0), axis=-2, dtype=jnp.int32) - 1


def layer(
    tokens,
    cotangent,
    lengths,
    dealing,
    query_weight,
    key_weight,
    value_weight,
    out_weight,
    query_bias,
    value_bias,
    out_bias,
    up_weight,
    up_bias,
    down_weight,
    down_bias,
    attn_gain,
    attn_shift,
    mlp_gain,
    mlp_shift,
):
    tok_rows = tokens.shape[1]
    col_width = tokens.shape[2]
    width = out_weight.shape[1]
    seq_dev = lengths.shape[2]
    depth = lax.axis_size("z")
    parts = lax.axis_size("y") * 4
    own_rows = tok_rows // 4
    y, x, core, z = (lax.axis_index(name) for name in ("y", "x", "core", "z"))
    team = 2 * x + core
    eighth = 2 * team + y
    residue = 4 * y + team
    group = 2 * z + y

    given_off = []
    for micro_step in range(MICRO):
        given_off.append(given_layout(lengths[micro_step], dealing[micro_step])[2])
    starts = jnp.stack(given_off).reshape(lengths.shape)
    quarter_low = (jnp.arange(4, dtype=jnp.int32) * own_rows)[None, None, :, None]
    begin, count, _ = piece_tables(
        lengths[:, :, None, :], starts[:, :, None, :], quarter_low, own_rows, residue, parts
    )
    micro_ids = jnp.arange(MICRO, dtype=jnp.int32)[:, None, None, None]
    begin = jnp.transpose(begin + micro_ids * tok_rows, (1, 2, 0, 3)).reshape(-1, MICRO * seq_dev)
    count = jnp.transpose(count, (1, 2, 0, 3)).reshape(-1, MICRO * seq_dev)
    send_row = slot_lookup(begin, count, lambda held: held).reshape(-1)

    my_lengths = lax.dynamic_index_in_dim(lengths, group, 1, keepdims=False)
    my_starts = lax.dynamic_index_in_dim(starts, group, 1, keepdims=False)
    residues = jnp.arange(parts, dtype=jnp.int32)[:, None, None]
    my_begin, my_count, my_shift = piece_tables(
        my_lengths[None], my_starts[None], team * own_rows, own_rows, residues, parts
    )
    flat = (parts, MICRO * seq_dev)
    row_shift = (
        my_shift + team * own_rows - jnp.arange(MICRO, dtype=jnp.int32)[None, :, None] * own_rows
    )
    row_shift = jnp.broadcast_to(row_shift, my_count.shape).reshape(flat)
    own_row = slot_lookup(
        my_begin.reshape(flat),
        my_count.reshape(flat),
        lambda held: held * parts + residues - row_shift[..., None],
    ).reshape(-1)
    head_rows = HEAD_DIM
    half_units = up_weight.shape[1] // 8

    shard_heads = query_weight.shape[1]

    def bias_rows(half):
        row = jnp.concatenate(
            [
                lax.dynamic_slice_in_dim(bias, (2 * team + half) * size, size)
                for bias, size in ((query_bias, HEAD_DIM), (value_bias, HEAD_DIM), (up_bias, half_units))
            ]
        )
        return jnp.pad(row[None, :], ((0, 7), (0, width - row.shape[0])))

    attn_mine, attn_other = attn_pack(
        query_weight, key_weight, value_weight, out_weight, bias_rows(y), bias_rows(1 - y), team, y
    )
    blocks = half_units // 128
    up_mine = flipped(up_weight, (2 * team + y) * blocks, blocks)
    up_other = flipped(up_weight, (2 * team + 1 - y) * blocks, blocks)
    down_mine = lax.dynamic_slice_in_dim(down_weight, (2 * team + y) * half_units, half_units, 0)
    down_other = lax.dynamic_slice_in_dim(down_weight, (2 * team + 1 - y) * half_units, half_units, 0)

    order = Order()

    def spread_out(array):
        spread = array.reshape(MICRO, tok_rows // parts, parts, col_width)
        spread = lax.all_to_all(spread, PLANE, split_axis=2, concat_axis=1, tiled=True)
        return spread.reshape(MICRO * tok_rows, col_width)

    def box_exchange(sent):
        return lax.all_to_all(sent, EVERY, split_axis=0, concat_axis=0, tiled=True)

    def boxes(spread):
        return pick_rows(send_row, spread, 384)

    def settle(got):
        return settle_rows(own_row, got.reshape(depth, parts * SLOTS, col_width), MICRO * own_rows)

    gain_one, shift_one, gain_two, shift_two, out_b, down_b = (
        array.astype(jnp.float32)[None, :]
        for array in (attn_gain, attn_shift, mlp_gain, mlp_shift, out_bias, down_bias)
    )

    rank = jnp.full((1,), team, jnp.int32)
    infos = []
    for micro_step in range(MICRO):
        holder, position, _ = buffer_layout(my_lengths[micro_step], my_starts[micro_step], tok_rows)
        segment = holder * tok_rows + position // (SEG + SUMM)
        summary = jnp.where(position % (SEG + SUMM) >= SEG, holder, -1)
        infos.append((jnp.stack([segment, summary], axis=1), jnp.stack([segment, holder], axis=0)))

    def up_down(piece):
        piece = order.take(piece)
        return (shift(piece, 1), shift(piece, -1))

    def onward(piece):
        piece = order.step(piece)
        return (piece, shift(piece, 1), swap_along(piece, "y"))

    def swapped(piece):
        piece = order.step(piece)
        return (piece, swap_along(piece, "y"))

    def team_start(rows):
        return (rows, swap_along(rows, "x"))

    def team_middle(started):
        own, by_x = started
        near = order.mark(join_rows([own, order.take(by_x)]))
        return (near, swap_along(near, "core"))

    def team_end(started):
        near, far = started
        return (near, order.step(far))

    def sum_start(left, weight):
        near, far = order.mark(partial_sums(order.take(left), weight))
        return (near, swap_along(far, "core"))

    def sum_middle(started):
        near, got = started
        kept, moving = order.mark(middle_rows(near, order.take(got)))
        return (kept, swap_along(moving, "x"))

    def sum_end(started):
        kept, got = started
        return (kept, order.take(got))

    def unsettle(array):
        return unsettle_rows(own_row, array, depth).reshape(-1, col_width)

    def unbox(got):
        return drop_rows(send_row, got, MICRO * tok_rows, 256)

    def spread_back(held):
        held = held.reshape(MICRO, tok_rows, 1, col_width)
        back = lax.all_to_all(held, PLANE, split_axis=1, concat_axis=2, tiled=True)
        return back.reshape(MICRO, tok_rows, col_width)

    order.mark(attn_mine)
    attn_1 = shift(attn_mine, 1)
    tok_spread = spread_out(tokens)
    attn_1 = order.step(attn_1)
    attn_2 = shift(attn_1, 1)
    attn_y1 = swap_along(attn_1, "y")
    tok_spread = order.step(tok_spread)
    attn_2 = order.step(attn_2)
    attn_3 = shift(order.take(attn_mine), -1)
    attn_y2 = swap_along(attn_2, "y")
    tok_sent = order.mark(boxes(order.take(tok_spread)))
    tok_got = box_exchange(tok_sent)
    attn_3, attn_y3 = swapped(attn_3)
    tok = order.mark(settle(order.take(tok_got)))
    up_1, up_3 = up_down(up_mine)
    cot_spread = spread_out(after(cotangent, tok))

    first_a = team_start(order.mark(norm_in(tok, 0, gain_one, shift_one)))
    first_b = team_start(order.mark(norm_in(order.take(tok), 1, gain_one, shift_one)))
    attn_all = [attn_mine, attn_1, attn_2, attn_3, attn_other, *order.take((attn_y1, attn_y2, attn_y3))]
    qkv_w, out_w, bias_w = order.mark(attn_join(attn_all))
    bias_w = bias_w.reshape(2 * depth, 8, width)[:, 0, :].astype(jnp.float32)
    query_b = bias_w[:, :head_rows].reshape(1, -1)
    value_b = bias_w[:, head_rows : 2 * head_rows].reshape(1, -1)
    up_b = bias_w[:, 2 * head_rows : 2 * head_rows + half_units].reshape(1, -1)
    qkv_b = jnp.concatenate([query_b, jnp.zeros_like(query_b), value_b], axis=1)
    no_b = jnp.zeros((1, out_w.shape[0]), jnp.float32)

    first_a = team_middle(first_a)
    cot_sent = order.mark(boxes(order.take(cot_spread)))
    first_a = team_end(first_a)
    up_1, up_2, up_y1 = onward(up_1)
    up_3, up_y3 = swapped(up_3)
    qkv_a = order.mark(project(*order.take(first_a), qkv_w, qkv_b))
    mixed_a = order.mark(attend(order.take(qkv_a), rank, *infos[0]))
    up_y1 = order.step(up_y1)
    up_2, up_y2 = swapped(up_2)
    down_1, down_3 = up_down(down_mine)
    first_b = team_middle(first_b)
    sum_a1 = sum_start(mixed_a, out_w)
    first_b = team_end(first_b)
    qkv_b_ = order.mark(project(*order.take(first_b), qkv_w, qkv_b))
    up_y3 = order.step(up_y3)
    sum_a1 = sum_middle(sum_a1)
    mixed_b = order.mark(attend(order.take(qkv_b_), rank, *infos[1]))
    up_y2 = order.step(up_y2)
    down_1, down_2, down_y1 = onward(down_1)
    resid_a, second_a = order.mark(resid_norm(tok, 0, *sum_end(sum_a1), out_b, gain_two, shift_two))
    second_a = team_start(second_a)
    down_3, down_y3 = swapped(down_3)
    cot_got = box_exchange(order.take(cot_sent))
    sum_b1 = sum_start(mixed_b, out_w)
    up_w = order.mark(join_rows([up_mine, up_1, up_2, up_3, up_other, *order.take((up_y1, up_y2, up_y3))]))
    sum_b1 = sum_middle(sum_b1)
    down_y1 = order.step(down_y1)
    second_a = team_end(team_middle(second_a))

    hidden_a, slope_a = order.mark(expand(*order.take(second_a), up_w, up_b))
    down_2, down_y2 = swapped(down_2)
    down_y3 = order.step(down_y3)
    resid_b, second_b = order.mark(resid_norm(tok, 1, *sum_end(sum_b1), out_b, gain_two, shift_two))
    second_b = team_start(second_b)
    cot = order.mark(settle(order.take(cot_got)))
    cot_own = cot.reshape(MICRO, own_rows, width)
    second_b = team_middle(second_b)
    cot_parts = [team_start(cot_own[m]) for m in range(MICRO)]
    second_b = team_end(second_b)
    hidden_b, slope_b = order.mark(expand(*order.take(second_b), up_w, up_b))
    down_w = order.mark(
        join_rows([down_mine, down_1, down_2, down_3, down_other, *order.take((down_y1, down_y2, down_y3))])
    )
    sum_a4 = sum_start(hidden_a, down_w)
    cot_parts[0] = team_middle(cot_parts[0])
    sum_b4 = sum_start(hidden_b, down_w)
    cot_a = team_end(cot_parts[0])

    low_a, up_sum_a = order.mark(expand_back(*order.take(cot_a), down_w, slope_a))
    cot_parts[1] = team_middle(cot_parts[1])
    sum_a2 = sum_start(low_a, up_w)
    cot_b = team_end(cot_parts[1])
    low_b, up_sum_b = order.mark(expand_back(*order.take(cot_b), down_w, slope_b))
    up_sum_a, up_sum_b = up_sum_a[0], up_sum_b[0]
    sum_a2 = sum_middle(sum_a2)
    sum_b2 = sum_start(low_b, up_w)

    def cross_half(left_a, right_a, left_b, right_b, half):
        size = left_a.shape[1] // 2
        return order.mark(cross_sums(order.take(left_a), right_a, left_b, right_b, half * size, size))

    down_far = cross_half(hidden_a, cot_a, hidden_b, cot_b, 1)
    down_swap = swap_along(down_far, "y")
    sum_b2 = sum_middle(sum_b2)

    def second_back(started, resid, m):
        return order.mark(second_back_rows(*sum_end(started), resid, cot, m, gain_two))

    resid_grad_a, attn_low_a, norm_sums_a = second_back(sum_a2, resid_a, 0)
    attn_low_a = team_start(attn_low_a)
    down_near = cross_half(hidden_a, cot_a, hidden_b, cot_b, 0)
    resid_grad_b, attn_low_b, norm_sums_b = second_back(sum_b2, resid_b, 1)
    attn_low_b = team_start(attn_low_b)
    sum_a4 = sum_middle(sum_a4)
    up_far = cross_half(low_a, second_a, low_b, second_b, 1)
    attn_low_a = team_middle(attn_low_a)
    sum_b4 = sum_middle(sum_b4)
    attn_low_a = team_end(attn_low_a)

    def ring_start(near, got):
        got = order.take(got)
        far_2 = order.mark(add_rows(near, got, 2))
        move = shift(far_2, 1)
        far_1 = order.mark(add_rows(near, order.take(got), 1))
        back = shift(far_1, -1)
        return (near, got, move, back)

    def ring_middle(started):
        near, got, move, back = started
        far_3 = order.mark(add_three(near, got, order.take(move), 3))
        return (near, got, shift(far_3, 1), back)

    def ring_end(started):
        near, got, move, back = started
        move, back = order.take((move, back))
        return order.mark(add_four(near, got, move, back, 0))

    def attn_back(attn_low, qkv, m):
        mixed_grad = order.mark(project(*order.take(attn_low), out_w, no_b))
        return order.mark(attend_back(qkv, order.take(mixed_grad), rank, *infos[m]))

    def sum_start_three(lefts, weight):
        near, far = order.mark(partial_three(*order.take(lefts), weight))
        return (near, swap_along(far, "core"))

    *lows_a, sums_a = attn_back(attn_low_a, qkv_a, 0)
    attn_low_b = team_middle(attn_low_b)
    down_ring = ring_start(down_near, down_swap)
    up_swap = swap_along(order.take(up_far), "y")
    sum_a3 = sum_start_three(lows_a, qkv_w)
    attn_low_b = team_end(attn_low_b)
    up_near = cross_half(low_a, second_a, low_b, second_b, 0)
    sum_a3 = sum_middle(sum_a3)
    layer_a = order.mark(layer_rows_of(resid_a, *sum_end(sum_a4), down_b))
    layer_b = order.mark(layer_rows_of(resid_b, *sum_end(sum_b4), down_b))
    layer_sent = order.mark(unsettle(join_rows([layer_a, layer_b])))
    down_ring = ring_middle(down_ring)
    layer_got = box_exchange(order.take(layer_sent))

    def pack_small():
        slots = jnp.arange(8 * depth, dtype=jnp.int32)
        index = jnp.arange(2 * depth, dtype=jnp.int32)
        owner = lax.rem(z - index % depth + depth, depth)
        flip = jnp.where(index < depth, y, 1 - y)
        hot = (slots[:, None] == (owner * 8 + 2 * team + flip)[None, :]).astype(jnp.float32)

        def place(vector):
            local = vector.reshape(2 * depth, -1)
            return jnp.dot(hot, local, precision=lax.Precision.HIGHEST).reshape(-1)

        head_sums = sums_a + sums_b
        norm_sums = norm_sums_a + norm_sums_b
        back_sums = back_sums_a + back_sums_b
        return jnp.concatenate(
            [
                place(head_sums[0]),
                place(head_sums[1]),
                place(up_sum_a + up_sum_b),
                norm_sums[:4].reshape(-1),
                back_sums[:2].reshape(-1),
            ]
        ).reshape(-1, 128)

    def ring_start(near, got):
        piece = near.shape[0] // depth
        got = order.take(got)
        far_2 = order.mark(add_rows(near, got, 2))
        move = shift(far_2, 1)
        far_1 = order.mark(add_rows(near, order.take(got), 1))
        back = shift(far_1, -1)
        return (near, got, move, back)

    def ring_middle(started):
        near, got, move, back = started
        far_3 = order.mark(add_three(near, got, order.take(move), 3))
        return (near, got, shift(far_3, 1), back)

    def ring_end(started):
        near, got, move, back = started
        move, back = order.take((move, back))
        return order.mark(add_four(near, got, move, back, 0))

    *lows_b, sums_b = attn_back(attn_low_b, qkv_b_, 1)
    def first_back(started, resid_grad, m):
        return order.mark(first_back_rows(*sum_end(started), tok, m, resid_grad, gain_one))

    firsts = (*first_a, *first_b)

    def one_half(half):
        lefts = order.take((lows_a[0], lows_b[0]))
        return order.mark(cross_pair(lefts, (lows_a[1], lows_b[1]), (firsts,), half))

    def two_half(half):
        lefts = order.take((lows_a[2], lows_b[2]))
        rights = (firsts, (*attn_low_a, *attn_low_b))
        return order.mark(cross_pair(lefts, (mixed_a, mixed_b), rights, half))

    input_a, back_sums_a = first_back(sum_a3, resid_grad_a, 0)
    up_ring = ring_start(up_near, up_swap)
    sum_b3 = sum_start_three(lows_b, qkv_w)
    one_far = one_half(1)
    one_swap = swap_along(one_far, "y")
    sum_b3 = sum_middle(sum_b3)
    two_far = two_half(1)
    two_swap = swap_along(two_far, "y")
    layer_held = order.mark(unbox(order.take(layer_got)))
    layer_out = spread_back(layer_held)
    one_near = one_half(0)
    down_total = ring_end(down_ring)
    down_plane = plane_start(down_total)
    up_ring = ring_middle(up_ring)
    input_b, back_sums_b = first_back(sum_b3, resid_grad_b, 1)
    input_sent = order.mark(unsettle(join_rows([input_a, input_b])))
    one_ring = ring_start(one_near, one_swap)
    layer_out = order.step(layer_out)
    input_got = box_exchange(order.take(input_sent))
    two_near = two_half(0)
    up_total = ring_end(up_ring)
    up_plane = plane_start(up_total)
    one_ring = ring_middle(one_ring)
    two_ring = ring_start(two_near, two_swap)
    down_plane = plane_middle(down_plane, order)
    small = order.mark(order.take(pack_small()))
    small_got = swap_along(small, "core")
    one_total = ring_end(one_ring)
    one_plane = plane_start(one_total)
    two_ring = ring_middle(two_ring)
    small = order.mark(small + order.take(small_got))
    small_got = swap_along(small, "x")
    down_plane = plane_end(down_plane, order)
    own = jnp.full((1,), eighth, jnp.int32)
    down_grad = order.mark(stack_pieces(*order.take(down_plane), own, False))
    input_held = order.mark(unbox(order.take(input_got)))
    input_grad = spread_back(input_held)
    up_plane = plane_middle(up_plane, order)
    two_total = ring_end(two_ring)
    two_plane = plane_start(two_total)
    small = order.mark(small + order.take(small_got))
    small_got = swap_along(small, "y")
    up_plane = plane_end(up_plane, order)
    one_plane = plane_middle(one_plane, order)
    up_grad = order.mark(stack_pieces(*order.take(up_plane), own, True))
    two_plane = plane_middle(two_plane, order)
    small = order.mark(small + order.take(small_got))
    small_got = lax.ppermute(small, "z", [(i, i ^ 1) for i in range(depth)])
    one_plane = plane_end(one_plane, order)
    query_grad, key_grad = order.mark(stack_heads(*order.take(one_plane), own, (True, True)))
    input_grad = order.step(input_grad)
    small = order.mark(small + order.take(small_got))
    small_got = lax.ppermute(small, "z", [(i, i ^ 2) for i in range(depth)])
    two_plane = plane_end(two_plane, order)
    value_grad, out_w_grad = order.mark(stack_heads(*order.take(two_plane), own, (True, False)))
    packed = small + order.take(small_got)
    packed = packed.reshape(-1)
    pieces = []
    offset = 0
    heads_all = depth * shard_heads
    for size in (heads_all, heads_all, depth * up_weight.shape[1]) + (width,) * 6:
        pieces.append(packed[offset : offset + size])
        offset += size
    query_b_grad, value_b_grad, up_b_grad, out_b_grad, down_b_grad, gain_two_g, shift_two_g, *norm_grads = pieces
    norm_grads = norm_grads + [gain_two_g, shift_two_g]

    def own_shard(vector):
        size = vector.shape[0] // depth
        return lax.dynamic_slice_in_dim(vector, z * size, size)

    return (
        layer_out,
        input_grad,
        query_grad,
        key_grad,
        value_grad,
        out_w_grad,
        own_shard(query_b_grad),
        own_shard(value_b_grad),
        out_b_grad,
        up_grad,
        own_shard(up_b_grad),
        down_grad,
        down_b_grad,
        *norm_grads,
    )


def team_layer(mesh):
    axes = ("y", "x", "core", "z")
    inner = Mesh(mesh.devices.reshape(2, 2, 2, 4), axes)
    rows = P(None, PLANE, "z")
    in_specs = (
        rows, rows, P(), P(), P(None, "z"), P(None, "z"), P(None, "z"), P("z", None), P("z"), P("z"),
        P(), P(None, "z"), P("z"), P("z", None), P(), P(), P(), P(), P(),
    )
    out_specs = (
        rows, rows, P(None, "z"), P(None, "z"), P(None, "z"), P("z", None), P("z"), P("z"),
        P(), P(None, "z"), P("z"), P("z", None), P(), P(), P(), P(), P(),
    )
    return jax.shard_map(layer, mesh=inner, in_specs=in_specs, out_specs=out_specs, check_vma=False)


def solution(mesh):
    if dict(mesh.shape) == {"dp": 8, "tensor": 4}:
        return team_layer(mesh)
    return general_layer(mesh)
```
